32 devices in a mesh: lon: 16 (over z, y, x), mlp: 2 (over core).
Axes of the slice: x: 2, y: 2, z: 4, core: 2. Of those that a mesh axis runs over, the one named last changes fastest.
Arguments:
- fields: bfloat16 [12, 1440, 1024], P('mlp', 'lon'), may hold values from -40 to 40
- cotangent: bfloat16 [12, 1440, 1024], P('mlp', 'lon'), may hold values from -6 to 6
- conv_weight: bfloat16 [7, 7, 1024], replicated, may hold values from -0.875 to 0.875
- norm_gain: bfloat16 [1024], replicated, may hold values from 0.099609375 to 1.8984375
- weight_in: bfloat16 [1024, 4096], P(None, 'mlp'), may hold values from -0.1875 to 0.1875
- weight_out: bfloat16 [4096, 1024], P('mlp'), may hold values from -0.09375 to 0.09375
Outputs:
- grad_fields: bfloat16 [12, 1440, 1024], P('mlp', 'lon')
- grad_weight_in: bfloat16 [1024, 4096], P(None, 'mlp')
- grad_weight_out: bfloat16 [4096, 1024], P('mlp')
The draws below stay inside these ranges and needn't reach their ends.
All inputs are finite; a program needn't handle non-finite values.
Results may differ from the reference program's by a relative error of at most 0.0095.
Values may be sent and summed in bfloat16 or wider, within the bound.
No kernel may reach another device: no remote copies, remote signals or barrier semaphores. Data moves between devices by JAX's collectives and lax.ppermute only.
A program may use at most 128 MiB of HBM per device.

```python
import math
import jax
import jax.numpy as jnp
import numpy as np
from jax import lax

C = 1024
H = 4096
KS = 7
LON = 1440
SLOTS = 90
LON_SLOTS = 1440
LAT = 12
N_LON = 16
N_MLP = 2


def draw_fields(key, part):
    keys = jax.random.split(key, 3)
    base = jnp.clip(jax.random.normal(keys[0], (LAT, LON_SLOTS, C), jnp.float32), -4.0, 4.0)
    row_scale = jnp.exp(jax.random.uniform(keys[1], (LAT, LON_SLOTS, 1), jnp.float32) * math.log(10.0))
    chan_scale = jnp.exp(jax.random.uniform(keys[2], (1, 1, C), jnp.float32) * math.log(10.0))
    return (base * row_scale * chan_scale * 0.1).astype(jnp.bfloat16)


def block_scale(stream_key, shape, pieces, low, high):
    level = 1.0
    for dim, blocks in pieces:
        heights = jax.random.uniform(jax.random.fold_in(jax.random.fold_in(stream_key, 6), dim), (blocks,), jnp.float32, low / len(pieces), high / len(pieces))
        level = level * jnp.repeat(jnp.exp(heights), shape[dim] // blocks).reshape((-1,) + (1,) * (len(shape) - 1 - dim))
    return level


def scatter_about(rng, dims, scale, bound, cuts=(), kind=jnp.bfloat16):
    entries = scale * jax.random.normal(rng, dims, jnp.float32)
    if cuts:
        entries = entries * block_scale(rng, dims, cuts, -0.22, 0.18)
    return jnp.clip(entries, -bound, bound).astype(kind)


def setup_inputs(seed: int = 0) -> dict:
    streams_of = jax.random.split(jax.random.key(seed), 7)
    return {
        "fields": draw_fields(jax.random.fold_in(streams_of[6], 71), 0),
        "cotangent": scatter_about(streams_of[1], (LAT, LON_SLOTS, C), 1.0, 6.0, ((0, 2), (1, 16))),
        "conv_weight": scatter_about(streams_of[2], (KS, KS, C), (KS * KS) ** -0.5, 0.875),
        "norm_gain": jnp.clip(1.0 + 0.18 * jax.random.normal(streams_of[3], (C,), jnp.float32), 0.099609375, 1.8984375).astype(jnp.bfloat16),
        "weight_in": scatter_about(streams_of[4], (C, H), C ** -0.5, 0.1875, ((1, 2),)),
        "weight_out": scatter_about(streams_of[5], (H, C), H ** -0.5, 0.09375, ((0, 2),)),
    }


def activate(values):
    return values * (0.5 * (1.0 + lax.erf(values * (1.0 / math.sqrt(2.0)))))

def slope(values):
    cumulative = 0.5 * (1.0 + lax.erf(values * (1.0 / math.sqrt(2.0))))
    return cumulative + values * jnp.exp(-0.5 * values * values) * (1.0 / math.sqrt(2.0 * math.pi))

def extend(field, reach):
    padded = jnp.pad(field, ((reach, reach), (0, 0), (0, 0)))
    return jnp.concatenate([padded[:, -reach:], padded, padded[:, :reach]], axis=1)

def live_columns():
    base_count = LON // N_LON
    surplus = LON % N_LON
    chosen = []
    for device in range(N_LON):
        count = base_count + (1 if device < surplus else 0)
        chosen.extend(range(device * SLOTS, device * SLOTS + count))
    return np.array(chosen, dtype=np.int32)

def reference(fields, cotangent, conv_weight, norm_gain, weight_in, weight_out):
    columns = live_columns()
    compact = jnp.take(fields, columns, axis=1)
    cot_compact = jnp.take(cotangent, columns, axis=1)
    lat_all, lon_all, width = compact.shape
    reach = KS // 2
    kernel = conv_weight.astype(jnp.float32)
    padded = extend(compact.astype(jnp.float32), reach)
    mixed = jnp.zeros((lat_all, lon_all, width), jnp.float32)
    for row_off in range(KS):
        for col_off in range(KS):
            mixed = mixed + kernel[row_off, col_off] * padded[row_off:row_off + lat_all, col_off:col_off + lon_all]
    centred = mixed - lax.optimization_barrier(jnp.mean(mixed, axis=-1, keepdims=True))
    inv_std = lax.rsqrt(lax.optimization_barrier(jnp.mean(centred * centred, axis=-1, keepdims=True)) + 1e-06)
    norm_hat = centred * inv_std
    gain = norm_gain.astype(jnp.float32)
    normed = (norm_hat * gain).astype(jnp.bfloat16).reshape(-1, width)
    cot_rows = cot_compact.reshape(-1, width)
    block = H // N_MLP
    grad_normed = jnp.zeros((normed.shape[0], width), jnp.float32)
    grads_in = []
    grads_out = []
    for index in range(N_MLP):
        w_first = weight_in[:, index * block:(index + 1) * block]
        w_second = weight_out[index * block:(index + 1) * block]
        hidden = jnp.dot(normed, w_first, preferred_element_type=jnp.float32)
        activated = activate(hidden).astype(jnp.bfloat16)
        upstream = lax.dot_general(cot_rows, w_second, (((1,), (1,)), ((), ())), preferred_element_type=jnp.float32)
        grad_hidden = (upstream * slope(hidden)).astype(jnp.bfloat16)
        grads_out.append(lax.dot_general(activated, cot_rows, (((0,), (0,)), ((), ())), preferred_element_type=jnp.float32))
        grads_in.append(lax.dot_general(normed, grad_hidden, (((0,), (0,)), ((), ())), preferred_element_type=jnp.float32))
        partial_sum = lax.dot_general(grad_hidden, w_first, (((1,), (1,)), ((), ())), preferred_element_type=jnp.float32)
        rounded = lax.optimization_barrier(partial_sum.astype(jnp.bfloat16))
        grad_normed = grad_normed + rounded.astype(jnp.float32)
    scale = jnp.float32(1.0 / math.sqrt(lat_all * lon_all))
    grad_weight_in = (jnp.concatenate(grads_in, axis=1) * scale).astype(jnp.bfloat16)
    grad_weight_out = (jnp.concatenate(grads_out, axis=0) * scale).astype(jnp.bfloat16)
    scaled = grad_normed.reshape(lat_all, lon_all, width) * gain
    grad_mixed = inv_std * (scaled - lax.optimization_barrier(jnp.mean(scaled, axis=-1, keepdims=True)) - norm_hat * lax.optimization_barrier(jnp.mean(scaled * norm_hat, axis=-1, keepdims=True)))
    grad_mixed = grad_mixed.astype(jnp.bfloat16)
    padded_grad = extend(grad_mixed.astype(jnp.float32), reach)
    result = cot_compact.astype(jnp.float32)
    for row_off in range(KS):
        for col_off in range(KS):
            row_start = 2 * reach - row_off
            col_start = 2 * reach - col_off
            result = result + kernel[row_off, col_off] * padded_grad[row_start:row_start + lat_all, col_start:col_start + lon_all]
    whole = jnp.zeros((lat_all, fields.shape[1], width), jnp.bfloat16)
    whole = whole.at[:, columns].set(result.astype(jnp.bfloat16))
    return (whole, grad_weight_in, grad_weight_out)
```

```python
import math

import jax
import jax.numpy as jnp
from jax import lax
from jax.sharding import PartitionSpec as P

KS = 7
LON = 1440


def passed_along(value, axis, by):
    count = lax.axis_size(axis)
    return lax.ppermute(value, axis, [(i, (i + by) % count) for i in range(count)])


def with_halo(cells, sides, width):
    for axis, dim in sides:
        count = lax.axis_size(axis)
        ends = count - 1
        head = lax.slice_in_dim(cells, 0, width, axis=dim)
        tail = lax.slice_in_dim(cells, cells.shape[dim] - width, cells.shape[dim], axis=dim)
        cells = jnp.concatenate(
            [
                lax.ppermute(tail, axis, [(i, (i + 1) % count) for i in range(ends)]),
                cells,
                lax.ppermute(head, axis, [((i + 1) % count, i) for i in range(ends)]),
            ],
            axis=dim,
        )
    return cells


def activate(values):
    return values * (0.5 * (1.0 + lax.erf(values * (1.0 / math.sqrt(2.0)))))


def slope(values):
    cumulative = 0.5 * (1.0 + lax.erf(values * (1.0 / math.sqrt(2.0))))
    return cumulative + values * jnp.exp(-0.5 * values * values) * (1.0 / math.sqrt(2.0 * math.pi))


def live_count():
    members = lax.axis_size("lon")
    position = lax.axis_index("lon")
    return LON // members + (position < LON % members).astype(jnp.int32)


def lon_cycle(field, held):
    reach = KS // 2
    first_cols = field[:, :reach]
    last_cols = lax.dynamic_slice_in_dim(field, held - reach, reach, 1)
    from_left = passed_along(last_cols, "lon", 1)
    from_right = passed_along(first_cols, "lon", -1)
    spare = jnp.zeros((field.shape[0], reach, field.shape[2]), field.dtype)
    joined = jnp.concatenate([from_left, field, spare], axis=1)
    return lax.dynamic_update_slice_in_dim(joined, from_right, reach + held, 1)


def extend(field, held):
    reach = KS // 2
    rows = with_halo(field, (("mlp", 0),), reach)
    padded = lon_cycle(rows, held)
    return padded.astype(jnp.float32)


def summed_over_lon(partial, factor):
    share = lax.psum_scatter(
        partial.astype(jnp.bfloat16), "lon", scatter_dimension=0, tiled=True
    ).astype(jnp.float32)
    return lax.all_gather((share * factor).astype(jnp.bfloat16), "lon", axis=0, tiled=True)


def body(fields, cotangent, conv_weight, norm_gain, weight_in, weight_out):
    lat_dev, slot_count, width = fields.shape
    reach = KS // 2
    held = live_count()
    slot_live = lax.broadcasted_iota(jnp.int32, (1, slot_count, 1), 1) < held
    kernel = conv_weight.astype(jnp.float32)
    padded = extend(fields, held)
    mixed = jnp.zeros((lat_dev, slot_count, width), jnp.float32)
    for row_off in range(KS):
        for col_off in range(KS):
            mixed = (
                mixed
                + kernel[row_off, col_off]
                * padded[row_off : row_off + lat_dev, col_off : col_off + slot_count]
            )
    centred = mixed - jnp.mean(mixed, axis=-1, keepdims=True)
    inv_std = lax.rsqrt(jnp.mean(centred * centred, axis=-1, keepdims=True) + 1e-06)
    norm_hat = centred * inv_std
    gain = norm_gain.astype(jnp.float32)
    normed = jnp.where(slot_live, norm_hat * gain, 0.0).astype(jnp.bfloat16).reshape(-1, width)
    normed_all = lax.all_gather(normed, "mlp", axis=0, tiled=True)
    cot_all = lax.all_gather(cotangent.reshape(-1, width), "mlp", axis=0, tiled=True)
    hidden = jnp.dot(normed_all, weight_in, preferred_element_type=jnp.float32)
    activated = activate(hidden).astype(jnp.bfloat16)
    upstream = lax.dot_general(
        cot_all, weight_out, (((1,), (1,)), ((), ())), preferred_element_type=jnp.float32
    )
    grad_hidden = (upstream * slope(hidden)).astype(jnp.bfloat16)
    grad_second = lax.dot_general(
        activated, cot_all, (((0,), (0,)), ((), ())), preferred_element_type=jnp.float32
    )
    grad_first = lax.dot_general(
        normed_all, grad_hidden, (((0,), (0,)), ((), ())), preferred_element_type=jnp.float32
    )
    grad_normed = lax.psum_scatter(
        lax.dot_general(
            grad_hidden, weight_in, (((1,), (1,)), ((), ())), preferred_element_type=jnp.float32
        ).astype(jnp.bfloat16),
        "mlp",
        scatter_dimension=0,
        tiled=True,
    ).astype(jnp.float32)
    cells = lax.axis_size("mlp") * lat_dev * LON
    factor = jnp.float32(1.0 / math.sqrt(cells))
    out_second = summed_over_lon(grad_second, factor)
    out_first = summed_over_lon(grad_first, factor)
    scaled = grad_normed.reshape(lat_dev, slot_count, width) * gain
    grad_mixed = inv_std * (
        scaled
        - jnp.mean(scaled, axis=-1, keepdims=True)
        - norm_hat * jnp.mean(scaled * norm_hat, axis=-1, keepdims=True)
    )
    grad_mixed = grad_mixed.astype(jnp.bfloat16)
    padded_grad = extend(grad_mixed, held)
    result = cotangent.astype(jnp.float32)
    for row_off in range(KS):
        for col_off in range(KS):
            row_start = 2 * reach - row_off
            col_start = 2 * reach - col_off
            result = (
                result
                + kernel[row_off, col_off]
                * padded_grad[row_start : row_start + lat_dev, col_start : col_start + slot_count]
            )
    result = jnp.where(slot_live, result, 0.0)
    return (result.astype(jnp.bfloat16), out_first, out_second)


def solution(mesh):
    in_specs = (
        P("mlp", "lon", None),
        P("mlp", "lon", None),
        P(),
        P(),
        P(None, "mlp"),
        P("mlp", None),
    )
    out_specs = (P("mlp", "lon", None), P(None, "mlp"), P("mlp", None))
    return jax.shard_map(body, mesh=mesh, in_specs=in_specs, out_specs=out_specs, check_vma=False)
```

```python
import math

import jax
import jax.numpy as jnp
from jax import lax
from jax.sharding import PartitionSpec as P

KS = 7
LON = 1440
REACH = KS // 2
BF16 = jnp.bfloat16
F32 = jnp.float32


def passed_along(value, axis, by):
    count = lax.axis_size(axis)
    return lax.ppermute(value, axis, [(i, (i + by) % count) for i in range(count)])


def row_halo(cells):
    count = lax.axis_size("mlp")
    ends = count - 1
    head, tail = cells[:REACH], cells[-REACH:]
    return jnp.concatenate(
        [
            lax.ppermute(tail, "mlp", [(i, i + 1) for i in range(ends)]),
            cells,
            lax.ppermute(head, "mlp", [(i + 1, i) for i in range(ends)]),
        ],
        axis=0,
    )


def live_count():
    members = lax.axis_size("lon")
    position = lax.axis_index("lon")
    return LON // members + (position < LON % members).astype(jnp.int32)


def lon_cycle(field, held):
    first_cols = field[:, :REACH]
    last_cols = lax.dynamic_slice_in_dim(field, held - REACH, REACH, 1)
    from_left = passed_along(last_cols, "lon", 1)
    from_right = passed_along(first_cols, "lon", -1)
    spare = jnp.zeros((field.shape[0], REACH, field.shape[2]), field.dtype)
    joined = jnp.concatenate([from_left, field, spare], axis=1)
    return lax.dynamic_update_slice_in_dim(joined, from_right, REACH + held, 1)


def extend(field, held):
    return lon_cycle(row_halo(field), held).astype(F32)


def gate(values):
    cumulative = 0.5 * (1.0 + lax.erf(values * (1.0 / math.sqrt(2.0))))
    density = jnp.exp(-0.5 * values * values) * (1.0 / math.sqrt(2.0 * math.pi))
    return cumulative, density


def swapped(value, bit):
    count = lax.axis_size("lon")
    return lax.ppermute(value, "lon", [(i, i ^ bit) for i in range(count)])


def upper(bit):
    return (lax.axis_index("lon") & bit) // bit


def scattered_sum(part, bits):
    for bit in bits:
        half = part.shape[0] // 2
        mine = upper(bit)
        got = swapped(lax.dynamic_slice_in_dim(part, (1 - mine) * half, half, 0), bit)
        kept = lax.dynamic_slice_in_dim(part, mine * half, half, 0)
        total = kept.astype(F32) + got.astype(F32)
        part = total.astype(BF16)
    return total


def gathered(part, bits):
    for bit in reversed(bits):
        got = swapped(part, bit)
        high = upper(bit) == 1
        part = jnp.concatenate([jnp.where(high, got, part), jnp.where(high, part, got)], axis=0)
    return part


def orders():
    count = lax.axis_size("lon")
    bits = []
    bit = 1
    while bit < count:
        bits.append(bit)
        bit *= 2
    return (bits, [bits[1], bits[0]] + bits[2:])


def summed_over_lon(halves, factor):
    outs = []
    for half, bits in zip(halves, orders()):
        share = (scattered_sum(half, bits) * factor).astype(BF16)
        outs.append(gathered(share, bits))
    return jnp.concatenate(outs, axis=0)


def all_rows(own):
    count = lax.axis_size("mlp")
    if count == 2:
        return jnp.concatenate([own, lax.ppermute(own, "mlp", [(0, 1), (1, 0)])], axis=0)
    return lax.all_gather(own, "mlp", axis=0, tiled=True)


def own_rows_sum(partial):
    count = lax.axis_size("mlp")
    if count == 2:
        rows = partial.shape[0] // 2
        theirs = lax.ppermute(partial[rows:].astype(BF16), "mlp", [(0, 1), (1, 0)])
        return partial[:rows].astype(BF16).astype(F32) + theirs.astype(F32)
    return lax.psum_scatter(partial.astype(BF16), "mlp", scatter_dimension=0, tiled=True).astype(F32)


def across_rows(left, right, out=F32):
    return lax.dot_general(left, right, (((0,), (0,)), ((), ())), preferred_element_type=out)


def body(fields, cotangent, conv_weight, norm_gain, weight_in, weight_out):
    lat_dev, slot_count, width = fields.shape
    slots_pad = -(-slot_count // 16) * 16
    held = live_count()
    slot_live = lax.broadcasted_iota(jnp.int32, (1, slot_count, 1), 1) < held
    kernel = conv_weight.astype(F32)
    spare = ((0, 0), (0, slots_pad - slot_count), (0, 0))
    cot_all = all_rows(jnp.pad(jnp.where(slot_live, cotangent, 0), spare).reshape(-1, width))
    padded = extend(fields, held)
    mixed = jnp.zeros((lat_dev, slot_count, width), F32)
    for row_off in range(KS):
        for col_off in range(KS):
            mixed = (
                mixed
                + kernel[row_off, col_off]
                * padded[row_off : row_off + lat_dev, col_off : col_off + slot_count]
            )
    centred = mixed - jnp.mean(mixed, axis=-1, keepdims=True)
    inv_std = lax.rsqrt(jnp.mean(centred * centred, axis=-1, keepdims=True) + 1e-06)
    norm_hat = centred * inv_std
    gain = norm_gain.astype(F32)
    normed = jnp.where(slot_live, norm_hat * gain, 0.0).astype(BF16)
    normed_all = all_rows(jnp.pad(normed, spare).reshape(-1, width))
    cells = lax.axis_size("mlp") * lat_dev * LON
    factor = jnp.float32(1.0 / math.sqrt(cells))
    hid = weight_in.shape[1] // 2
    seconds = []
    grad_hidden = []
    for cols in (slice(0, hid), slice(hid, 2 * hid)):
        hidden = jnp.dot(normed_all, weight_in[:, cols], preferred_element_type=F32)
        cumulative, density = gate(hidden)
        activated = (hidden * cumulative).astype(BF16)
        seconds.append(across_rows(activated, cot_all).astype(BF16))
        upstream = lax.dot_general(
            cot_all, weight_out[cols], (((1,), (1,)), ((), ())), preferred_element_type=F32
        )
        grad_hidden.append((upstream * (cumulative + hidden * density)).astype(BF16))
    grad_hidden = jnp.concatenate(grad_hidden, axis=1)
    half = width // 2
    firsts = [
        across_rows(normed_all[:, :half], grad_hidden).astype(BF16),
        across_rows(normed_all[:, half:], grad_hidden).astype(BF16),
    ]
    out_second = summed_over_lon(seconds, factor)
    out_first = summed_over_lon(firsts, factor)
    grad_normed = own_rows_sum(
        lax.dot_general(
            grad_hidden, weight_in, (((1,), (1,)), ((), ())), preferred_element_type=F32
        )
    )
    scaled = grad_normed.reshape(lat_dev, slots_pad, width)[:, :slot_count] * gain
    grad_mixed = inv_std * (
        scaled
        - jnp.mean(scaled, axis=-1, keepdims=True)
        - norm_hat * jnp.mean(scaled * norm_hat, axis=-1, keepdims=True)
    )
    padded_grad = extend(grad_mixed.astype(BF16), held)
    result = cotangent.astype(F32)
    for row_off in range(KS):
        for col_off in range(KS):
            row_start = 2 * REACH - row_off
            col_start = 2 * REACH - col_off
            result = (
                result
                + kernel[row_off, col_off]
                * padded_grad[row_start : row_start + lat_dev, col_start : col_start + slot_count]
            )
    result = jnp.where(slot_live, result, 0.0)
    return (result.astype(BF16), out_first, out_second)


def solution(mesh):
    in_specs = (
        P("mlp", "lon", None),
        P("mlp", "lon", None),
        P(),
        P(),
        P(None, "mlp"),
        P("mlp", None),
    )
    out_specs = (P("mlp", "lon", None), P(None, "mlp"), P("mlp", None))
    return jax.shard_map(body, mesh=mesh, in_specs=in_specs, out_specs=out_specs, check_vma=False)
```

```python
import functools
import math

import jax
import jax.numpy as jnp
from jax import lax
from jax.experimental import pallas as pl
from jax.experimental.pallas import tpu as pltpu
from jax.sharding import PartitionSpec as P

KS = 7
LON = 1440
REACH = KS // 2
LANES = 128
BF16 = jnp.bfloat16
F32 = jnp.float32
LEAD = 8


def passed_along(value, axis, by):
    count = lax.axis_size(axis)
    return lax.ppermute(value, axis, [(i, (i + by) % count) for i in range(count)])


def after(value, *others):
    return lax.optimization_barrier((value,) + others)[0]


def live_count():
    members = lax.axis_size("lon")
    position = lax.axis_index("lon")
    return LON // members + (position < LON % members).astype(jnp.int32)


def halo(own, slots, held):
    lat, count = own.shape[0], lax.axis_size("mlp")
    if count == 2:
        mine = jnp.where(lax.axis_index("mlp") == 0, own[lat - REACH :], own[:REACH])
        other = lax.ppermute(mine, "mlp", [(0, 1), (1, 0)])
    else:
        ends = count - 1
        other = jnp.concatenate(
            [
                lax.ppermute(own[lat - REACH :], "mlp", [(i, i + 1) for i in range(ends)]),
                lax.ppermute(own[:REACH], "mlp", [(i + 1, i) for i in range(ends)]),
            ],
            axis=0,
        )
    even = LON % lax.axis_size("lon") == 0
    both = (own, other)
    first = jnp.concatenate([v[:, :REACH] for v in both], axis=0)
    if even:
        last = jnp.concatenate([v[:, slots - REACH : slots] for v in both], axis=0)
    else:
        last = jnp.concatenate(
            [lax.dynamic_slice_in_dim(v, held - REACH, REACH, 1) for v in both], axis=0
        )
    left = passed_along(last, "lon", 1)
    right = passed_along(first, "lon", -1)
    if not even:
        rows = jnp.concatenate([v[:, :slots] for v in both], axis=0)
        joined = jnp.concatenate([rows, jnp.zeros_like(right)], axis=1)
        joined = lax.dynamic_update_slice_in_dim(joined, right, held, 1)
        own, other, right = joined[:lat, :slots], joined[lat:, :slots], joined[:, slots:]
    return own, other, left, right


def places(lat, held):
    core, count = lax.axis_index("mlp"), lax.axis_size("mlp")
    far = lat + REACH
    if count == 2:
        near = jnp.where(core == 0, far, 0)
        spare = jnp.where(core == 0, 0, far)
    else:
        near, spare = 0, far
    return jnp.stack([jnp.int32(near), jnp.int32(spare), held.astype(jnp.int32)])


def conv_tile(lat, slots, flip, where_ref, own, other, left, right, weight, wide, lane, sink):
    groups = other.shape[0] // REACH
    wide[REACH : REACH + lat, LEAD : LEAD + slots, :] = own[:, :slots, lane].astype(F32)
    wide[REACH : REACH + lat, LEAD - REACH : LEAD, :] = left[:lat, :, lane].astype(F32)
    wide[REACH : REACH + lat, LEAD + slots : LEAD + slots + REACH, :] = right[:lat, :, lane].astype(F32)
    for g in range(groups):
        for k in range(REACH):
            at, src = where_ref[g] + k, g * REACH + k
            wide[at, LEAD : LEAD + slots, :] = other[src, :slots, lane].astype(F32)
            wide[at, LEAD - REACH : LEAD, :] = left[lat + src, :, lane].astype(F32)
            wide[at, LEAD + slots : LEAD + slots + REACH, :] = right[lat + src, :, lane].astype(F32)

    def step(jt, carry):
        start = jt * 16
        acc = [[jnp.zeros((8, LANES), F32) for _ in range(lat)] for _ in range(2)]
        for b in range(KS):
            taps = [a * KS + b for a in range(KS)]
            if flip:
                taps = [KS * KS - 1 - t for t in taps]
            taken = [weight[t, :, lane] for t in taps]
            for r in range(lat + 2 * REACH):
                for half in range(2):
                    cells = wide[r, pl.ds(start + 8 * half + LEAD - REACH + b, 8), :]
                    for i in range(max(0, r - KS + 1), min(lat, r + 1)):
                        acc[half][i] = acc[half][i] + taken[r - i] * cells
        for half in range(2):
            for i in range(lat):
                sink(i, pl.ds(pl.multiple_of(start + 8 * half, 8), 8), acc[half][i])
        return carry

    lax.fori_loop(0, -(-slots // 16), step, 0)


def clear_spare(where_ref, other, wide):
    if other.shape[0] == REACH:
        for k in range(REACH):
            wide[where_ref[1] + k] = jnp.zeros(wide.shape[1:], F32)


def forward_kernel(
    lat, slots, where_ref, own, other, left, right, weight, gain, normed, hat, inv, wide, mixed
):
    width = mixed.shape[-1]
    clear_spare(where_ref, other, wide)

    def channels(ct, carry):
        lane = pl.ds(pl.multiple_of(ct * LANES, LANES), LANES)

        def sink(i, at, value):
            mixed[i, at, lane] = value

        conv_tile(lat, slots, False, where_ref, own, other, left, right, weight, wide, lane, sink)
        return carry

    lax.fori_loop(0, width // LANES, channels, 0)
    tiles = mixed.shape[1] // 16

    def norm(step, carry):
        i, start = step // tiles, pl.multiple_of(step % tiles * 16, 16)
        at = pl.ds(start, 16)
        values = mixed[i, at, :]
        centred = values - jnp.mean(values, axis=-1, keepdims=True)
        scale = lax.rsqrt(jnp.mean(centred * centred, axis=-1, keepdims=True) + 1e-06)
        live = start + lax.broadcasted_iota(jnp.int32, (16, 1), 0) < where_ref[2]
        unit = jnp.where(live, centred * scale, 0.0)
        hat[i, at, :] = unit
        normed[i, at, :] = (unit * gain[...]).astype(BF16)
        inv[i, at, :] = jnp.broadcast_to(jnp.where(live, scale, 0.0), (16, LANES))
        return carry

    lax.fori_loop(0, lat * tiles, norm, 0)


def backward_kernel(
    lat, slots, where_ref, own, other, left, right, weight, cot, out, wide, mixed
):
    clear_spare(where_ref, other, wide)

    def channels(ct, carry):
        lane = pl.ds(pl.multiple_of(ct * LANES, LANES), LANES)

        def sink(i, at, value):
            mixed[i, at, :] = value

        conv_tile(lat, slots, True, where_ref, own, other, left, right, weight, wide, lane, sink)
        live = lax.broadcasted_iota(jnp.int32, (slots, 1), 0) < where_ref[2]
        for i in range(lat):
            total = cot[i, :, lane].astype(F32) + mixed[i, :slots, :]
            out[i, :, lane] = jnp.where(live, total, 0.0).astype(BF16)
        return carry

    lax.fori_loop(0, out.shape[-1] // LANES, channels, 0)


def kernel_call(kernel, lat, slots, slots_pad, width, outs, mixed, operands):
    vmem = pl.BlockSpec(memory_space=pltpu.VMEM)
    taps = 2 * lat * slots_pad * width * KS * KS
    return pl.pallas_call(
        functools.partial(kernel, lat, slots),
        out_shape=outs,
        in_specs=[pl.BlockSpec(memory_space=pltpu.SMEM)] + [vmem] * (len(operands) - 1),
        out_specs=jax.tree.map(lambda _: vmem, outs),
        scratch_shapes=[
            pltpu.VMEM((lat + 2 * REACH, slots_pad + 16, LANES), F32),
            pltpu.VMEM(mixed, F32),
        ],
        compiler_params=pltpu.CompilerParams(vmem_limit_bytes=32 * 2**20),
        cost_estimate=pl.CostEstimate(flops=taps, bytes_accessed=8 * 2**20, transcendentals=0),
    )(*operands)


def gate(values):
    cumulative = 0.5 * (1.0 + lax.erf(values * (1.0 / math.sqrt(2.0))))
    density = jnp.exp(-0.5 * values * values) * (1.0 / math.sqrt(2.0 * math.pi))
    return cumulative, density


def upper(bit):
    return (lax.axis_index("lon") & bit) // bit


def swapped(value, bit):
    count = lax.axis_size("lon")
    return lax.ppermute(value, "lon", [(i, i ^ bit) for i in range(count)])


def cut(part, which):
    half = part.shape[1] // 2
    return lax.dynamic_slice_in_dim(part, which * half, half, 1)


def merged(low_first, own, got):
    high = low_first == 1
    return jnp.concatenate([jnp.where(high, got, own), jnp.where(high, own, got)], axis=1)


class Order:
    def __init__(self):
        self.last = None

    def swap(self, value, bit):
        if self.last is not None:
            value = after(value, self.last)
        self.last = value
        return swapped(value, bit)


def halves_added(kept, got):
    return kept.astype(F32) + got.astype(F32)


def lon_bits():
    bits, bit = [], 1
    while bit < lax.axis_size("lon"):
        bits.append(bit)
        bit *= 2
    return bits


def scatter_open(order, parts, bits):
    return [order.swap(cut(p, 1 - upper(b)), b) for p, b in zip(parts, bits)]


def scatter_step(order, parts, got, bits, nexts):
    totals = [
        halves_added(cut(p, upper(b)), g).astype(BF16) for p, g, b in zip(parts, got, bits)
    ]
    if len(totals) != len(nexts):
        totals = [jnp.concatenate(totals, axis=0)]
    return totals, [order.swap(cut(t, 1 - upper(b)), b) for t, b in zip(totals, nexts)]


def all_rows(own):
    if lax.axis_size("mlp") == 2:
        return jnp.concatenate([own, lax.ppermute(own, "mlp", [(0, 1), (1, 0)])], axis=0)
    return lax.all_gather(own, "mlp", axis=0, tiled=True)


def own_rows_sum(partial):
    if lax.axis_size("mlp") == 2:
        rows = partial.shape[0] // 2
        theirs = lax.ppermute(partial[rows:], "mlp", [(0, 1), (1, 0)])
        return partial[:rows].astype(F32) + theirs.astype(F32)
    return lax.psum_scatter(partial, "mlp", scatter_dimension=0, tiled=True).astype(F32)


def across_rows(left, right):
    return lax.dot_general(left, right, (((0,), (0,)), ((), ())), preferred_element_type=F32)


def across_width(left, right):
    return lax.dot_general(left, right, (((1,), (1,)), ((), ())), preferred_element_type=F32)


def body(fields, cotangent, conv_weight, norm_gain, weight_in, weight_out):
    lat, slots, width = fields.shape
    slots_pad = -(-slots // 16) * 16
    held = live_count()
    slot_live = lax.broadcasted_iota(jnp.int32, (1, slots, 1), 1) < held
    spare = ((0, 0), (0, slots_pad - slots), (0, 0))
    where = places(lat, held)
    taps = jnp.broadcast_to(
        conv_weight.astype(F32).reshape(KS * KS, 1, width), (KS * KS, 8, width)
    )
    gain = norm_gain.astype(F32).reshape(1, width)
    cot_all = all_rows(jnp.pad(jnp.where(slot_live, cotangent, 0), spare).reshape(-1, width))

    grid = (lat, slots_pad, width)
    normed, hat, inv = kernel_call(
        forward_kernel, lat, slots, slots_pad, width,
        (
            jax.ShapeDtypeStruct(grid, BF16),
            jax.ShapeDtypeStruct(grid, F32),
            jax.ShapeDtypeStruct((lat, slots_pad, LANES), F32),
        ),
        grid,
        (where,) + halo(fields, slots, held) + (taps, gain),
    )
    normed_all = all_rows(normed.reshape(-1, width))

    hid = weight_in.shape[1] // 2
    pieces = (slice(0, hid), slice(hid, 2 * hid))
    bits = lon_bits()
    fast, slow = bits[:2], bits[2:]
    turned = fast[::-1]
    order = Order()
    seconds, opened, gates = [], [], []
    for cols, bit in zip(pieces, fast):
        hidden = jnp.dot(normed_all, weight_in[:, cols], preferred_element_type=F32)
        cumulative, density = gate(hidden)
        activated = (hidden * cumulative).astype(BF16)
        seconds.append(across_rows(activated, cot_all).astype(BF16)[None])
        opened += scatter_open(order, seconds[-1:], [bit])
        gates.append(cumulative + hidden * density)
    grad_hidden = jnp.concatenate(
        [
            (across_width(cot_all, weight_out[cols]) * slope).astype(BF16)
            for cols, slope in zip(pieces, gates)
        ],
        axis=1,
    )
    firsts, opened_first = [], []
    half = width // 2
    for cols, bit in zip((slice(0, half), slice(half, width)), fast):
        firsts.append(across_rows(normed_all[:, cols], grad_hidden).astype(BF16)[None])
        opened_first += scatter_open(order, firsts[-1:], [bit])
    partial = across_width(after(grad_hidden, order.last), weight_in).astype(BF16)
    grad_normed = own_rows_sum(partial)

    cells = lax.axis_size("mlp") * lat * LON
    factor = jnp.float32(1.0 / math.sqrt(cells))

    part2, got2 = scatter_step(order, seconds, opened, fast, turned)
    scaled = grad_normed.reshape(grid) * gain
    inv = inv[:, :, :1]
    grad_mixed = inv * (
        scaled
        - jnp.mean(scaled, axis=-1, keepdims=True)
        - hat * jnp.mean(scaled * hat, axis=-1, keepdims=True)
    )
    grad_mixed = grad_mixed.astype(BF16)
    around = halo(grad_mixed, slots, held)
    part2, got2 = scatter_step(order, part2, got2, turned, slow[:1])
    part1, got1 = scatter_step(order, firsts, opened_first, fast, turned)
    for bit, later in zip(slow[:-1], slow[1:]):
        part2, got2 = scatter_step(order, part2, got2, [bit], [later])
    last2 = [(halves_added(cut(part2[0], upper(slow[-1])), got2[0]) * factor).astype(BF16)]
    share2 = last2[0]
    for bit in reversed(slow):
        share2 = merged(upper(bit), share2, order.swap(share2, bit))
    part1, got1 = scatter_step(order, part1, got1, turned, slow[:1])

    def open_pair(share):
        parts = [share[0:1], share[1:2]]
        return parts, [order.swap(p, b) for p, b in zip(parts, turned)]

    def close_pair(parts, got, bits):
        return [merged(upper(b), p, g) for p, g, b in zip(parts, got, bits)]

    wide2, got2 = open_pair(share2)
    for bit, later in zip(slow[:-1], slow[1:]):
        part1, got1 = scatter_step(order, part1, got1, [bit], [later])
    share1 = (halves_added(cut(part1[0], upper(slow[-1])), got1[0]) * factor).astype(BF16)
    wide2 = close_pair(wide2, got2, turned)
    got2 = [order.swap(p, b) for p, b in zip(wide2, fast)]
    for bit in reversed(slow):
        share1 = merged(upper(bit), share1, order.swap(share1, bit))
    wide1, got1 = open_pair(share1)
    wide1 = close_pair(wide1, got1, turned)
    got1 = [order.swap(p, b) for p, b in zip(wide1, fast)]

    own, other, left, right = around
    other = after(other, order.last)
    result = kernel_call(
        backward_kernel, lat, slots, slots_pad, width,
        jax.ShapeDtypeStruct((lat, slots, width), BF16),
        (lat, slots_pad, LANES),
        (where, own, other, left, right, taps, cotangent),
    )
    out_second = jnp.concatenate([v[0] for v in close_pair(wide2, got2, fast)], axis=0)
    out_first = jnp.concatenate([v[0] for v in close_pair(wide1, got1, fast)], axis=0)
    return (result, out_first, out_second)


def solution(mesh):
    in_specs = (
        P("mlp", "lon", None),
        P("mlp", "lon", None),
        P(),
        P(),
        P(None, "mlp"),
        P("mlp", None),
    )
    out_specs = (P("mlp", "lon", None), P(None, "mlp"), P("mlp", None))
    return jax.shard_map(body, mesh=mesh, in_specs=in_specs, out_specs=out_specs, check_vma=False)
```

```python
import functools
import math

import jax
import jax.numpy as jnp
from jax import lax
from jax.experimental import pallas as pl
from jax.experimental.pallas import tpu as pltpu
from jax.sharding import PartitionSpec as P

KS = 7
LON = 1440
REACH = KS // 2
LANES = 128
BF16 = jnp.bfloat16
F32 = jnp.float32
LEAD = 8


def passed_along(value, axis, by):
    count = lax.axis_size(axis)
    return lax.ppermute(value, axis, [(i, (i + by) % count) for i in range(count)])


def after(value, *others):
    return lax.optimization_barrier((value,) + others)[0]


def live_count():
    members = lax.axis_size("lon")
    position = lax.axis_index("lon")
    return LON // members + (position < LON % members).astype(jnp.int32)


def halo(own, slots, held):
    lat, count = own.shape[0], lax.axis_size("mlp")
    if count == 2:
        mine = jnp.where(lax.axis_index("mlp") == 0, own[lat - REACH :], own[:REACH])
        other = lax.ppermute(mine, "mlp", [(0, 1), (1, 0)])
    else:
        ends = count - 1
        other = jnp.concatenate(
            [
                lax.ppermute(own[lat - REACH :], "mlp", [(i, i + 1) for i in range(ends)]),
                lax.ppermute(own[:REACH], "mlp", [(i + 1, i) for i in range(ends)]),
            ],
            axis=0,
        )
    even = LON % lax.axis_size("lon") == 0
    both = (own, other)
    first = jnp.concatenate([v[:, :REACH] for v in both], axis=0)
    if even:
        last = jnp.concatenate([v[:, slots - REACH : slots] for v in both], axis=0)
    else:
        last = jnp.concatenate(
            [lax.dynamic_slice_in_dim(v, held - REACH, REACH, 1) for v in both], axis=0
        )
    left = passed_along(last, "lon", 1)
    right = passed_along(first, "lon", -1)
    if not even:
        rows = jnp.concatenate([v[:, :slots] for v in both], axis=0)
        joined = jnp.concatenate([rows, jnp.zeros_like(right)], axis=1)
        joined = lax.dynamic_update_slice_in_dim(joined, right, held, 1)
        own, other, right = joined[:lat, :slots], joined[lat:, :slots], joined[:, slots:]
    return own, other, left, right


def places(lat, held):
    near = jnp.int32(0)
    if lax.axis_size("mlp") == 2:
        near = jnp.where(lax.axis_index("mlp") == 0, lat + REACH, 0).astype(jnp.int32)
        return jnp.stack([near, held.astype(jnp.int32)])
    return jnp.stack([near, held.astype(jnp.int32), jnp.int32(lat + REACH)])


def conv_tile(lat, slots, rows, flip, where_ref, own, other, left, right, taps, wide, lane, sink):
    groups = other.shape[0] // REACH
    wide[REACH : REACH + lat, LEAD : LEAD + slots, :] = own[:, :slots, lane].astype(F32)
    wide[REACH : REACH + lat, LEAD - REACH : LEAD, :] = left[:lat, :, lane].astype(F32)
    wide[REACH : REACH + lat, LEAD + slots : LEAD + slots + REACH, :] = right[:lat, :, lane].astype(F32)
    for g in range(groups):
        for k in range(REACH):
            at, src = where_ref[2 * g] + k, g * REACH + k
            wide[at, LEAD : LEAD + slots, :] = other[src, :slots, lane].astype(F32)
            wide[at, LEAD - REACH : LEAD, :] = left[lat + src, :, lane].astype(F32)
            wide[at, LEAD + slots : LEAD + slots + REACH, :] = right[lat + src, :, lane].astype(F32)

    def step(jt, carry):
        start = jt * 16
        acc = [[jnp.zeros((8, LANES), F32) for _ in range(lat)] for _ in range(2)]
        for b in range(KS):
            used = [a * KS + b for a in range(KS)]
            if flip:
                used = [KS * KS - 1 - t for t in used]
            taken = [taps[t] for t in used]
            for r in rows:
                for half in range(2):
                    cells = wide[r, pl.ds(start + 8 * half + LEAD - REACH + b, 8), :]
                    for i in range(max(0, r - KS + 1), min(lat, r + 1)):
                        acc[half][i] = acc[half][i] + taken[r - i] * cells
        for half in range(2):
            for i in range(lat):
                sink(i, pl.ds(pl.multiple_of(start + 8 * half, 8), 8), acc[half][i])
        return carry

    lax.fori_loop(0, -(-slots // 16), step, 0)


def conv(lat, slots, flip, where_ref, own, other, left, right, weight, taps, wide, finish, sink):
    width = own.shape[-1]

    def over(rows):
        def channels(ct, carry):
            lane = pl.ds(pl.multiple_of(ct * LANES, LANES), LANES)
            for t in range(KS * KS):
                taps[t] = jnp.broadcast_to(weight[t : t + 1, lane], (8, LANES))
            conv_tile(
                lat, slots, rows, flip, where_ref, own, other, left, right, taps, wide, lane,
                functools.partial(sink, lane),
            )
            finish(lane)
            return carry

        lax.fori_loop(0, width // LANES, channels, 0)

    if other.shape[0] == REACH:
        first = where_ref[0] != 0
        pl.when(first)(lambda: over(range(REACH, lat + 2 * REACH)))
        pl.when(jnp.logical_not(first))(lambda: over(range(lat + REACH)))
    else:
        over(range(lat + 2 * REACH))


def forward_kernel(
    lat, slots, where_ref, own, other, left, right, weight, gain, normed, hat, inv, taps, wide, mixed
):
    def sink(lane, i, at, value):
        mixed[i, at, lane] = value

    conv(
        lat, slots, False, where_ref, own, other, left, right, weight, taps, wide,
        lambda lane: None, sink,
    )
    tile = 32 if mixed.shape[1] % 32 == 0 else 16
    tiles = mixed.shape[1] // tile

    def norm(step, carry):
        i, start = step // tiles, pl.multiple_of(step % tiles * tile, tile)
        at = pl.ds(start, tile)
        values = mixed[i, at, :]
        centred = values - jnp.mean(values, axis=-1, keepdims=True)
        scale = lax.rsqrt(jnp.mean(centred * centred, axis=-1, keepdims=True) + 1e-06)
        live = start + lax.broadcasted_iota(jnp.int32, (tile, 1), 0) < where_ref[1]
        unit = jnp.where(live, centred * scale, 0.0)
        hat[i, at, :] = unit
        normed[i, at, :] = (unit * gain[...]).astype(BF16)
        inv[i, at, :] = jnp.broadcast_to(jnp.where(live, scale, 0.0), (tile, LANES))
        return carry

    lax.fori_loop(0, lat * tiles, norm, 0)


def backward_kernel(
    lat, slots, where_ref, own, other, left, right, weight, cot, out, taps, wide, mixed
):
    def sink(lane, i, at, value):
        mixed[i, at, :] = value

    def finish(lane):
        live = lax.broadcasted_iota(jnp.int32, (slots, 1), 0) < where_ref[1]
        for i in range(lat):
            total = cot[i, :, lane].astype(F32) + mixed[i, :slots, :]
            out[i, :, lane] = jnp.where(live, total, 0.0).astype(BF16)

    conv(lat, slots, True, where_ref, own, other, left, right, weight, taps, wide, finish, sink)


def kernel_call(kernel, lat, slots, slots_pad, width, outs, mixed, operands):
    vmem = pl.BlockSpec(memory_space=pltpu.VMEM)
    flops = 2 * lat * slots_pad * width * KS * KS
    return pl.pallas_call(
        functools.partial(kernel, lat, slots),
        out_shape=outs,
        in_specs=[pl.BlockSpec(memory_space=pltpu.SMEM)] + [vmem] * (len(operands) - 1),
        out_specs=jax.tree.map(lambda _: vmem, outs),
        scratch_shapes=[
            pltpu.VMEM((KS * KS, 8, LANES), F32),
            pltpu.VMEM((lat + 2 * REACH, slots_pad + 16, LANES), F32),
            pltpu.VMEM(mixed, F32),
        ],
        compiler_params=pltpu.CompilerParams(vmem_limit_bytes=32 * 2**20),
        cost_estimate=pl.CostEstimate(flops=flops, bytes_accessed=8 * 2**20, transcendentals=0),
    )(*operands)


def gate(values):
    cumulative = 0.5 * (1.0 + lax.erf(values * (1.0 / math.sqrt(2.0))))
    density = jnp.exp(-0.5 * values * values) * (1.0 / math.sqrt(2.0 * math.pi))
    return cumulative, density


def upper(bit):
    return (lax.axis_index("lon") & bit) // bit


def swapped(value, bit):
    count = lax.axis_size("lon")
    return lax.ppermute(value, "lon", [(i, i ^ bit) for i in range(count)])


def cut(part, which):
    half = part.shape[1] // 2
    return lax.dynamic_slice_in_dim(part, which * half, half, 1)


def merged(low_first, own, got):
    high = low_first == 1
    return jnp.concatenate([jnp.where(high, got, own), jnp.where(high, own, got)], axis=1)


def lon_bits():
    bits, bit = [], 1
    while bit < lax.axis_size("lon"):
        bits.append(bit)
        bit *= 2
    return bits


class Fence:
    def __init__(self):
        self.past = ()

    def behind(self, value):
        return after(value, *self.past) if self.past else value

    def mark(self, *values):
        self.past = values


class Unit:
    def __init__(self, fence, piece, factor):
        bits = lon_bits()
        fast, slow = bits[:2], bits[2:]
        down = [(b, True) for b in [tuple(fast), tuple(fast[::-1])] + [(b,) for b in slow]]
        self.steps = down + [(b, False) for b, _ in reversed(down)]
        self.fence, self.factor = fence, factor
        self.parts, self.at, self.got = [piece], 0, None
        self.open()

    def open(self):
        self.bits, self.summing = self.steps[self.at]
        if len(self.bits) != len(self.parts):
            if len(self.bits) == 1:
                self.parts = [jnp.concatenate(self.parts, axis=0)]
            else:
                self.parts = [self.parts[0][0:1], self.parts[0][1:2]]
        sent = [
            cut(p, 1 - upper(b)) if self.summing else p for p, b in zip(self.parts, self.bits)
        ]
        sent = [self.fence.behind(v) for v in sent]
        self.fence.mark(*sent)
        self.got = [swapped(v, b) for v, b in zip(sent, self.bits)]

    def close(self):
        scaled = self.summing and not self.steps[self.at + 1][1]
        parts = []
        for p, g, b in zip(self.parts, self.got, self.bits):
            if self.summing:
                total = cut(p, upper(b)).astype(F32) + g.astype(F32)
                parts.append((total * self.factor if scaled else total).astype(BF16))
            else:
                parts.append(merged(upper(b), p, g))
        self.parts = parts
        self.at += 1

    def advance(self, times=1):
        for _ in range(times):
            self.close()
            self.open()

    def result(self):
        while self.at < len(self.steps) - 1:
            self.advance()
        self.close()
        return [p[0] for p in self.parts]


def all_rows(own):
    if lax.axis_size("mlp") == 2:
        return jnp.concatenate([own, lax.ppermute(own, "mlp", [(0, 1), (1, 0)])], axis=0)
    return lax.all_gather(own, "mlp", axis=0, tiled=True)


def own_rows_sum(partial):
    if lax.axis_size("mlp") == 2:
        rows = partial.shape[0] // 2
        theirs = lax.ppermute(partial[rows:], "mlp", [(0, 1), (1, 0)])
        return partial[:rows].astype(F32) + theirs.astype(F32)
    return lax.psum_scatter(partial, "mlp", scatter_dimension=0, tiled=True).astype(F32)


def across_rows(left, right):
    return lax.dot_general(left, right, (((0,), (0,)), ((), ())), preferred_element_type=F32)


def across_width(left, right):
    return lax.dot_general(left, right, (((1,), (1,)), ((), ())), preferred_element_type=F32)


def body(fields, cotangent, conv_weight, norm_gain, weight_in, weight_out):
    lat, slots, width = fields.shape
    slots_pad = -(-slots // 16) * 16
    held = live_count()
    slot_live = lax.broadcasted_iota(jnp.int32, (1, slots, 1), 1) < held
    spare = ((0, 0), (0, slots_pad - slots), (0, 0))
    where = places(lat, held)
    taps = conv_weight.astype(F32).reshape(KS * KS, width)
    gain = norm_gain.astype(F32).reshape(1, width)
    cot_all = all_rows(jnp.pad(jnp.where(slot_live, cotangent, 0), spare).reshape(-1, width))

    grid = (lat, slots_pad, width)
    normed, hat, inv = kernel_call(
        forward_kernel, lat, slots, slots_pad, width,
        (
            jax.ShapeDtypeStruct(grid, BF16),
            jax.ShapeDtypeStruct(grid, F32),
            jax.ShapeDtypeStruct((lat, slots_pad, LANES), F32),
        ),
        grid,
        (where,) + halo(fields, slots, held) + (taps, gain),
    )
    normed_all = all_rows(normed.reshape(-1, width))

    cells = lax.axis_size("mlp") * lat * LON
    factor = jnp.float32(1.0 / math.sqrt(cells))
    fence = Fence()

    def unit(grad):
        return Unit(fence, grad.astype(BF16).reshape(2, grad.shape[0] // 2, -1), factor)

    hid = weight_in.shape[1] // 2
    pieces = (slice(0, hid), slice(hid, 2 * hid))
    seconds, slopes = [], []
    for cols in pieces:
        hidden = jnp.dot(fence.behind(normed_all), weight_in[:, cols], preferred_element_type=F32)
        cumulative, density = gate(hidden)
        activated = (hidden * cumulative).astype(BF16)
        seconds.append(unit(across_rows(activated, cot_all)))
        slopes.append(cumulative + hidden * density)
    a, b = seconds
    a.advance()
    grad_hidden = jnp.concatenate(
        [
            (across_width(fence.behind(cot_all), weight_out[cols]) * slope).astype(BF16)
            for cols, slope in zip(pieces, slopes)
        ],
        axis=1,
    )
    fence.mark(grad_hidden)
    a.advance()
    b.advance()
    half = width // 2
    c = unit(across_rows(fence.behind(normed_all[:, :half]), grad_hidden))
    a.advance()
    d = unit(across_rows(fence.behind(normed_all[:, half:]), grad_hidden))
    a.advance()
    partial = across_width(fence.behind(grad_hidden), weight_in).astype(BF16)
    fence.mark(partial)
    grad_normed = own_rows_sum(partial)
    a.advance()
    b.advance()
    a.advance()
    c.advance()
    scaled = fence.behind(grad_normed).reshape(grid) * gain
    inv = inv[:, :, :1]
    grad_mixed = inv * (
        scaled
        - jnp.mean(scaled, axis=-1, keepdims=True)
        - hat * jnp.mean(scaled * hat, axis=-1, keepdims=True)
    )
    grad_mixed = grad_mixed.astype(BF16)
    fence.mark(grad_mixed)
    around = halo(grad_mixed, slots, held)
    b.advance(2)
    a.advance()
    d.advance()
    b.advance()
    c.advance()
    b.advance()
    c.advance()
    d.advance()
    seconds = a.result()
    fence.mark(*seconds)
    c.advance()
    b.advance()
    c.advance()
    d.advance()
    c.advance()
    d.advance()
    seconds += b.result()
    fence.mark(*seconds)
    c.advance()
    d.advance(3)
    own, other, left, right = around
    result = kernel_call(
        backward_kernel, lat, slots, slots_pad, width,
        jax.ShapeDtypeStruct((lat, slots, width), BF16),
        (lat, slots_pad, LANES),
        (where, own, fence.behind(other), left, right, taps, cotangent),
    )
    out_second = jnp.concatenate(seconds, axis=0)
    out_first = jnp.concatenate(c.result() + d.result(), axis=0)
    return (result, out_first, out_second)


def solution(mesh):
    in_specs = (
        P("mlp", "lon", None),
        P("mlp", "lon", None),
        P(),
        P(),
        P(None, "mlp"),
        P("mlp", None),
    )
    out_specs = (P("mlp", "lon", None), P(None, "mlp"), P("mlp", None))
    return jax.shard_map(body, mesh=mesh, in_specs=in_specs, out_specs=out_specs, check_vma=False)
```

```python
import functools
import math

import jax
import jax.numpy as jnp
from jax import lax
from jax.experimental import pallas as pl
from jax.experimental.pallas import tpu as pltpu
from jax.sharding import PartitionSpec as P

KS = 7
LON = 1440
REACH = KS // 2
LANES = 128
BF16 = jnp.bfloat16
F32 = jnp.float32
LEAD = 8


def passed_along(value, axis, by):
    count = lax.axis_size(axis)
    return lax.ppermute(value, axis, [(i, (i + by) % count) for i in range(count)])


def after(value, *others):
    return lax.optimization_barrier((value,) + others)[0]


def live_count():
    members = lax.axis_size("lon")
    position = lax.axis_index("lon")
    return LON // members + (position < LON % members).astype(jnp.int32)


def halo(own, slots, held):
    lat, count = own.shape[0], lax.axis_size("mlp")
    if count == 2:
        mine = jnp.where(lax.axis_index("mlp") == 0, own[lat - REACH :], own[:REACH])
        other = lax.ppermute(mine, "mlp", [(0, 1), (1, 0)])
    else:
        ends = count - 1
        other = jnp.concatenate(
            [
                lax.ppermute(own[lat - REACH :], "mlp", [(i, i + 1) for i in range(ends)]),
                lax.ppermute(own[:REACH], "mlp", [(i + 1, i) for i in range(ends)]),
            ],
            axis=0,
        )
    even = LON % lax.axis_size("lon") == 0
    both = (own, other)
    first = jnp.concatenate([v[:, :REACH] for v in both], axis=0)
    if even:
        last = jnp.concatenate([v[:, slots - REACH : slots] for v in both], axis=0)
    else:
        last = jnp.concatenate(
            [lax.dynamic_slice_in_dim(v, held - REACH, REACH, 1) for v in both], axis=0
        )
    left = passed_along(last, "lon", 1)
    right = passed_along(first, "lon", -1)
    if not even:
        rows = jnp.concatenate([v[:, :slots] for v in both], axis=0)
        joined = jnp.concatenate([rows, jnp.zeros_like(right)], axis=1)
        joined = lax.dynamic_update_slice_in_dim(joined, right, held, 1)
        own, other, right = joined[:lat, :slots], joined[lat:, :slots], joined[:, slots:]
    return own, other, left, right


def places(lat, held):
    near = jnp.int32(0)
    if lax.axis_size("mlp") == 2:
        near = jnp.where(lax.axis_index("mlp") == 0, lat + REACH, 0).astype(jnp.int32)
        return jnp.stack([near, held.astype(jnp.int32)])
    return jnp.stack([near, held.astype(jnp.int32), jnp.int32(lat + REACH)])


def conv_tile(lat, slots, rows, flip, where_ref, own, other, left, right, taps, wide, lane, sink):
    groups = other.shape[0] // REACH
    wide[REACH : REACH + lat, LEAD : LEAD + slots, :] = own[:, :slots, lane].astype(F32)
    wide[REACH : REACH + lat, LEAD - REACH : LEAD, :] = left[:lat, :, lane].astype(F32)
    wide[REACH : REACH + lat, LEAD + slots : LEAD + slots + REACH, :] = right[:lat, :, lane].astype(F32)
    for g in range(groups):
        for k in range(REACH):
            at, src = where_ref[2 * g] + k, g * REACH + k
            wide[at, LEAD : LEAD + slots, :] = other[src, :slots, lane].astype(F32)
            wide[at, LEAD - REACH : LEAD, :] = left[lat + src, :, lane].astype(F32)
            wide[at, LEAD + slots : LEAD + slots + REACH, :] = right[lat + src, :, lane].astype(F32)

    def step(jt, carry):
        start = jt * 16
        acc = [[jnp.zeros((8, LANES), F32) for _ in range(lat)] for _ in range(2)]
        for b in range(KS):
            used = [a * KS + b for a in range(KS)]
            if flip:
                used = [KS * KS - 1 - t for t in used]
            taken = [taps[t] for t in used]
            for r in rows:
                for half in range(2):
                    cells = wide[r, pl.ds(start + 8 * half + LEAD - REACH + b, 8), :]
                    for i in range(max(0, r - KS + 1), min(lat, r + 1)):
                        acc[half][i] = acc[half][i] + taken[r - i] * cells
        for half in range(2):
            for i in range(lat):
                sink(i, pl.ds(pl.multiple_of(start + 8 * half, 8), 8), acc[half][i])
        return carry

    lax.fori_loop(0, -(-slots // 16), step, 0)


def conv(lat, slots, flip, where_ref, own, other, left, right, weight, taps, wide, finish, sink):
    width = own.shape[-1]

    def over(rows):
        def channels(ct, carry):
            lane = pl.ds(pl.multiple_of(ct * LANES, LANES), LANES)
            for t in range(KS * KS):
                taps[t] = jnp.broadcast_to(weight[t : t + 1, lane], (8, LANES))
            conv_tile(
                lat, slots, rows, flip, where_ref, own, other, left, right, taps, wide, lane,
                functools.partial(sink, lane),
            )
            finish(lane)
            return carry

        lax.fori_loop(0, width // LANES, channels, 0)

    if other.shape[0] == REACH:
        first = where_ref[0] != 0
        pl.when(first)(lambda: over(range(REACH, lat + 2 * REACH)))
        pl.when(jnp.logical_not(first))(lambda: over(range(lat + REACH)))
    else:
        over(range(lat + 2 * REACH))


def forward_kernel(
    lat, slots, where_ref, own, other, left, right, weight, gain, normed, hat, inv, taps, wide, mixed
):
    def sink(lane, i, at, value):
        mixed[i, at, lane] = value

    conv(
        lat, slots, False, where_ref, own, other, left, right, weight, taps, wide,
        lambda lane: None, sink,
    )
    tile = 32 if mixed.shape[1] % 32 == 0 else 16
    tiles = mixed.shape[1] // tile

    def norm(step, carry):
        i, start = step // tiles, pl.multiple_of(step % tiles * tile, tile)
        at = pl.ds(start, tile)
        values = mixed[i, at, :]
        centred = values - jnp.mean(values, axis=-1, keepdims=True)
        scale = lax.rsqrt(jnp.mean(centred * centred, axis=-1, keepdims=True) + 1e-06)
        live = start + lax.broadcasted_iota(jnp.int32, (tile, 1), 0) < where_ref[1]
        unit = jnp.where(live, centred * scale, 0.0)
        hat[i, at, :] = unit
        normed[i, at, :] = (unit * gain[...]).astype(BF16)
        inv[i, at, :] = jnp.broadcast_to(jnp.where(live, scale, 0.0), (tile, LANES))
        return carry

    lax.fori_loop(0, lat * tiles, norm, 0)


def backward_kernel(
    lat, slots, where_ref, own, other, left, right, weight, cot, out, taps, wide, mixed
):
    def sink(lane, i, at, value):
        mixed[i, at, :] = value

    def finish(lane):
        live = lax.broadcasted_iota(jnp.int32, (slots, 1), 0) < where_ref[1]
        for i in range(lat):
            total = cot[i, :, lane].astype(F32) + mixed[i, :slots, :]
            out[i, :, lane] = jnp.where(live, total, 0.0).astype(BF16)

    conv(lat, slots, True, where_ref, own, other, left, right, weight, taps, wide, finish, sink)


def kernel_call(kernel, lat, slots, slots_pad, width, outs, mixed, operands):
    vmem = pl.BlockSpec(memory_space=pltpu.VMEM)
    flops = 2 * lat * slots_pad * width * KS * KS
    return pl.pallas_call(
        functools.partial(kernel, lat, slots),
        out_shape=outs,
        in_specs=[pl.BlockSpec(memory_space=pltpu.SMEM)] + [vmem] * (len(operands) - 1),
        out_specs=jax.tree.map(lambda _: vmem, outs),
        scratch_shapes=[
            pltpu.VMEM((KS * KS, 8, LANES), F32),
            pltpu.VMEM((lat + 2 * REACH, slots_pad + 16, LANES), F32),
            pltpu.VMEM(mixed, F32),
        ],
        compiler_params=pltpu.CompilerParams(vmem_limit_bytes=12 * 2**20),
        cost_estimate=pl.CostEstimate(flops=flops, bytes_accessed=8 * 2**20, transcendentals=0),
    )(*operands)


def gate(values):
    cumulative = 0.5 * (1.0 + lax.erf(values * (1.0 / math.sqrt(2.0))))
    density = jnp.exp(-0.5 * values * values) * (1.0 / math.sqrt(2.0 * math.pi))
    return cumulative, density


def upper(bit):
    return (lax.axis_index("lon") & bit) // bit


def swapped(value, bit):
    count = lax.axis_size("lon")
    return lax.ppermute(value, "lon", [(i, i ^ bit) for i in range(count)])


def cut(part, which):
    half = part.shape[0] // 2
    return lax.dynamic_slice_in_dim(part, which * half, half, 0)


def merged(low_first, own, got):
    high = low_first == 1
    return jnp.concatenate([jnp.where(high, got, own), jnp.where(high, own, got)], axis=0)


def lon_bits():
    bits, bit = [], 1
    while bit < lax.axis_size("lon"):
        bits.append(bit)
        bit *= 2
    return bits


class Fence:
    def __init__(self):
        self.past = ()

    def behind(self, value):
        return after(value, *self.past) if self.past else value

    def mark(self, *values):
        self.past = values


def summed_far(part, bits, turn):
    near = bits[0]
    count = lax.axis_size("lon")
    firsts = [(first + turn) % near for first in range(near)]
    groups = [list(range(first, count, near)) for first in firsts]
    return lax.psum(part, "lon", axis_index_groups=groups)


class Unit:
    def __init__(self, fence, piece):
        bits = lon_bits()
        self.fast, self.slow = bits[:2], bits[2:]
        self.fence = fence
        self.parts = [piece[0], piece[1]]
        self.open(self.fast, True)

    def open(self, bits, summing):
        self.bits, self.summing = bits, summing
        sent = [cut(p, 1 - upper(b)) if summing else p for p, b in zip(self.parts, bits)]
        sent = [self.fence.behind(v) for v in sent]
        self.fence.mark(*sent)
        self.got = [swapped(v, b) for v, b in zip(sent, bits)]

    def close(self):
        parts = []
        for p, g, b in zip(self.parts, self.got, self.bits):
            p = self.fence.behind(p)
            if self.summing:
                parts.append((cut(p, upper(b)).astype(F32) + g.astype(F32)).astype(BF16))
            else:
                parts.append(merged(upper(b), p, g))
        self.parts = parts
        self.fence.mark(*parts)

    def scatter(self):
        self.close()
        self.open(self.fast[::-1], True)

    def far(self, turn):
        self.close()
        self.total = summed_far(jnp.concatenate(self.parts, axis=0), self.slow, turn)

    def gather(self):
        half = self.total.shape[0] // 2
        total = self.fence.behind(self.total)
        self.parts = [total[:half], total[half:]]
        self.open(self.fast[::-1], False)

    def widen(self):
        self.close()
        self.open(self.fast, False)

    def result(self):
        self.close()
        return self.parts


def all_rows(own):
    if lax.axis_size("mlp") == 2:
        return jnp.concatenate([own, lax.ppermute(own, "mlp", [(0, 1), (1, 0)])], axis=0)
    return lax.all_gather(own, "mlp", axis=0, tiled=True)


def own_rows_sum(partial):
    if lax.axis_size("mlp") == 2:
        rows = partial.shape[0] // 2
        theirs = lax.ppermute(partial[rows:], "mlp", [(0, 1), (1, 0)])
        return partial[:rows].astype(F32) + theirs.astype(F32)
    return lax.psum_scatter(partial, "mlp", scatter_dimension=0, tiled=True).astype(F32)


def across_rows(left, right):
    return lax.dot_general(left, right, (((0,), (0,)), ((), ())), preferred_element_type=F32)


def across_width(left, right):
    return lax.dot_general(left, right, (((1,), (1,)), ((), ())), preferred_element_type=F32)


def body(fields, cotangent, conv_weight, norm_gain, weight_in, weight_out):
    lat, slots, width = fields.shape
    slots_pad = -(-slots // 16) * 16
    held = live_count()
    slot_live = lax.broadcasted_iota(jnp.int32, (1, slots, 1), 1) < held
    spare = ((0, 0), (0, slots_pad - slots), (0, 0))
    where = places(lat, held)
    taps = conv_weight.astype(F32).reshape(KS * KS, width)
    gain = norm_gain.astype(F32).reshape(1, width)
    cot_all = all_rows(jnp.pad(jnp.where(slot_live, cotangent, 0), spare).reshape(-1, width))

    grid = (lat, slots_pad, width)
    normed, hat, inv = kernel_call(
        forward_kernel, lat, slots, slots_pad, width,
        (
            jax.ShapeDtypeStruct(grid, BF16),
            jax.ShapeDtypeStruct(grid, F32),
            jax.ShapeDtypeStruct((lat, slots_pad, LANES), F32),
        ),
        grid,
        (where,) + halo(fields, slots, held) + (taps, gain),
    )
    normed_all = all_rows(normed.reshape(-1, width))

    cells = lax.axis_size("mlp") * lat * LON
    factor = jnp.float32(1.0 / math.sqrt(cells))
    fence = Fence()

    def unit(grad):
        return Unit(fence, (grad * factor).astype(BF16).reshape(2, grad.shape[0] // 2, -1))

    hid = weight_in.shape[1] // 2
    pieces = (slice(0, hid), slice(hid, 2 * hid))
    seconds, slopes = [], []
    for cols in pieces:
        hidden = jnp.dot(fence.behind(normed_all), weight_in[:, cols], preferred_element_type=F32)
        cumulative, density = gate(hidden)
        activated = (hidden * cumulative).astype(BF16)
        seconds.append(unit(across_rows(activated, cot_all)))
        slopes.append(cumulative + hidden * density)
    a, b = seconds
    a.scatter()
    grad_hidden = jnp.concatenate(
        [
            (across_width(fence.behind(cot_all), weight_out[cols]) * slope).astype(BF16)
            for cols, slope in zip(pieces, slopes)
        ],
        axis=1,
    )
    fence.mark(grad_hidden)
    a.far(0)
    b.scatter()
    half = width // 2
    c = unit(across_rows(fence.behind(normed_all[:, :half]), grad_hidden))
    b.far(1)
    d = unit(across_rows(fence.behind(normed_all[:, half:]), grad_hidden))
    c.scatter()
    partial = across_width(fence.behind(grad_hidden), weight_in).astype(BF16)
    fence.mark(partial)
    grad_normed = own_rows_sum(partial)
    c.far(2)
    a.gather()
    d.scatter()
    scaled = fence.behind(grad_normed).reshape(grid) * gain
    inv = inv[:, :, :1]
    grad_mixed = inv * (
        scaled
        - jnp.mean(scaled, axis=-1, keepdims=True)
        - hat * jnp.mean(scaled * hat, axis=-1, keepdims=True)
    )
    grad_mixed = grad_mixed.astype(BF16)
    fence.mark(grad_mixed)
    around = halo(grad_mixed, slots, held)
    a.widen()
    d.far(3)
    b.gather()
    seconds = a.result()
    b.widen()
    c.gather()
    seconds += b.result()
    c.widen()
    d.gather()
    firsts = c.result()
    d.widen()
    own, other, left, right = around
    result = kernel_call(
        backward_kernel, lat, slots, slots_pad, width,
        jax.ShapeDtypeStruct((lat, slots, width), BF16),
        (lat, slots_pad, LANES),
        (where, own, fence.behind(other), left, right, taps, cotangent),
    )
    out_second = jnp.concatenate(seconds, axis=0)
    out_first = jnp.concatenate(firsts + d.result(), axis=0)
    return (result, out_first, out_second)


def solution(mesh):
    in_specs = (
        P("mlp", "lon", None),
        P("mlp", "lon", None),
        P(),
        P(),
        P(None, "mlp"),
        P("mlp", None),
    )
    out_specs = (P("mlp", "lon", None), P(None, "mlp"), P("mlp", None))
    return jax.shard_map(body, mesh=mesh, in_specs=in_specs, out_specs=out_specs, check_vma=False)
```

```python
import functools
import math

import jax
import jax.numpy as jnp
from jax import lax
from jax.experimental import pallas as pl
from jax.experimental.pallas import tpu as pltpu
from jax.sharding import PartitionSpec as P

KS = 7
LON = 1440
REACH = KS // 2
LANES = 128
BF16 = jnp.bfloat16
F32 = jnp.float32
LEAD = 8


def passed_along(value, axis, by):
    count = lax.axis_size(axis)
    return lax.ppermute(value, axis, [(i, (i + by) % count) for i in range(count)])


def live_count():
    members = lax.axis_size("lon")
    position = lax.axis_index("lon")
    return LON // members + (position < LON % members).astype(jnp.int32)


def halo(own, slots, held):
    lat, count = own.shape[0], lax.axis_size("mlp")
    if count == 2:
        mine = jnp.where(lax.axis_index("mlp") == 0, own[lat - REACH :], own[:REACH])
        other = lax.ppermute(mine, "mlp", [(0, 1), (1, 0)])
    else:
        ends = count - 1
        other = jnp.concatenate(
            [
                lax.ppermute(own[lat - REACH :], "mlp", [(i, i + 1) for i in range(ends)]),
                lax.ppermute(own[:REACH], "mlp", [(i + 1, i) for i in range(ends)]),
            ],
            axis=0,
        )
    even = LON % lax.axis_size("lon") == 0
    both = (own, other)
    first = jnp.concatenate([v[:, :REACH] for v in both], axis=0)
    if even:
        last = jnp.concatenate([v[:, slots - REACH : slots] for v in both], axis=0)
    else:
        last = jnp.concatenate(
            [lax.dynamic_slice_in_dim(v, held - REACH, REACH, 1) for v in both], axis=0
        )
    left = passed_along(last, "lon", 1)
    right = passed_along(first, "lon", -1)
    if not even:
        rows = jnp.concatenate([v[:, :slots] for v in both], axis=0)
        joined = jnp.concatenate([rows, jnp.zeros_like(right)], axis=1)
        joined = lax.dynamic_update_slice_in_dim(joined, right, held, 1)
        own, other, right = joined[:lat, :slots], joined[lat:, :slots], joined[:, slots:]
    return own, other, jnp.concatenate([left, right], axis=1)


def places(lat, held):
    near = jnp.int32(0)
    if lax.axis_size("mlp") == 2:
        near = jnp.where(lax.axis_index("mlp") == 0, lat + REACH, 0).astype(jnp.int32)
        return jnp.stack([near, held.astype(jnp.int32)])
    return jnp.stack([near, held.astype(jnp.int32), jnp.int32(lat + REACH)])


def conv_tile(lat, slots, rows, flip, where_ref, own, other, sides, taps, wide, lane, sink):
    groups = other.shape[0] // REACH
    wide[REACH : REACH + lat, LEAD : LEAD + slots, :] = own[:, :slots, lane].astype(F32)
    ends = sides[:, :, lane].astype(F32)
    wide[REACH : REACH + lat, LEAD - REACH : LEAD, :] = ends[:lat, :REACH]
    wide[REACH : REACH + lat, LEAD + slots : LEAD + slots + REACH, :] = ends[:lat, REACH:]
    for g in range(groups):
        for k in range(REACH):
            at, src = where_ref[2 * g] + k, g * REACH + k
            wide[at, LEAD : LEAD + slots, :] = other[src, :slots, lane].astype(F32)
            wide[at, LEAD - REACH : LEAD, :] = ends[lat + src, :REACH]
            wide[at, LEAD + slots : LEAD + slots + REACH, :] = ends[lat + src, REACH:]

    def step(jt, carry):
        start = jt * 16
        acc = [[jnp.zeros((8, LANES), F32) for _ in range(lat)] for _ in range(2)]
        for b in range(KS):
            used = [a * KS + b for a in range(KS)]
            if flip:
                used = [KS * KS - 1 - t for t in used]
            taken = [taps[t] for t in used]
            for r in rows:
                for half in range(2):
                    cells = wide[r, pl.ds(start + 8 * half + LEAD - REACH + b, 8), :]
                    for i in range(max(0, r - KS + 1), min(lat, r + 1)):
                        acc[half][i] = acc[half][i] + taken[r - i] * cells
        for half in range(2):
            for i in range(lat):
                sink(i, pl.ds(pl.multiple_of(start + 8 * half, 8), 8), acc[half][i])
        return carry

    lax.fori_loop(0, -(-slots // 16), step, 0)


def conv(lat, slots, flip, where_ref, own, other, sides, weight, taps, wide, finish, sink):
    width = own.shape[-1]

    def over(rows):
        def channels(ct, carry):
            lane = pl.ds(pl.multiple_of(ct * LANES, LANES), LANES)
            for a in range(KS):
                row = weight[a, :, lane].astype(F32)
                for b in range(KS):
                    taps[a * KS + b] = jnp.broadcast_to(row[b : b + 1], (8, LANES))
            conv_tile(
                lat, slots, rows, flip, where_ref, own, other, sides, taps, wide, lane,
                functools.partial(sink, lane),
            )
            finish(lane)
            return carry

        lax.fori_loop(0, width // LANES, channels, 0)

    if other.shape[0] == REACH:
        first = where_ref[0] != 0
        pl.when(first)(lambda: over(range(REACH, lat + 2 * REACH)))
        pl.when(jnp.logical_not(first))(lambda: over(range(lat + REACH)))
    else:
        over(range(lat + 2 * REACH))


def forward_kernel(
    lat, slots, where_ref, own, other, sides, weight, gain, normed, hat, inv, taps, wide, mixed
):
    def sink(lane, i, at, value):
        mixed[i, at, lane] = value

    conv(
        lat, slots, False, where_ref, own, other, sides, weight, taps, wide,
        lambda lane: None, sink,
    )
    tile = 32 if mixed.shape[1] % 32 == 0 else 16
    tiles = mixed.shape[1] // tile

    def norm(step, carry):
        i, start = step // tiles, pl.multiple_of(step % tiles * tile, tile)
        at = pl.ds(start, tile)
        values = mixed[i, at, :]
        centred = values - jnp.mean(values, axis=-1, keepdims=True)
        scale = lax.rsqrt(jnp.mean(centred * centred, axis=-1, keepdims=True) + 1e-06)
        live = start + lax.broadcasted_iota(jnp.int32, (tile, 1), 0) < where_ref[1]
        unit = jnp.where(live, centred * scale, 0.0)
        hat[i, at, :] = unit
        normed[i, at, :] = (unit * gain[...]).astype(BF16)
        inv[i, at, :] = jnp.broadcast_to(jnp.where(live, scale, 0.0), (tile, LANES))
        return carry

    lax.fori_loop(0, lat * tiles, norm, 0)


def backward_kernel(
    lat, slots, where_ref, own, other, sides, weight, cot, out, taps, wide, mixed
):
    def sink(lane, i, at, value):
        mixed[i, at, :] = value

    def finish(lane):
        live = lax.broadcasted_iota(jnp.int32, (slots, 1), 0) < where_ref[1]
        for i in range(lat):
            total = cot[i, :, lane].astype(F32) + mixed[i, :slots, :]
            out[i, :, lane] = jnp.where(live, total, 0.0).astype(BF16)

    conv(lat, slots, True, where_ref, own, other, sides, weight, taps, wide, finish, sink)


def kernel_call(kernel, lat, slots, slots_pad, width, outs, mixed, operands):
    vmem = pl.BlockSpec(memory_space=pltpu.VMEM)
    flops = 2 * lat * slots_pad * width * KS * KS
    return pl.pallas_call(
        functools.partial(kernel, lat, slots),
        out_shape=outs,
        in_specs=[pl.BlockSpec(memory_space=pltpu.SMEM)] + [vmem] * (len(operands) - 1),
        out_specs=jax.tree.map(lambda _: vmem, outs),
        scratch_shapes=[
            pltpu.VMEM((KS * KS, 8, LANES), F32),
            pltpu.VMEM((lat + 2 * REACH, slots_pad + 16, LANES), F32),
            pltpu.VMEM(mixed, F32),
        ],
        compiler_params=pltpu.CompilerParams(vmem_limit_bytes=12 * 2**20),
        cost_estimate=pl.CostEstimate(flops=flops, bytes_accessed=8 * 2**20, transcendentals=0),
    )(*operands)


def gate(values):
    cumulative = 0.5 * (1.0 + lax.erf(values * (1.0 / math.sqrt(2.0))))
    density = jnp.exp(-0.5 * values * values) * (1.0 / math.sqrt(2.0 * math.pi))
    return cumulative, density


def upper(bit):
    return (lax.axis_index("lon") & bit) // bit


def swapped(value, bit):
    count = lax.axis_size("lon")
    return lax.ppermute(value, "lon", [(i, i ^ bit) for i in range(count)])


def cut(part, which):
    half = part.shape[0] // 2
    return lax.dynamic_slice_in_dim(part, which * half, half, 0)


def merged(low_first, own, got):
    high = low_first == 1
    return jnp.concatenate([jnp.where(high, got, own), jnp.where(high, own, got)], axis=0)


def lon_bits():
    bits, bit = [], 1
    while bit < lax.axis_size("lon"):
        bits.append(bit)
        bit *= 2
    return bits


class State:
    def __init__(self):
        self.held = {}

    def sync(self, *more):
        names = list(self.held)
        tied = lax.optimization_barrier(tuple(self.held.values()) + more)
        self.held = dict(zip(names, tied))
        return tied[len(names) :]


class Pair:
    def __init__(self, state, name, parts, ways):
        self.state, self.names, self.sent = state, (name + "0", name + "1"), None
        self.keep(parts)
        self.stages = []
        for near, far in ways:
            middle = len(far) // 2
            groups = [[b] for b in near] + [far[:middle], far[middle:]]
            down = [(g, True) for g in groups]
            self.stages.append(down + [(g[::-1], False) for g in groups[::-1]])
        self.open_next()

    def keep(self, parts):
        self.state.held.update(zip(self.names, parts))

    def parts(self):
        return [self.state.held[name] for name in self.names]

    def open(self, bits, summing):
        sent = [cut(p, 1 - upper(b)) if summing else p for p, b in zip(self.parts(), bits)]
        sent = self.state.sync(*sent) if summing else (self.state.sync(), self.parts())[1]
        self.sent = (bits, summing, [swapped(v, b) for v, b in zip(sent, bits)])

    def close(self):
        bits, summing, got = self.sent
        each = zip(self.parts(), got, bits)
        if summing:
            self.keep(
                [(cut(p, upper(b)).astype(F32) + g.astype(F32)).astype(BF16) for p, g, b in each]
            )
        else:
            self.keep([merged(upper(b), p, g) for p, g, b in each])

    def open_next(self):
        groups = [stages.pop(0) for stages in self.stages]
        summing = groups[0][1]
        steps = list(zip(*(bits for bits, _ in groups)))
        for bits in steps[:-1]:
            self.open(bits, summing)
            self.close()
        self.open(steps[-1], summing)

    def advance(self):
        self.close()
        self.open_next()


def both_ways():
    bits = lon_bits()
    fast, slow = bits[:2], bits[2:]
    return (fast, slow), (fast[::-1], slow[::-1])


def all_rows(own):
    if lax.axis_size("mlp") == 2:
        return jnp.concatenate([own, lax.ppermute(own, "mlp", [(0, 1), (1, 0)])], axis=0)
    return lax.all_gather(own, "mlp", axis=0, tiled=True)


def own_rows_sum(partial):
    if lax.axis_size("mlp") == 2:
        rows = partial.shape[0] // 2
        theirs = lax.ppermute(partial[rows:], "mlp", [(0, 1), (1, 0)])
        return partial[:rows].astype(F32) + theirs.astype(F32)
    return lax.psum_scatter(partial, "mlp", scatter_dimension=0, tiled=True).astype(F32)


def across_rows(left, right):
    return lax.dot_general(left, right, (((0,), (0,)), ((), ())), preferred_element_type=F32)


def across_width(left, right):
    return lax.dot_general(left, right, (((1,), (1,)), ((), ())), preferred_element_type=F32)


def body(fields, cotangent, conv_weight, norm_gain, weight_in, weight_out):
    lat, slots, width = fields.shape
    slots_pad = -(-slots // 16) * 16
    held = live_count()
    slot_live = lax.broadcasted_iota(jnp.int32, (1, slots, 1), 1) < held
    spare = ((0, 0), (0, slots_pad - slots), (0, 0))
    where = places(lat, held)
    gain = norm_gain.astype(F32).reshape(1, width)
    cot_all = all_rows(jnp.pad(jnp.where(slot_live, cotangent, 0), spare).reshape(-1, width))

    grid = (lat, slots_pad, width)
    normed, hat, inv = kernel_call(
        forward_kernel, lat, slots, slots_pad, width,
        (
            jax.ShapeDtypeStruct(grid, BF16),
            jax.ShapeDtypeStruct(grid, F32),
            jax.ShapeDtypeStruct((lat, slots_pad, LANES), F32),
        ),
        grid,
        (where,) + halo(fields, slots, held) + (conv_weight, gain),
    )
    normed_all = all_rows(normed.reshape(-1, width))

    cells = lax.axis_size("mlp") * lat * LON
    factor = jnp.float32(1.0 / math.sqrt(cells))
    state = State()
    ways = both_ways()

    def pair(name, grad):
        grad = (grad * factor).astype(BF16)
        half = grad.shape[0] // 2
        return Pair(state, name, (grad[:half], grad[half:]), ways)

    def go(*pairs):
        for each in pairs:
            each.advance()

    hidden = jnp.dot(normed_all, weight_in, preferred_element_type=F32)
    cumulative, density = gate(hidden)
    activated = (hidden * cumulative).astype(BF16)
    state.held["cot"] = cot_all
    a = pair("a", across_rows(activated, cot_all))
    upstream = across_width(state.held["cot"], weight_out)
    grad_hidden = (upstream * (cumulative + hidden * density)).astype(BF16)
    grad_first = (across_rows(normed_all, grad_hidden) * factor).astype(BF16)
    state.held["first"] = grad_first
    state.held["hidden"] = grad_hidden
    go(a)
    partial = across_width(state.held["hidden"], weight_in).astype(BF16)
    grad_normed = own_rows_sum(partial)
    half = width // 2
    first = state.held.pop("first")
    state.held["partial"] = partial
    b = Pair(state, "b", (first[:half], first[half:]), ways)
    go(a, a, a, b, a)
    del state.held["cot"], state.held["hidden"], state.held["partial"]
    state.held["hat"] = hat
    state.sync()
    hat = state.held.pop("hat")
    scaled = grad_normed.reshape(grid) * gain
    inv = inv[:, :, :1]
    grad_mixed = inv * (
        scaled
        - jnp.mean(scaled, axis=-1, keepdims=True)
        - hat * jnp.mean(scaled * hat, axis=-1, keepdims=True)
    )
    state.held["mixed"] = grad_mixed.astype(BF16)
    go(b, a, b, a, b, b)
    own, other, sides = halo(state.held.pop("mixed"), slots, held)
    a.close()
    go(b, b)
    state.held["sides"] = sides
    state.sync()
    result = kernel_call(
        backward_kernel, lat, slots, slots_pad, width,
        jax.ShapeDtypeStruct((lat, slots, width), BF16),
        (lat, slots_pad, LANES),
        (where, own, other, state.held["sides"], conv_weight, cotangent),
    )
    b.close()
    out_second = jnp.concatenate(a.parts(), axis=0)
    out_first = jnp.concatenate(b.parts(), axis=0)
    return (result, out_first, out_second)


def solution(mesh):
    in_specs = (
        P("mlp", "lon", None),
        P("mlp", "lon", None),
        P(),
        P(),
        P(None, "mlp"),
        P("mlp", None),
    )
    out_specs = (P("mlp", "lon", None), P(None, "mlp"), P("mlp", None))
    return jax.shard_map(body, mesh=mesh, in_specs=in_specs, out_specs=out_specs, check_vma=False)
```

```python
import functools
import math

import jax
import jax.numpy as jnp
from jax import lax
from jax.experimental import pallas as pl
from jax.experimental.pallas import tpu as pltpu
from jax.sharding import PartitionSpec as P

KS = 7
LON = 1440
REACH = KS // 2
LANES = 128
BF16 = jnp.bfloat16
F32 = jnp.float32
LEAD = 8


def passed_along(value, axis, by):
    count = lax.axis_size(axis)
    return lax.ppermute(value, axis, [(i, (i + by) % count) for i in range(count)])


def live_count():
    members = lax.axis_size("lon")
    position = lax.axis_index("lon")
    return LON // members + (position < LON % members).astype(jnp.int32)


def halo(own, slots, held):
    lat, count = own.shape[0], lax.axis_size("mlp")
    if count == 2:
        mine = jnp.where(lax.axis_index("mlp") == 0, own[lat - REACH :], own[:REACH])
        other = lax.ppermute(mine, "mlp", [(0, 1), (1, 0)])
    else:
        ends = count - 1
        other = jnp.concatenate(
            [
                lax.ppermute(own[lat - REACH :], "mlp", [(i, i + 1) for i in range(ends)]),
                lax.ppermute(own[:REACH], "mlp", [(i + 1, i) for i in range(ends)]),
            ],
            axis=0,
        )
    even = LON % lax.axis_size("lon") == 0
    both = (own, other)
    first = jnp.concatenate([v[:, :REACH] for v in both], axis=0)
    if even:
        last = jnp.concatenate([v[:, slots - REACH : slots] for v in both], axis=0)
    else:
        last = jnp.concatenate(
            [lax.dynamic_slice_in_dim(v, held - REACH, REACH, 1) for v in both], axis=0
        )
    left = passed_along(last, "lon", 1)
    right = passed_along(first, "lon", -1)
    if not even:
        rows = jnp.concatenate([v[:, :slots] for v in both], axis=0)
        joined = jnp.concatenate([rows, jnp.zeros_like(right)], axis=1)
        joined = lax.dynamic_update_slice_in_dim(joined, right, held, 1)
        own, other, right = joined[:lat, :slots], joined[lat:, :slots], joined[:, slots:]
    return own, other, jnp.concatenate([left, right], axis=1)


def places(lat, held):
    near = jnp.int32(0)
    if lax.axis_size("mlp") == 2:
        near = jnp.where(lax.axis_index("mlp") == 0, lat + REACH, 0).astype(jnp.int32)
        return jnp.stack([near, held.astype(jnp.int32)])
    return jnp.stack([near, held.astype(jnp.int32), jnp.int32(lat + REACH)])


def conv_tile(lat, slots, rows, flip, where_ref, own, other, sides, taps, wide, lane, sink):
    groups = other.shape[0] // REACH
    wide[REACH : REACH + lat, LEAD : LEAD + slots, :] = own[:, :slots, lane].astype(F32)
    ends = sides[:, :, lane].astype(F32)
    wide[REACH : REACH + lat, LEAD - REACH : LEAD, :] = ends[:lat, :REACH]
    wide[REACH : REACH + lat, LEAD + slots : LEAD + slots + REACH, :] = ends[:lat, REACH:]
    for g in range(groups):
        for k in range(REACH):
            at, src = where_ref[2 * g] + k, g * REACH + k
            wide[at, LEAD : LEAD + slots, :] = other[src, :slots, lane].astype(F32)
            wide[at, LEAD - REACH : LEAD, :] = ends[lat + src, :REACH]
            wide[at, LEAD + slots : LEAD + slots + REACH, :] = ends[lat + src, REACH:]

    def step(jt, carry):
        start = jt * 16
        acc = [[jnp.zeros((8, LANES), F32) for _ in range(lat)] for _ in range(2)]
        for b in range(KS):
            used = [a * KS + b for a in range(KS)]
            if flip:
                used = [KS * KS - 1 - t for t in used]
            taken = [taps[t] for t in used]
            for r in rows:
                for half in range(2):
                    cells = wide[r, pl.ds(start + 8 * half + LEAD - REACH + b, 8), :]
                    for i in range(max(0, r - KS + 1), min(lat, r + 1)):
                        acc[half][i] = acc[half][i] + taken[r - i] * cells
        for half in range(2):
            for i in range(lat):
                sink(i, pl.ds(pl.multiple_of(start + 8 * half, 8), 8), acc[half][i])
        return carry

    lax.fori_loop(0, -(-slots // 16), step, 0)


def conv(lat, slots, flip, where_ref, own, other, sides, weight, taps, wide, finish, sink):
    width = own.shape[-1]

    def over(rows):
        def channels(ct, carry):
            lane = pl.ds(pl.multiple_of(ct * LANES, LANES), LANES)
            for a in range(KS):
                row = weight[a, :, lane].astype(F32)
                for b in range(KS):
                    taps[a * KS + b] = jnp.broadcast_to(row[b : b + 1], (8, LANES))
            conv_tile(
                lat, slots, rows, flip, where_ref, own, other, sides, taps, wide, lane,
                functools.partial(sink, lane),
            )
            finish(lane)
            return carry

        lax.fori_loop(0, width // LANES, channels, 0)

    if other.shape[0] == REACH:
        first = where_ref[0] != 0
        pl.when(first)(lambda: over(range(REACH, lat + 2 * REACH)))
        pl.when(jnp.logical_not(first))(lambda: over(range(lat + REACH)))
    else:
        over(range(lat + 2 * REACH))


def forward_kernel(
    lat, slots, where_ref, own, other, sides, weight, gain, normed, hat, inv, taps, wide, mixed
):
    def sink(lane, i, at, value):
        mixed[i, at, lane] = value

    conv(
        lat, slots, False, where_ref, own, other, sides, weight, taps, wide,
        lambda lane: None, sink,
    )
    tile = 32 if mixed.shape[1] % 32 == 0 else 16
    tiles = mixed.shape[1] // tile

    def norm(step, carry):
        i, start = step // tiles, pl.multiple_of(step % tiles * tile, tile)
        at = pl.ds(start, tile)
        values = mixed[i, at, :]
        centred = values - jnp.mean(values, axis=-1, keepdims=True)
        scale = lax.rsqrt(jnp.mean(centred * centred, axis=-1, keepdims=True) + 1e-06)
        live = start + lax.broadcasted_iota(jnp.int32, (tile, 1), 0) < where_ref[1]
        unit = jnp.where(live, centred * scale, 0.0)
        hat[i, at, :] = unit
        normed[i, at, :] = (unit * gain[...]).astype(BF16)
        inv[i, at, :] = jnp.broadcast_to(jnp.where(live, scale, 0.0), (tile, LANES))
        return carry

    lax.fori_loop(0, lat * tiles, norm, 0)


def backward_kernel(
    lat, slots, where_ref, own, other, sides, weight, cot, out, taps, wide, mixed
):
    def sink(lane, i, at, value):
        mixed[i, at, :] = value

    def finish(lane):
        live = lax.broadcasted_iota(jnp.int32, (slots, 1), 0) < where_ref[1]
        for i in range(lat):
            total = cot[i, :, lane].astype(F32) + mixed[i, :slots, :]
            out[i, :, lane] = jnp.where(live, total, 0.0).astype(BF16)

    conv(lat, slots, True, where_ref, own, other, sides, weight, taps, wide, finish, sink)


def kernel_call(kernel, lat, slots, slots_pad, width, outs, mixed, operands):
    vmem = pl.BlockSpec(memory_space=pltpu.VMEM)
    flops = 2 * lat * slots_pad * width * KS * KS
    return pl.pallas_call(
        functools.partial(kernel, lat, slots),
        out_shape=outs,
        in_specs=[pl.BlockSpec(memory_space=pltpu.SMEM)] + [vmem] * (len(operands) - 1),
        out_specs=jax.tree.map(lambda _: vmem, outs),
        scratch_shapes=[
            pltpu.VMEM((KS * KS, 8, LANES), F32),
            pltpu.VMEM((lat + 2 * REACH, slots_pad + 16, LANES), F32),
            pltpu.VMEM(mixed, F32),
        ],
        compiler_params=pltpu.CompilerParams(vmem_limit_bytes=12 * 2**20),
        cost_estimate=pl.CostEstimate(flops=flops, bytes_accessed=8 * 2**20, transcendentals=0),
    )(*operands)


def gate(values):
    cumulative = 0.5 * (1.0 + lax.erf(values * (1.0 / math.sqrt(2.0))))
    density = jnp.exp(-0.5 * values * values) * (1.0 / math.sqrt(2.0 * math.pi))
    return cumulative, density


def upper(bit):
    return (lax.axis_index("lon") & bit) // bit


def swapped(value, bit):
    count = lax.axis_size("lon")
    return lax.ppermute(value, "lon", [(i, i ^ bit) for i in range(count)])


def cut(part, which):
    half = part.shape[0] // 2
    return lax.dynamic_slice_in_dim(part, which * half, half, 0)


def merged(low_first, own, got):
    high = low_first == 1
    return jnp.concatenate([jnp.where(high, got, own), jnp.where(high, own, got)], axis=0)


def lon_bits():
    bits, bit = [], 1
    while bit < lax.axis_size("lon"):
        bits.append(bit)
        bit *= 2
    return bits


class State:
    def __init__(self):
        self.held = {}

    def sync(self, *more):
        names = list(self.held)
        tied = lax.optimization_barrier(tuple(self.held.values()) + more)
        self.held = dict(zip(names, tied))
        return tied[len(names) :]


class Pair:
    def __init__(self, state, name, parts, ways):
        self.state, self.names, self.sent = state, (name + "0", name + "1"), None
        self.keep(parts)
        self.stages = []
        for near, far in ways:
            middle = len(far) // 2
            groups = [[b] for b in near] + [far[:middle], far[middle:]]
            down = [(g, True) for g in groups]
            self.stages.append(down + [(g[::-1], False) for g in groups[::-1]])

    def keep(self, parts):
        self.state.held.update(zip(self.names, parts))

    def parts(self):
        return [self.state.held[name] for name in self.names]

    def outgoing(self, bits, summing):
        if summing:
            return [cut(p, 1 - upper(b)) for p, b in zip(self.parts(), bits)]
        return self.parts()

    def launch(self, bits, summing, sent):
        self.sent = (bits, summing, [swapped(v, b) for v, b in zip(sent, bits)])

    def start(self, bits, summing):
        self.launch(bits, summing, self.state.sync(*self.outgoing(bits, summing)))

    def close(self):
        bits, summing, got = self.sent
        each = zip(self.parts(), got, bits)
        if summing:
            self.keep(
                [(cut(p, upper(b)).astype(F32) + g.astype(F32)).astype(BF16) for p, g, b in each]
            )
        else:
            self.keep([merged(upper(b), p, g) for p, g, b in each])

    def next_stage(self):
        groups = [stages.pop(0) for stages in self.stages]
        return list(zip(*(bits for bits, _ in groups))), groups[0][1]

    def open(self):
        steps, summing = self.next_stage()
        for bits in steps[:-1]:
            self.start(bits, summing)
            self.close()
        self.start(steps[-1], summing)

    def open_first(self):
        (bits,), summing = self.next_stage()
        sent = self.outgoing(bits, summing)
        half = sent[0].shape[0] // 2
        tied = self.state.sync(*[v[:half] for v in sent], *[v[half:] for v in sent])
        self.launch(bits, summing, tied[: len(sent)])
        self.state.held.update(zip(self.rest(), tied[len(sent) :]))

    def rest(self):
        return [name + "r" for name in self.names]

    def arrived(self):
        self.state.held.update(zip([name + "g" for name in self.names], self.sent[2]))

    def open_second(self):
        sent = [self.state.held.pop(name) for name in self.rest()]
        sent = self.state.sync(*sent)
        got = [self.state.held.pop(name + "g") for name in self.names]
        self.launch(self.sent[0], self.sent[1], sent)
        both = [jnp.concatenate(pair, axis=0) for pair in zip(got, self.sent[2])]
        self.sent = (*self.sent[:2], both)

    def advance(self):
        self.close()
        self.open()


def both_ways():
    bits = lon_bits()
    fast, slow = bits[:2], bits[2:]
    return (fast, slow), (fast[::-1], slow[::-1])


def all_rows(own):
    if lax.axis_size("mlp") == 2:
        return jnp.concatenate([own, lax.ppermute(own, "mlp", [(0, 1), (1, 0)])], axis=0)
    return lax.all_gather(own, "mlp", axis=0, tiled=True)


def own_rows_sum(partial):
    if lax.axis_size("mlp") == 2:
        rows = partial.shape[0] // 2
        theirs = lax.ppermute(partial[rows:], "mlp", [(0, 1), (1, 0)])
        return partial[:rows].astype(F32) + theirs.astype(F32)
    return lax.psum_scatter(partial, "mlp", scatter_dimension=0, tiled=True).astype(F32)


def across_rows(left, right):
    return lax.dot_general(left, right, (((0,), (0,)), ((), ())), preferred_element_type=F32)


def across_width(left, right):
    return lax.dot_general(left, right, (((1,), (1,)), ((), ())), preferred_element_type=F32)


def body(fields, cotangent, conv_weight, norm_gain, weight_in, weight_out):
    lat, slots, width = fields.shape
    slots_pad = -(-slots // 16) * 16
    held = live_count()
    slot_live = lax.broadcasted_iota(jnp.int32, (1, slots, 1), 1) < held
    spare = ((0, 0), (0, slots_pad - slots), (0, 0))
    where = places(lat, held)
    gain = norm_gain.astype(F32).reshape(1, width)
    cot_all = all_rows(jnp.pad(jnp.where(slot_live, cotangent, 0), spare).reshape(-1, width))

    grid = (lat, slots_pad, width)
    normed, hat, inv = kernel_call(
        forward_kernel, lat, slots, slots_pad, width,
        (
            jax.ShapeDtypeStruct(grid, BF16),
            jax.ShapeDtypeStruct(grid, F32),
            jax.ShapeDtypeStruct((lat, slots_pad, LANES), F32),
        ),
        grid,
        (where,) + halo(fields, slots, held) + (conv_weight, gain),
    )
    normed_all = all_rows(normed.reshape(-1, width))

    cells = lax.axis_size("mlp") * lat * LON
    factor = jnp.float32(1.0 / math.sqrt(cells))
    state = State()
    ways = both_ways()

    def pair(name, grad):
        half = grad.shape[0] // 2
        return Pair(state, name, (grad[:half], grad[half:]), ways)

    hidden = jnp.dot(normed_all, weight_in, preferred_element_type=F32)
    cumulative, density = gate(hidden)
    activated = (hidden * cumulative).astype(BF16)
    state.held["cot"] = cot_all
    a = pair("a", (across_rows(activated, cot_all) * factor).astype(BF16))
    a.open()
    upstream = across_width(state.held.pop("cot"), weight_out)
    grad_hidden = (upstream * (cumulative + hidden * density)).astype(BF16)
    grad_first = (across_rows(normed_all, grad_hidden) * factor).astype(BF16)
    partial = across_width(grad_hidden, weight_in).astype(BF16)
    grad_normed = own_rows_sum(partial)
    b = pair("b", grad_first)
    state.held["partial"] = partial
    a.advance()
    a.advance()
    b.open_first()

    b.arrived()
    a.advance()
    b.open_second()
    a.advance()
    a.advance()
    b.advance()
    state.held["hat"] = hat
    state.sync()
    hat = state.held.pop("hat")
    del state.held["partial"]
    scaled = grad_normed.reshape(grid) * gain
    inv = inv[:, :, :1]
    grad_mixed = inv * (
        scaled
        - jnp.mean(scaled, axis=-1, keepdims=True)
        - hat * jnp.mean(scaled * hat, axis=-1, keepdims=True)
    )
    state.held["mixed"] = grad_mixed.astype(BF16)
    a.advance()
    b.advance()
    own, other, sides = halo(state.held.pop("mixed"), slots, held)

    a.close()
    a.open_first()
    b.advance()
    b.advance()
    a.arrived()
    b.advance()
    a.open_second()
    a.close()
    b.advance()
    b.advance()
    state.held["sides"] = sides
    state.sync()
    result = kernel_call(
        backward_kernel, lat, slots, slots_pad, width,
        jax.ShapeDtypeStruct((lat, slots, width), BF16),
        (lat, slots_pad, LANES),
        (where, own, other, state.held["sides"], conv_weight, cotangent),
    )
    b.close()
    out_second = jnp.concatenate(a.parts(), axis=0)
    out_first = jnp.concatenate(b.parts(), axis=0)
    return (result, out_first, out_second)


def solution(mesh):
    in_specs = (
        P("mlp", "lon", None),
        P("mlp", "lon", None),
        P(),
        P(),
        P(None, "mlp"),
        P("mlp", None),
    )
    out_specs = (P("mlp", "lon", None), P(None, "mlp"), P("mlp", None))
    return jax.shard_map(body, mesh=mesh, in_specs=in_specs, out_specs=out_specs, check_vma=False)
```

```python
import functools
import math

import jax
import jax.numpy as jnp
from jax import lax
from jax.experimental import pallas as pl
from jax.experimental.pallas import tpu as pltpu
from jax.sharding import PartitionSpec as P

KS = 7
LON = 1440
REACH = KS // 2
LANES = 128
BF16 = jnp.bfloat16
F32 = jnp.float32
LEAD = 8


def passed_along(value, axis, by):
    count = lax.axis_size(axis)
    return lax.ppermute(value, axis, [(i, (i + by) % count) for i in range(count)])


def live_count():
    members = lax.axis_size("lon")
    position = lax.axis_index("lon")
    return LON // members + (position < LON % members).astype(jnp.int32)


def halo(own, slots, held):
    lat, count = own.shape[0], lax.axis_size("mlp")
    if count == 2:
        mine = jnp.where(lax.axis_index("mlp") == 0, own[lat - REACH :], own[:REACH])
        other = lax.ppermute(mine, "mlp", [(0, 1), (1, 0)])
    else:
        ends = count - 1
        other = jnp.concatenate(
            [
                lax.ppermute(own[lat - REACH :], "mlp", [(i, i + 1) for i in range(ends)]),
                lax.ppermute(own[:REACH], "mlp", [(i + 1, i) for i in range(ends)]),
            ],
            axis=0,
        )
    even = LON % lax.axis_size("lon") == 0
    both = (own, other)
    first = jnp.concatenate([v[:, :REACH] for v in both], axis=0)
    if even:
        last = jnp.concatenate([v[:, slots - REACH : slots] for v in both], axis=0)
    else:
        last = jnp.concatenate(
            [lax.dynamic_slice_in_dim(v, held - REACH, REACH, 1) for v in both], axis=0
        )
    left = passed_along(last, "lon", 1)
    right = passed_along(first, "lon", -1)
    if not even:
        rows = jnp.concatenate([v[:, :slots] for v in both], axis=0)
        joined = jnp.concatenate([rows, jnp.zeros_like(right)], axis=1)
        joined = lax.dynamic_update_slice_in_dim(joined, right, held, 1)
        own, other, right = joined[:lat, :slots], joined[lat:, :slots], joined[:, slots:]
    return own, other, jnp.concatenate([left, right], axis=1)


def places(lat, held):
    near = jnp.int32(0)
    if lax.axis_size("mlp") == 2:
        near = jnp.where(lax.axis_index("mlp") == 0, lat + REACH, 0).astype(jnp.int32)
        return jnp.stack([near, held.astype(jnp.int32)])
    return jnp.stack([near, held.astype(jnp.int32), jnp.int32(lat + REACH)])


def conv_tile(lat, slots, rows, flip, where_ref, own, other, sides, taps, wide, lane, sink):
    groups = other.shape[0] // REACH
    wide[REACH : REACH + lat, LEAD : LEAD + slots, :] = own[:, :slots, lane].astype(F32)
    ends = sides[:, :, lane].astype(F32)
    wide[REACH : REACH + lat, LEAD - REACH : LEAD, :] = ends[:lat, :REACH]
    wide[REACH : REACH + lat, LEAD + slots : LEAD + slots + REACH, :] = ends[:lat, REACH:]
    for g in range(groups):
        for k in range(REACH):
            at, src = where_ref[2 * g] + k, g * REACH + k
            wide[at, LEAD : LEAD + slots, :] = other[src, :slots, lane].astype(F32)
            wide[at, LEAD - REACH : LEAD, :] = ends[lat + src, :REACH]
            wide[at, LEAD + slots : LEAD + slots + REACH, :] = ends[lat + src, REACH:]

    def step(jt, carry):
        start = jt * 16
        acc = [[jnp.zeros((8, LANES), F32) for _ in range(lat)] for _ in range(2)]
        for b in range(KS):
            used = [a * KS + b for a in range(KS)]
            if flip:
                used = [KS * KS - 1 - t for t in used]
            taken = [taps[t] for t in used]
            for r in rows:
                for half in range(2):
                    cells = wide[r, pl.ds(start + 8 * half + LEAD - REACH + b, 8), :]
                    for i in range(max(0, r - KS + 1), min(lat, r + 1)):
                        acc[half][i] = acc[half][i] + taken[r - i] * cells
        for half in range(2):
            for i in range(lat):
                sink(i, pl.ds(pl.multiple_of(start + 8 * half, 8), 8), acc[half][i])
        return carry

    lax.fori_loop(0, -(-slots // 16), step, 0)


def conv(lat, slots, flip, where_ref, own, other, sides, weight, taps, wide, finish, sink):
    width = own.shape[-1]

    def over(rows):
        def channels(ct, carry):
            lane = pl.ds(pl.multiple_of(ct * LANES, LANES), LANES)
            for a in range(KS):
                row = weight[a, :, lane].astype(F32)
                for b in range(KS):
                    taps[a * KS + b] = jnp.broadcast_to(row[b : b + 1], (8, LANES))
            conv_tile(
                lat, slots, rows, flip, where_ref, own, other, sides, taps, wide, lane,
                functools.partial(sink, lane),
            )
            finish(lane)
            return carry

        lax.fori_loop(0, width // LANES, channels, 0)

    if other.shape[0] == REACH:
        first = where_ref[0] != 0
        pl.when(first)(lambda: over(range(REACH, lat + 2 * REACH)))
        pl.when(jnp.logical_not(first))(lambda: over(range(lat + REACH)))
    else:
        over(range(lat + 2 * REACH))


def forward_kernel(
    lat, slots, where_ref, own, other, sides, weight, gain, normed, hat, inv, taps, wide, mixed
):
    def sink(lane, i, at, value):
        mixed[i, at, lane] = value

    conv(
        lat, slots, False, where_ref, own, other, sides, weight, taps, wide,
        lambda lane: None, sink,
    )
    tile = 32 if mixed.shape[1] % 32 == 0 else 16
    tiles = mixed.shape[1] // tile

    def norm(step, carry):
        i, start = step // tiles, pl.multiple_of(step % tiles * tile, tile)
        at = pl.ds(start, tile)
        values = mixed[i, at, :]
        centred = values - jnp.mean(values, axis=-1, keepdims=True)
        scale = lax.rsqrt(jnp.mean(centred * centred, axis=-1, keepdims=True) + 1e-06)
        live = start + lax.broadcasted_iota(jnp.int32, (tile, 1), 0) < where_ref[1]
        unit = jnp.where(live, centred * scale, 0.0)
        hat[i, at, :] = unit
        normed[i, at, :] = (unit * gain[...]).astype(BF16)
        inv[i, at, :] = jnp.broadcast_to(jnp.where(live, scale, 0.0), (tile, LANES))
        return carry

    lax.fori_loop(0, lat * tiles, norm, 0)


def backward_kernel(
    lat, slots, where_ref, own, other, sides, weight, cot, out, taps, wide, mixed
):
    def sink(lane, i, at, value):
        mixed[i, at, :] = value

    def finish(lane):
        live = lax.broadcasted_iota(jnp.int32, (slots, 1), 0) < where_ref[1]
        for i in range(lat):
            total = cot[i, :, lane].astype(F32) + mixed[i, :slots, :]
            out[i, :, lane] = jnp.where(live, total, 0.0).astype(BF16)

    conv(lat, slots, True, where_ref, own, other, sides, weight, taps, wide, finish, sink)


def kernel_call(kernel, lat, slots, slots_pad, width, outs, mixed, operands):
    vmem = pl.BlockSpec(memory_space=pltpu.VMEM)
    return pl.pallas_call(
        functools.partial(kernel, lat, slots),
        out_shape=outs,
        in_specs=[pl.BlockSpec(memory_space=pltpu.SMEM)] + [vmem] * (len(operands) - 1),
        out_specs=jax.tree.map(lambda _: vmem, outs),
        scratch_shapes=[
            pltpu.VMEM((KS * KS, 8, LANES), F32),
            pltpu.VMEM((lat + 2 * REACH, slots_pad + 16, LANES), F32),
            pltpu.VMEM(mixed, F32),
        ],
        compiler_params=pltpu.CompilerParams(vmem_limit_bytes=12 * 2**20),
        cost_estimate=pl.CostEstimate(flops=2**20, bytes_accessed=2**20, transcendentals=0),
    )(*operands)


def gate(values):
    cumulative = 0.5 * (1.0 + lax.erf(values * (1.0 / math.sqrt(2.0))))
    density = jnp.exp(-0.5 * values * values) * (1.0 / math.sqrt(2.0 * math.pi))
    return cumulative, density


def upper(bit):
    return (lax.axis_index("lon") & bit) // bit


def swapped(value, bit):
    count = lax.axis_size("lon")
    return lax.ppermute(value, "lon", [(i, i ^ bit) for i in range(count)])


def cut(part, which):
    half = part.shape[0] // 2
    return lax.dynamic_slice_in_dim(part, which * half, half, 0)


def merged(low_first, own, got):
    high = low_first == 1
    return jnp.concatenate([jnp.where(high, got, own), jnp.where(high, own, got)], axis=0)


def lon_bits():
    bits, bit = [], 1
    while bit < lax.axis_size("lon"):
        bits.append(bit)
        bit *= 2
    return bits


class State:
    def __init__(self):
        self.held = {}

    def sync(self, *more):
        names = list(self.held)
        tied = lax.optimization_barrier(tuple(self.held.values()) + more)
        self.held = dict(zip(names, tied))
        return tied[len(names) :]


class Pair:
    def __init__(self, state, name, parts, ways):
        self.state, self.names, self.sent = state, (name + "0", name + "1"), None
        self.keep(parts)
        self.stages = []
        for near, far in ways:
            middle = len(far) // 2
            groups = [[b] for b in near] + [far[:middle], far[middle:]]
            down = [(g, True) for g in groups]
            self.stages.append(down + [(g[::-1], False) for g in groups[::-1]])

    def keep(self, parts):
        self.state.held.update(zip(self.names, parts))

    def parts(self):
        return [self.state.held[name] for name in self.names]

    def outgoing(self, bits, summing):
        if summing:
            return [cut(p, 1 - upper(b)) for p, b in zip(self.parts(), bits)]
        return self.parts()

    def launch(self, bits, summing, sent):
        self.sent = (bits, summing, [swapped(v, b) for v, b in zip(sent, bits)])

    def start(self, bits, summing):
        self.launch(bits, summing, self.state.sync(*self.outgoing(bits, summing)))

    def close(self):
        bits, summing, got = self.sent
        each = zip(self.parts(), got, bits)
        if summing:
            self.keep(
                [(cut(p, upper(b)).astype(F32) + g.astype(F32)).astype(BF16) for p, g, b in each]
            )
        else:
            self.keep([merged(upper(b), p, g) for p, g, b in each])

    def next_stage(self):
        groups = [stages.pop(0) for stages in self.stages]
        return list(zip(*(bits for bits, _ in groups))), groups[0][1]

    def open(self):
        steps, summing = self.next_stage()
        for bits in steps[:-1]:
            self.start(bits, summing)
            self.close()
        self.start(steps[-1], summing)

    def open_pieces(self, shares):
        (bits,), summing = self.next_stage()
        sent = self.outgoing(bits, summing)
        rows, at, pieces = sent[0].shape[0], 0, []
        for share in shares:
            pieces.append([v[at : at + rows // share] for v in sent])
            at += rows // share
        flat = self.state.sync(*[v for piece in pieces for v in piece])
        count = len(sent)
        for k in range(1, len(shares)):
            self.state.held.update(zip(self.tags("r", k), flat[k * count : (k + 1) * count]))
        self.launch(bits, summing, flat[:count])
        self.piece, self.pieces = 0, len(shares)

    def tags(self, kind, k):
        return [name + kind + str(k) for name in self.names]

    def arrived(self):
        self.state.held.update(zip(self.tags("g", self.piece), self.sent[2]))

    def next_piece(self):
        self.piece += 1
        sent = [self.state.held.pop(tag) for tag in self.tags("r", self.piece)]
        self.launch(self.sent[0], self.sent[1], self.state.sync(*sent))

    def gather_pieces(self):
        self.arrived()
        got = [
            [self.state.held.pop(tag) for tag in self.tags("g", k)] for k in range(self.pieces)
        ]
        both = [jnp.concatenate(parts, axis=0) for parts in zip(*got)]
        self.sent = (*self.sent[:2], both)

    def advance(self):
        self.close()
        self.open()


def both_ways():
    bits = lon_bits()
    fast, slow = bits[:2], bits[2:]
    return (fast, slow), (fast[::-1], slow[::-1])


def all_rows(own):
    if lax.axis_size("mlp") == 2:
        return jnp.concatenate([own, lax.ppermute(own, "mlp", [(0, 1), (1, 0)])], axis=0)
    return lax.all_gather(own, "mlp", axis=0, tiled=True)


def own_rows_sum(partial):
    if lax.axis_size("mlp") == 2:
        rows = partial.shape[0] // 2
        theirs = lax.ppermute(partial[rows:], "mlp", [(0, 1), (1, 0)])
        return partial[:rows].astype(F32) + theirs.astype(F32)
    return lax.psum_scatter(partial, "mlp", scatter_dimension=0, tiled=True).astype(F32)


def across_rows(left, right):
    return lax.dot_general(left, right, (((0,), (0,)), ((), ())), preferred_element_type=F32)


def across_width(left, right):
    return lax.dot_general(left, right, (((1,), (1,)), ((), ())), preferred_element_type=F32)


def body(fields, cotangent, conv_weight, norm_gain, weight_in, weight_out):
    lat, slots, width = fields.shape
    slots_pad = -(-slots // 16) * 16
    held = live_count()
    slot_live = lax.broadcasted_iota(jnp.int32, (1, slots, 1), 1) < held
    spare = ((0, 0), (0, slots_pad - slots), (0, 0))
    where = places(lat, held)
    gain = norm_gain.astype(F32).reshape(1, width)
    cot_all = all_rows(jnp.pad(jnp.where(slot_live, cotangent, 0), spare).reshape(-1, width))

    grid = (lat, slots_pad, width)
    normed, hat, inv = kernel_call(
        forward_kernel, lat, slots, slots_pad, width,
        (
            jax.ShapeDtypeStruct(grid, BF16),
            jax.ShapeDtypeStruct(grid, F32),
            jax.ShapeDtypeStruct((lat, slots_pad, LANES), F32),
        ),
        grid,
        (where,) + halo(fields, slots, held) + (conv_weight, gain),
    )
    normed_all = all_rows(normed.reshape(-1, width))

    cells = lax.axis_size("mlp") * lat * LON
    factor = jnp.float32(1.0 / math.sqrt(cells))
    state = State()
    ways = both_ways()

    def pair(name, grad):
        half = grad.shape[0] // 2
        return Pair(state, name, (grad[:half], grad[half:]), ways)

    hidden = jnp.dot(normed_all, weight_in, preferred_element_type=F32)
    cumulative, density = gate(hidden)
    activated = (hidden * cumulative).astype(BF16)
    state.held["cot"] = cot_all
    a = pair("a", (across_rows(activated, cot_all) * factor).astype(BF16))
    a.open()
    upstream = across_width(state.held.pop("cot"), weight_out)
    grad_hidden = (upstream * (cumulative + hidden * density)).astype(BF16)
    partial = across_width(grad_hidden, weight_in).astype(BF16)
    grad_normed = own_rows_sum(partial)
    state.held["hidden"] = grad_hidden
    state.held["partial"] = partial
    a.advance()
    grad_first = across_rows(normed_all, state.held.pop("hidden")) * factor
    b = pair("b", grad_first.astype(BF16))
    a.advance()
    b.open_pieces((2, 4, 4))

    b.arrived()
    a.advance()
    b.next_piece()
    b.arrived()
    a.advance()
    b.next_piece()
    b.arrived()
    a.advance()
    b.gather_pieces()
    b.advance()
    state.held["gain"] = gain
    state.sync()
    gain = state.held.pop("gain")
    del state.held["partial"]
    scaled = grad_normed.reshape(grid) * gain
    inv = inv[:, :, :1]
    grad_mixed = inv * (
        scaled
        - jnp.mean(scaled, axis=-1, keepdims=True)
        - hat * jnp.mean(scaled * hat, axis=-1, keepdims=True)
    )
    state.held["mixed"] = grad_mixed.astype(BF16)
    a.advance()
    b.advance()
    own, other, sides = halo(state.held.pop("mixed"), slots, held)

    b.advance()
    a.close()
    a.open_pieces((4, 4, 2))
    a.arrived()
    b.advance()
    a.next_piece()
    a.arrived()
    b.advance()
    a.next_piece()
    a.arrived()
    b.advance()
    a.gather_pieces()
    a.close()
    b.advance()
    state.held["sides"] = sides
    state.sync()
    result = kernel_call(
        backward_kernel, lat, slots, slots_pad, width,
        jax.ShapeDtypeStruct((lat, slots, width), BF16),
        (lat, slots_pad, LANES),
        (where, own, other, state.held["sides"], conv_weight, cotangent),
    )
    b.close()
    out_second = jnp.concatenate(a.parts(), axis=0)
    out_first = jnp.concatenate(b.parts(), axis=0)
    return (result, out_first, out_second)


def solution(mesh):
    in_specs = (
        P("mlp", "lon", None),
        P("mlp", "lon", None),
        P(),
        P(),
        P(None, "mlp"),
        P("mlp", None),
    )
    out_specs = (P("mlp", "lon", None), P(None, "mlp"), P("mlp", None))
    return jax.shard_map(body, mesh=mesh, in_specs=in_specs, out_specs=out_specs, check_vma=False)
```

```python
import functools
import math

import jax
import jax.numpy as jnp
from jax import lax
from jax.experimental import pallas as pl
from jax.experimental.pallas import tpu as pltpu
from jax.sharding import PartitionSpec as P

KS = 7
LON = 1440
REACH = KS // 2
LANES = 128
BF16 = jnp.bfloat16
F32 = jnp.float32
LEAD = 8


def passed_along(value, axis, by):
    count = lax.axis_size(axis)
    return lax.ppermute(value, axis, [(i, (i + by) % count) for i in range(count)])


def live_count():
    members = lax.axis_size("lon")
    position = lax.axis_index("lon")
    return LON // members + (position < LON % members).astype(jnp.int32)


def halo(own, slots, held):
    lat, count = own.shape[0], lax.axis_size("mlp")
    if count == 2:
        mine = jnp.where(lax.axis_index("mlp") == 0, own[lat - REACH :], own[:REACH])
        other = lax.ppermute(mine, "mlp", [(0, 1), (1, 0)])
    else:
        ends = count - 1
        other = jnp.concatenate(
            [
                lax.ppermute(own[lat - REACH :], "mlp", [(i, i + 1) for i in range(ends)]),
                lax.ppermute(own[:REACH], "mlp", [(i + 1, i) for i in range(ends)]),
            ],
            axis=0,
        )
    even = LON % lax.axis_size("lon") == 0
    both = (own, other)
    first = jnp.concatenate([v[:, :REACH] for v in both], axis=0)
    if even:
        last = jnp.concatenate([v[:, slots - REACH : slots] for v in both], axis=0)
    else:
        last = jnp.concatenate(
            [lax.dynamic_slice_in_dim(v, held - REACH, REACH, 1) for v in both], axis=0
        )
    left = passed_along(last, "lon", 1)
    right = passed_along(first, "lon", -1)
    if not even:
        rows = jnp.concatenate([v[:, :slots] for v in both], axis=0)
        joined = jnp.concatenate([rows, jnp.zeros_like(right)], axis=1)
        joined = lax.dynamic_update_slice_in_dim(joined, right, held, 1)
        own, other, right = joined[:lat, :slots], joined[lat:, :slots], joined[:, slots:]
    return own, other, jnp.concatenate([left, right], axis=1)


def places(lat, held):
    near = jnp.int32(0)
    if lax.axis_size("mlp") == 2:
        near = jnp.where(lax.axis_index("mlp") == 0, lat + REACH, 0).astype(jnp.int32)
        return jnp.stack([near, held.astype(jnp.int32)])
    return jnp.stack([near, held.astype(jnp.int32), jnp.int32(lat + REACH)])


def conv_tile(lat, slots, rows, flip, where_ref, own, other, sides, taps, wide, lane, sink):
    groups = other.shape[0] // REACH
    wide[REACH : REACH + lat, LEAD : LEAD + slots, :] = own[:, :slots, lane].astype(F32)
    ends = sides[:, :, lane].astype(F32)
    wide[REACH : REACH + lat, LEAD - REACH : LEAD, :] = ends[:lat, :REACH]
    wide[REACH : REACH + lat, LEAD + slots : LEAD + slots + REACH, :] = ends[:lat, REACH:]
    for g in range(groups):
        for k in range(REACH):
            at, src = where_ref[2 * g] + k, g * REACH + k
            wide[at, LEAD : LEAD + slots, :] = other[src, :slots, lane].astype(F32)
            wide[at, LEAD - REACH : LEAD, :] = ends[lat + src, :REACH]
            wide[at, LEAD + slots : LEAD + slots + REACH, :] = ends[lat + src, REACH:]

    def step(jt, carry):
        start = jt * 16
        acc = [[jnp.zeros((8, LANES), F32) for _ in range(lat)] for _ in range(2)]
        for b in range(KS):
            used = [a * KS + b for a in range(KS)]
            if flip:
                used = [KS * KS - 1 - t for t in used]
            taken = [taps[t] for t in used]
            for r in rows:
                for half in range(2):
                    cells = wide[r, pl.ds(start + 8 * half + LEAD - REACH + b, 8), :]
                    for i in range(max(0, r - KS + 1), min(lat, r + 1)):
                        acc[half][i] = acc[half][i] + taken[r - i] * cells
        for half in range(2):
            for i in range(lat):
                sink(i, pl.ds(pl.multiple_of(start + 8 * half, 8), 8), acc[half][i])
        return carry

    lax.fori_loop(0, -(-slots // 16), step, 0)


def conv(lat, slots, flip, where_ref, own, other, sides, weight, taps, wide, finish, sink):
    width = own.shape[-1]

    def over(rows):
        def channels(ct, carry):
            lane = pl.ds(pl.multiple_of(ct * LANES, LANES), LANES)
            for a in range(KS):
                row = weight[a, :, lane].astype(F32)
                for b in range(KS):
                    taps[a * KS + b] = jnp.broadcast_to(row[b : b + 1], (8, LANES))
            conv_tile(
                lat, slots, rows, flip, where_ref, own, other, sides, taps, wide, lane,
                functools.partial(sink, lane),
            )
            finish(lane)
            return carry

        lax.fori_loop(0, width // LANES, channels, 0)

    if other.shape[0] == REACH:
        first = where_ref[0] != 0
        pl.when(first)(lambda: over(range(REACH, lat + 2 * REACH)))
        pl.when(jnp.logical_not(first))(lambda: over(range(lat + REACH)))
    else:
        over(range(lat + 2 * REACH))


def forward_kernel(
    lat, slots, where_ref, own, other, sides, weight, gain, normed, hat, inv, taps, wide, mixed
):
    def sink(lane, i, at, value):
        mixed[i, at, lane] = value

    conv(
        lat, slots, False, where_ref, own, other, sides, weight, taps, wide,
        lambda lane: None, sink,
    )
    tile = 32 if mixed.shape[1] % 32 == 0 else 16
    tiles = mixed.shape[1] // tile

    def norm(step, carry):
        i, start = step // tiles, pl.multiple_of(step % tiles * tile, tile)
        at = pl.ds(start, tile)
        values = mixed[i, at, :]
        centred = values - jnp.mean(values, axis=-1, keepdims=True)
        scale = lax.rsqrt(jnp.mean(centred * centred, axis=-1, keepdims=True) + 1e-06)
        live = start + lax.broadcasted_iota(jnp.int32, (tile, 1), 0) < where_ref[1]
        unit = jnp.where(live, centred * scale, 0.0)
        hat[i, at, :] = unit
        normed[i, at, :] = (unit * gain[...]).astype(BF16)
        inv[i, at, :] = jnp.broadcast_to(jnp.where(live, scale, 0.0), (tile, LANES))
        return carry

    lax.fori_loop(0, lat * tiles, norm, 0)


def backward_kernel(
    lat, slots, where_ref, own, other, sides, weight, cot, out, taps, wide, mixed
):
    def sink(lane, i, at, value):
        mixed[i, at, :] = value

    def finish(lane):
        live = lax.broadcasted_iota(jnp.int32, (slots, 1), 0) < where_ref[1]
        for i in range(lat):
            total = cot[i, :, lane].astype(F32) + mixed[i, :slots, :]
            out[i, :, lane] = jnp.where(live, total, 0.0).astype(BF16)

    conv(lat, slots, True, where_ref, own, other, sides, weight, taps, wide, finish, sink)


def kernel_call(kernel, lat, slots, slots_pad, width, outs, mixed, operands):
    vmem = pl.BlockSpec(memory_space=pltpu.VMEM)
    return pl.pallas_call(
        functools.partial(kernel, lat, slots),
        out_shape=outs,
        in_specs=[pl.BlockSpec(memory_space=pltpu.SMEM)] + [vmem] * (len(operands) - 1),
        out_specs=jax.tree.map(lambda _: vmem, outs),
        scratch_shapes=[
            pltpu.VMEM((KS * KS, 8, LANES), F32),
            pltpu.VMEM((lat + 2 * REACH, slots_pad + 16, LANES), F32),
            pltpu.VMEM(mixed, F32),
        ],
        compiler_params=pltpu.CompilerParams(vmem_limit_bytes=12 * 2**20),
        cost_estimate=pl.CostEstimate(flops=2**20, bytes_accessed=2**20, transcendentals=0),
    )(*operands)


def gate(values):
    cumulative = 0.5 * (1.0 + lax.erf(values * (1.0 / math.sqrt(2.0))))
    density = jnp.exp(-0.5 * values * values) * (1.0 / math.sqrt(2.0 * math.pi))
    return cumulative, density


def upper(bit):
    return (lax.axis_index("lon") & bit) // bit


def swapped(value, bit):
    count = lax.axis_size("lon")
    return lax.ppermute(value, "lon", [(i, i ^ bit) for i in range(count)])


def cut(part, which):
    half = part.shape[0] // 2
    return lax.dynamic_slice_in_dim(part, which * half, half, 0)


def merged(low_first, own, got):
    high = low_first == 1
    return jnp.concatenate([jnp.where(high, got, own), jnp.where(high, own, got)], axis=0)


def lon_bits():
    bits, bit = [], 1
    while bit < lax.axis_size("lon"):
        bits.append(bit)
        bit *= 2
    return bits


class State:
    def __init__(self):
        self.held = {}

    def sync(self, *more):
        names = list(self.held)
        tied = lax.optimization_barrier(tuple(self.held.values()) + more)
        self.held = dict(zip(names, tied))
        return tied[len(names) :]


class Pair:
    def __init__(self, state, name, parts, ways):
        self.state, self.names, self.sent = state, (name + "0", name + "1"), None
        self.keep(parts)
        self.stages = []
        for near, far in ways:
            groups = [[b] for b in near] + [far[:-1]]
            down = [(g, "down") for g in groups]
            up = [(g[::-1], "up") for g in groups[::-1]]
            self.stages.append(down + [(far[-1:], "meet")] + up)

    def keep(self, parts):
        self.state.held.update(zip(self.names, parts))

    def parts(self):
        return [self.state.held[name] for name in self.names]

    def outgoing(self, bits, kind):
        if kind == "down":
            return [cut(p, 1 - upper(b)) for p, b in zip(self.parts(), bits)]
        return self.parts()

    def launch(self, bits, kind, sent):
        self.sent = (bits, kind, [swapped(v, b) for v, b in zip(sent, bits)])

    def start(self, bits, kind):
        sent = self.outgoing(bits, kind)
        self.launch(bits, kind, self.state.sync(*sent))

    def close(self):
        bits, kind, got = self.sent
        parts = self.parts()
        if kind == "up":
            self.keep([merged(upper(b), p, g) for p, g, b in zip(parts, got, bits)])
            return
        if kind == "down":
            parts = [cut(p, upper(b)) for p, b in zip(parts, bits)]
        self.keep([(p.astype(F32) + g.astype(F32)).astype(BF16) for p, g in zip(parts, got)])

    def next_stage(self):
        groups = [stages.pop(0) for stages in self.stages]
        return list(zip(*(bits for bits, _ in groups))), groups[0][1]

    def open(self):
        steps, kind = self.next_stage()
        for bits in steps[:-1]:
            self.start(bits, kind)
            self.close()
        self.start(steps[-1], kind)

    def open_pieces(self, shares):
        (bits,), kind = self.next_stage()
        sent = self.outgoing(bits, kind)
        rows, at, pieces = sent[0].shape[0], 0, []
        for share in shares:
            pieces.append([v[at : at + rows // share] for v in sent])
            at += rows // share
        flat = self.state.sync(*[v for piece in pieces for v in piece])
        count = len(sent)
        for k in range(1, len(shares)):
            self.state.held.update(zip(self.tags("r", k), flat[k * count : (k + 1) * count]))
        self.launch(bits, kind, flat[:count])
        self.piece, self.pieces = 0, len(shares)

    def tags(self, kind, k):
        return [name + kind + str(k) for name in self.names]

    def arrived(self):
        self.state.held.update(zip(self.tags("g", self.piece), self.sent[2]))

    def next_piece(self):
        self.piece += 1
        sent = [self.state.held.pop(tag) for tag in self.tags("r", self.piece)]
        self.launch(self.sent[0], self.sent[1], self.state.sync(*sent))

    def gather_pieces(self):
        self.arrived()
        got = [
            [self.state.held.pop(tag) for tag in self.tags("g", k)] for k in range(self.pieces)
        ]
        both = [jnp.concatenate(parts, axis=0) for parts in zip(*got)]
        self.sent = (*self.sent[:2], both)

    def advance(self):
        self.close()
        self.open()


def both_ways():
    bits = lon_bits()
    fast, slow = bits[:2], bits[2:]
    return (fast, slow), (fast[::-1], slow[::-1])


def all_rows(own):
    if lax.axis_size("mlp") == 2:
        return jnp.concatenate([own, lax.ppermute(own, "mlp", [(0, 1), (1, 0)])], axis=0)
    return lax.all_gather(own, "mlp", axis=0, tiled=True)


def own_rows_sum(partial):
    if lax.axis_size("mlp") == 2:
        rows = partial.shape[0] // 2
        theirs = lax.ppermute(partial[rows:], "mlp", [(0, 1), (1, 0)])
        return partial[:rows].astype(F32) + theirs.astype(F32)
    return lax.psum_scatter(partial, "mlp", scatter_dimension=0, tiled=True).astype(F32)


def across_rows(left, right):
    return lax.dot_general(left, right, (((0,), (0,)), ((), ())), preferred_element_type=F32)


def across_width(left, right):
    return lax.dot_general(left, right, (((1,), (1,)), ((), ())), preferred_element_type=F32)


def body(fields, cotangent, conv_weight, norm_gain, weight_in, weight_out):
    lat, slots, width = fields.shape
    slots_pad = -(-slots // 16) * 16
    held = live_count()
    slot_live = lax.broadcasted_iota(jnp.int32, (1, slots, 1), 1) < held
    spare = ((0, 0), (0, slots_pad - slots), (0, 0))
    where = places(lat, held)
    gain = norm_gain.astype(F32).reshape(1, width)
    cot_all = all_rows(jnp.pad(jnp.where(slot_live, cotangent, 0), spare).reshape(-1, width))

    grid = (lat, slots_pad, width)
    normed, hat, inv = kernel_call(
        forward_kernel, lat, slots, slots_pad, width,
        (
            jax.ShapeDtypeStruct(grid, BF16),
            jax.ShapeDtypeStruct(grid, F32),
            jax.ShapeDtypeStruct((lat, slots_pad, LANES), F32),
        ),
        grid,
        (where,) + halo(fields, slots, held) + (conv_weight, gain),
    )
    normed_all = all_rows(normed.reshape(-1, width))

    cells = lax.axis_size("mlp") * lat * LON
    factor = jnp.float32(1.0 / math.sqrt(cells))
    state = State()
    ways = both_ways()

    def pair(name, grad):
        half = grad.shape[0] // 2
        return Pair(state, name, (grad[:half], grad[half:]), ways)

    hidden = jnp.dot(normed_all, weight_in, preferred_element_type=F32)
    cumulative, density = gate(hidden)
    activated = (hidden * cumulative).astype(BF16)
    state.held["cot"] = cot_all
    a = pair("a", (across_rows(activated, cot_all) * factor).astype(BF16))
    a.open()
    upstream = across_width(state.held.pop("cot"), weight_out)
    grad_hidden = (upstream * (cumulative + hidden * density)).astype(BF16)
    partial = across_width(grad_hidden, weight_in).astype(BF16)
    grad_normed = own_rows_sum(partial)
    state.held["hidden"] = grad_hidden
    state.held["partial"] = partial
    a.advance()
    grad_first = across_rows(normed_all, state.held.pop("hidden")) * factor
    b = pair("b", grad_first.astype(BF16))
    a.advance()
    b.open_pieces((2, 2))

    b.arrived()
    a.advance()
    b.next_piece()
    b.arrived()
    a.advance()
    b.gather_pieces()
    b.advance()
    state.held["gain"] = gain
    state.sync()
    gain = state.held.pop("gain")
    del state.held["partial"]
    scaled = grad_normed.reshape(grid) * gain
    inv = inv[:, :, :1]
    grad_mixed = inv * (
        scaled
        - jnp.mean(scaled, axis=-1, keepdims=True)
        - hat * jnp.mean(scaled * hat, axis=-1, keepdims=True)
    )
    state.held["mixed"] = grad_mixed.astype(BF16)
    a.advance()
    b.advance()
    own, other, sides = halo(state.held.pop("mixed"), slots, held)

    b.advance()
    a.close()
    a.open_pieces((2, 2))
    a.arrived()
    b.advance()
    a.next_piece()
    a.arrived()
    b.advance()
    a.gather_pieces()
    a.close()
    b.advance()
    state.held["sides"] = sides
    state.sync()
    result = kernel_call(
        backward_kernel, lat, slots, slots_pad, width,
        jax.ShapeDtypeStruct((lat, slots, width), BF16),
        (lat, slots_pad, LANES),
        (where, own, other, state.held["sides"], conv_weight, cotangent),
    )
    b.close()
    out_second = jnp.concatenate(a.parts(), axis=0)
    out_first = jnp.concatenate(b.parts(), axis=0)
    return (result, out_first, out_second)


def solution(mesh):
    in_specs = (
        P("mlp", "lon", None),
        P("mlp", "lon", None),
        P(),
        P(),
        P(None, "mlp"),
        P("mlp", None),
    )
    out_specs = (P("mlp", "lon", None), P(None, "mlp"), P("mlp", None))
    return jax.shard_map(body, mesh=mesh, in_specs=in_specs, out_specs=out_specs, check_vma=False)
```

```python
import functools
import math

import jax
import jax.numpy as jnp
from jax import lax
from jax.experimental import pallas as pl
from jax.experimental.pallas import tpu as pltpu
from jax.sharding import PartitionSpec as P

KS = 7
LON = 1440
REACH = KS // 2
LANES = 128
BF16 = jnp.bfloat16
F32 = jnp.float32
LEAD = 8


def passed_along(value, axis, by):
    count = lax.axis_size(axis)
    return lax.ppermute(value, axis, [(i, (i + by) % count) for i in range(count)])


def live_count():
    members = lax.axis_size("lon")
    position = lax.axis_index("lon")
    return LON // members + (position < LON % members).astype(jnp.int32)


def halo(own, slots, held):
    lat, count = own.shape[0], lax.axis_size("mlp")
    if count == 2:
        mine = jnp.where(lax.axis_index("mlp") == 0, own[lat - REACH :], own[:REACH])
        other = lax.ppermute(mine, "mlp", [(0, 1), (1, 0)])
    else:
        ends = count - 1
        other = jnp.concatenate(
            [
                lax.ppermute(own[lat - REACH :], "mlp", [(i, i + 1) for i in range(ends)]),
                lax.ppermute(own[:REACH], "mlp", [(i + 1, i) for i in range(ends)]),
            ],
            axis=0,
        )
    even = LON % lax.axis_size("lon") == 0
    both = (own, other)
    first = jnp.concatenate([v[:, :REACH] for v in both], axis=0)
    if even:
        last = jnp.concatenate([v[:, slots - REACH : slots] for v in both], axis=0)
    else:
        last = jnp.concatenate(
            [lax.dynamic_slice_in_dim(v, held - REACH, REACH, 1) for v in both], axis=0
        )
    left = passed_along(last, "lon", 1)
    right = passed_along(first, "lon", -1)
    if not even:
        rows = jnp.concatenate([v[:, :slots] for v in both], axis=0)
        joined = jnp.concatenate([rows, jnp.zeros_like(right)], axis=1)
        joined = lax.dynamic_update_slice_in_dim(joined, right, held, 1)
        own, other, right = joined[:lat, :slots], joined[lat:, :slots], joined[:, slots:]
    return own, other, jnp.concatenate([left, right], axis=1)


def places(lat, held):
    near = jnp.int32(0)
    if lax.axis_size("mlp") == 2:
        near = jnp.where(lax.axis_index("mlp") == 0, lat + REACH, 0).astype(jnp.int32)
        return jnp.stack([near, held.astype(jnp.int32)])
    return jnp.stack([near, held.astype(jnp.int32), jnp.int32(lat + REACH)])


def conv_tile(lat, slots, rows, flip, where_ref, own, other, sides, taps, wide, lane, sink):
    groups = other.shape[0] // REACH
    wide[REACH : REACH + lat, LEAD : LEAD + slots, :] = own[:, :slots, lane].astype(F32)
    ends = sides[:, :, lane].astype(F32)
    wide[REACH : REACH + lat, LEAD - REACH : LEAD, :] = ends[:lat, :REACH]
    wide[REACH : REACH + lat, LEAD + slots : LEAD + slots + REACH, :] = ends[:lat, REACH:]
    for g in range(groups):
        for k in range(REACH):
            at, src = where_ref[2 * g] + k, g * REACH + k
            wide[at, LEAD : LEAD + slots, :] = other[src, :slots, lane].astype(F32)
            wide[at, LEAD - REACH : LEAD, :] = ends[lat + src, :REACH]
            wide[at, LEAD + slots : LEAD + slots + REACH, :] = ends[lat + src, REACH:]

    def step(jt, carry):
        start = jt * 16
        acc = [[jnp.zeros((8, LANES), F32) for _ in range(lat)] for _ in range(2)]
        for b in range(KS):
            used = [a * KS + b for a in range(KS)]
            if flip:
                used = [KS * KS - 1 - t for t in used]
            taken = [taps[t] for t in used]
            for r in rows:
                for half in range(2):
                    cells = wide[r, pl.ds(start + 8 * half + LEAD - REACH + b, 8), :]
                    for i in range(max(0, r - KS + 1), min(lat, r + 1)):
                        acc[half][i] = acc[half][i] + taken[r - i] * cells
        for half in range(2):
            for i in range(lat):
                sink(i, pl.ds(pl.multiple_of(start + 8 * half, 8), 8), acc[half][i])
        return carry

    lax.fori_loop(0, -(-slots // 16), step, 0)


def conv(lat, slots, flip, where_ref, own, other, sides, weight, taps, wide, finish, sink):
    width = own.shape[-1]

    def over(rows):
        def channels(ct, carry):
            lane = pl.ds(pl.multiple_of(ct * LANES, LANES), LANES)
            for a in range(KS):
                row = weight[a, :, lane].astype(F32)
                for b in range(KS):
                    taps[a * KS + b] = jnp.broadcast_to(row[b : b + 1], (8, LANES))
            conv_tile(
                lat, slots, rows, flip, where_ref, own, other, sides, taps, wide, lane,
                functools.partial(sink, lane),
            )
            finish(lane)
            return carry

        lax.fori_loop(0, width // LANES, channels, 0)

    if other.shape[0] == REACH:
        first = where_ref[0] != 0
        pl.when(first)(lambda: over(range(REACH, lat + 2 * REACH)))
        pl.when(jnp.logical_not(first))(lambda: over(range(lat + REACH)))
    else:
        over(range(lat + 2 * REACH))


def forward_kernel(
    lat, slots, where_ref, own, other, sides, weight, gain, normed, hat, inv, taps, wide, mixed
):
    def sink(lane, i, at, value):
        mixed[i, at, lane] = value

    conv(
        lat, slots, False, where_ref, own, other, sides, weight, taps, wide,
        lambda lane: None, sink,
    )
    tile = 32 if mixed.shape[1] % 32 == 0 else 16
    tiles = mixed.shape[1] // tile

    def norm(step, carry):
        i, start = step // tiles, pl.multiple_of(step % tiles * tile, tile)
        at = pl.ds(start, tile)
        values = mixed[i, at, :]
        centred = values - jnp.mean(values, axis=-1, keepdims=True)
        scale = lax.rsqrt(jnp.mean(centred * centred, axis=-1, keepdims=True) + 1e-06)
        live = start + lax.broadcasted_iota(jnp.int32, (tile, 1), 0) < where_ref[1]
        unit = jnp.where(live, centred * scale, 0.0)
        hat[i, at, :] = unit
        normed[i, at, :] = (unit * gain[...]).astype(BF16)
        inv[i, at, :] = jnp.broadcast_to(jnp.where(live, scale, 0.0), (tile, LANES))
        return carry

    lax.fori_loop(0, lat * tiles, norm, 0)


def backward_kernel(
    lat, slots, where_ref, own, other, sides, weight, cot, out, taps, wide, mixed
):
    def sink(lane, i, at, value):
        mixed[i, at, :] = value

    def finish(lane):
        live = lax.broadcasted_iota(jnp.int32, (slots, 1), 0) < where_ref[1]
        for i in range(lat):
            total = cot[i, :, lane].astype(F32) + mixed[i, :slots, :]
            out[i, :, lane] = jnp.where(live, total, 0.0).astype(BF16)

    conv(lat, slots, True, where_ref, own, other, sides, weight, taps, wide, finish, sink)


def kernel_call(kernel, lat, slots, slots_pad, width, outs, mixed, operands):
    vmem = pl.BlockSpec(memory_space=pltpu.VMEM)
    return pl.pallas_call(
        functools.partial(kernel, lat, slots),
        out_shape=outs,
        in_specs=[pl.BlockSpec(memory_space=pltpu.SMEM)] + [vmem] * (len(operands) - 1),
        out_specs=jax.tree.map(lambda _: vmem, outs),
        scratch_shapes=[
            pltpu.VMEM((KS * KS, 8, LANES), F32),
            pltpu.VMEM((lat + 2 * REACH, slots_pad + 16, LANES), F32),
            pltpu.VMEM(mixed, F32),
        ],
        compiler_params=pltpu.CompilerParams(vmem_limit_bytes=12 * 2**20),
        cost_estimate=pl.CostEstimate(flops=2**20, bytes_accessed=2**20, transcendentals=0),
    )(*operands)


def gate(values):
    cumulative = 0.5 * (1.0 + lax.erf(values * (1.0 / math.sqrt(2.0))))
    density = jnp.exp(-0.5 * values * values) * (1.0 / math.sqrt(2.0 * math.pi))
    return cumulative, density


def upper(bit):
    return (lax.axis_index("lon") & bit) // bit


def swapped(value, bit):
    count = lax.axis_size("lon")
    return lax.ppermute(value, "lon", [(i, i ^ bit) for i in range(count)])


def merged(low_first, own, got):
    place = lax.broadcasted_iota(jnp.int32, (2, 1, 1), 0) == low_first
    return jnp.where(place, own[None], got[None]).reshape(-1, own.shape[1])


def lon_bits():
    bits, bit = [], 1
    while bit < lax.axis_size("lon"):
        bits.append(bit)
        bit *= 2
    return bits


class State:
    def __init__(self):
        self.held = {}

    def sync(self, *more):
        names = list(self.held)
        tied = lax.optimization_barrier(tuple(self.held.values()) + more)
        self.held = dict(zip(names, tied))
        return tied[len(names) :]


class Pair:
    def __init__(self, state, name, parts, ways):
        self.state, self.names, self.sent = state, (name + "0", name + "1"), None
        self.terms, self.rows = [[], []], 0
        self.keep(parts)
        self.stages = []
        for near, far in ways:
            groups = [[b] for b in near] + [far[:-1]]
            down = [(g, "down") for g in groups]
            up = [(g[::-1], "up") for g in groups[::-1]]
            self.stages.append(down + [(far[-1:], "meet")] + up)

    def keep(self, parts):
        for terms in self.terms:
            for key, _ in terms:
                del self.state.held[key]
        self.terms = [[(name + "t0", 0)] for name in self.names]
        self.state.held.update((terms[0][0], p) for terms, p in zip(self.terms, parts))
        self.rows = parts[0].shape[0]

    def parts(self):
        return [self.state.held[terms[0][0]] for terms in self.terms]

    def rows_of(self, terms, start, rows):
        total = 0.0
        for key, offset in terms:
            rows_here = lax.dynamic_slice_in_dim(self.state.held[key], offset + start, rows, 0)
            total = total + rows_here.astype(F32)
        return total.astype(BF16)

    def outgoing(self, bits, kind):
        if kind == "down":
            half = self.rows // 2
            return [
                self.rows_of(terms, (1 - upper(b)) * half, half)
                for terms, b in zip(self.terms, bits)
            ]
        if kind == "meet":
            self.keep([self.rows_of(terms, 0, self.rows) for terms in self.terms])
        return self.parts()

    def launch(self, bits, kind, sent):
        self.sent = (bits, kind, [swapped(v, b) for v, b in zip(sent, bits)])

    def start(self, bits, kind):
        if kind == "down":
            self.launch(bits, kind, self.state.sync(*self.outgoing(bits, kind)))
        else:
            self.outgoing(bits, kind)
            self.state.sync()
            self.launch(bits, kind, self.parts())

    def close(self):
        bits, kind, got = self.sent
        if kind == "up":
            self.keep([merged(upper(b), p, g) for p, g, b in zip(self.parts(), got, bits)])
        elif kind == "meet":
            both = zip(self.parts(), got)
            self.keep([(p.astype(F32) + g.astype(F32)).astype(BF16) for p, g in both])
        else:
            self.rows //= 2
            for k, (g, b) in enumerate(zip(got, bits)):
                key = self.names[k] + "t" + str(len(self.terms[k]))
                moved = [(old, at + upper(b) * self.rows) for old, at in self.terms[k]]
                self.terms[k] = moved + [(key, 0)]
                self.state.held[key] = g

    def spread(self):
        return jnp.concatenate([p for p in self.parts() for _ in range(2)], axis=0)

    def fill(self, room):
        for k, (g, b) in enumerate(zip(self.sent[2], self.sent[0])):
            start = (2 * k + 1 - upper(b)) * self.rows
            room = lax.dynamic_update_slice_in_dim(room, g, start, 0)
        return room

    def joined(self):
        blocks = []
        for p, g, b in zip(self.parts(), self.sent[2], self.sent[0]):
            high = upper(b) == 1
            blocks += [jnp.where(high, g, p), jnp.where(high, p, g)]
        return jnp.concatenate(blocks, axis=0)

    def next_stage(self):
        groups = [stages.pop(0) for stages in self.stages]
        return list(zip(*(bits for bits, _ in groups))), groups[0][1]

    def open(self):
        steps, kind = self.next_stage()
        for bits in steps[:-1]:
            self.start(bits, kind)
            self.close()
        self.start(steps[-1], kind)

    def advance(self):
        self.close()
        self.open()

    def prepare(self, shares):
        (bits,), kind = self.next_stage()
        sent, at = self.outgoing(bits, kind), 0
        rows = sent[0].shape[0]
        for k, share in enumerate(shares):
            pieces = [v[at : at + rows // share] for v in sent]
            self.state.held.update(zip(self.tags("r", k), pieces))
            at += rows // share
        self.piece, self.pieces, self.going = -1, len(shares), (bits, kind)

    def tags(self, mark, k):
        return [name + mark + str(k) for name in self.names]

    def next_piece(self):
        self.piece += 1
        self.state.sync()
        sent = [self.state.held.pop(tag) for tag in self.tags("r", self.piece)]
        self.launch(*self.going, sent)

    def arrived(self):
        self.state.held.update(zip(self.tags("g", self.piece), self.sent[2]))

    def gather_pieces(self):
        self.arrived()
        got = [
            [self.state.held.pop(tag) for tag in self.tags("g", k)] for k in range(self.pieces)
        ]
        self.sent = (*self.going, [jnp.concatenate(parts, axis=0) for parts in zip(*got)])


def both_ways():
    bits = lon_bits()
    fast, slow = bits[:2], bits[2:]
    return (fast, slow), (fast[::-1], slow[::-1])


def all_rows(own):
    if lax.axis_size("mlp") == 2:
        return jnp.concatenate([own, lax.ppermute(own, "mlp", [(0, 1), (1, 0)])], axis=0)
    return lax.all_gather(own, "mlp", axis=0, tiled=True)


def own_rows_sum(partial):
    if lax.axis_size("mlp") == 2:
        rows = partial.shape[0] // 2
        theirs = lax.ppermute(partial[rows:], "mlp", [(0, 1), (1, 0)])
        return partial[:rows].astype(F32) + theirs.astype(F32)
    return lax.psum_scatter(partial, "mlp", scatter_dimension=0, tiled=True).astype(F32)


def across_rows(left, right):
    return lax.dot_general(left, right, (((0,), (0,)), ((), ())), preferred_element_type=F32)


def across_width(left, right):
    return lax.dot_general(left, right, (((1,), (1,)), ((), ())), preferred_element_type=F32)


def body(fields, cotangent, conv_weight, norm_gain, weight_in, weight_out):
    lat, slots, width = fields.shape
    slots_pad = -(-slots // 16) * 16
    held = live_count()
    slot_live = lax.broadcasted_iota(jnp.int32, (1, slots, 1), 1) < held
    spare = ((0, 0), (0, slots_pad - slots), (0, 0))
    where = places(lat, held)
    gain = norm_gain.astype(F32).reshape(1, width)
    cot_all = all_rows(jnp.pad(jnp.where(slot_live, cotangent, 0), spare).reshape(-1, width))

    grid = (lat, slots_pad, width)
    normed, hat, inv = kernel_call(
        forward_kernel, lat, slots, slots_pad, width,
        (
            jax.ShapeDtypeStruct(grid, BF16),
            jax.ShapeDtypeStruct(grid, F32),
            jax.ShapeDtypeStruct((lat, slots_pad, LANES), F32),
        ),
        grid,
        (where,) + halo(fields, slots, held) + (conv_weight, gain),
    )
    normed_all = all_rows(normed.reshape(-1, width))

    cells = lax.axis_size("mlp") * lat * LON
    factor = jnp.float32(1.0 / math.sqrt(cells))
    state = State()
    ways = both_ways()

    def pair(name, grad):
        half = grad.shape[0] // 2
        return Pair(state, name, (grad[:half], grad[half:]), ways)

    hidden = jnp.dot(normed_all, weight_in, preferred_element_type=F32)
    cumulative, density = gate(hidden)
    activated = (hidden * cumulative).astype(BF16)
    state.held["cot"] = cot_all
    a = pair("a", (across_rows(activated, cot_all) * factor).astype(BF16))
    a.open()
    upstream = across_width(state.held.pop("cot"), weight_out)
    grad_hidden = (upstream * (cumulative + hidden * density)).astype(BF16)
    partial = across_width(grad_hidden, weight_in).astype(BF16)
    grad_normed = own_rows_sum(partial)
    state.held["hidden"] = grad_hidden
    state.held["partial"] = partial
    a.advance()
    grad_first = across_rows(normed_all, state.held.pop("hidden")) * factor
    b = pair("b", grad_first.astype(BF16))
    b.prepare((2, 2))
    a.advance()
    b.next_piece()
    b.arrived()
    a.advance()
    b.next_piece()
    b.arrived()
    a.advance()
    b.gather_pieces()
    b.advance()
    state.held["gain"] = gain
    state.sync()
    gain = state.held.pop("gain")
    del state.held["partial"]
    scaled = grad_normed.reshape(grid) * gain
    inv = inv[:, :, :1]
    grad_mixed = inv * (
        scaled
        - jnp.mean(scaled, axis=-1, keepdims=True)
        - hat * jnp.mean(scaled * hat, axis=-1, keepdims=True)
    )
    state.held["mixed"] = grad_mixed.astype(BF16)
    a.advance()
    b.advance()
    own, other, sides = halo(state.held.pop("mixed"), slots, held)

    b.advance()
    a.close()
    a.prepare((2, 2))
    a.next_piece()
    a.arrived()
    b.advance()
    a.next_piece()
    a.arrived()
    b.advance()
    a.gather_pieces()
    b.advance()
    state.held["sides"] = sides
    state.held["room"] = b.spread()
    state.sync()
    result = kernel_call(
        backward_kernel, lat, slots, slots_pad, width,
        jax.ShapeDtypeStruct((lat, slots, width), BF16),
        (lat, slots_pad, LANES),
        (where, own, other, state.held["sides"], conv_weight, cotangent),
    )
    return (result, b.fill(state.held["room"]), a.joined())


def solution(mesh):
    in_specs = (
        P("mlp", "lon", None),
        P("mlp", "lon", None),
        P(),
        P(),
        P(None, "mlp"),
        P("mlp", None),
    )
    out_specs = (P("mlp", "lon", None), P(None, "mlp"), P("mlp", None))
    return jax.shard_map(body, mesh=mesh, in_specs=in_specs, out_specs=out_specs, check_vma=False)
```

```python
import functools
import math

import jax
import jax.numpy as jnp
from jax import lax
from jax.experimental import pallas as pl
from jax.experimental.pallas import tpu as pltpu
from jax.sharding import PartitionSpec as P

KS = 7
LON = 1440
REACH = KS // 2
LANES = 128
BF16 = jnp.bfloat16
F32 = jnp.float32
LEAD = 8


def passed_along(value, axis, by):
    count = lax.axis_size(axis)
    return lax.ppermute(value, axis, [(i, (i + by) % count) for i in range(count)])


def live_count():
    members = lax.axis_size("lon")
    position = lax.axis_index("lon")
    return LON // members + (position < LON % members).astype(jnp.int32)


def halo(own, slots, held):
    lat, count = own.shape[0], lax.axis_size("mlp")
    if count == 2:
        mine = jnp.where(lax.axis_index("mlp") == 0, own[lat - REACH :], own[:REACH])
        other = lax.ppermute(mine, "mlp", [(0, 1), (1, 0)])
    else:
        ends = count - 1
        other = jnp.concatenate(
            [
                lax.ppermute(own[lat - REACH :], "mlp", [(i, i + 1) for i in range(ends)]),
                lax.ppermute(own[:REACH], "mlp", [(i + 1, i) for i in range(ends)]),
            ],
            axis=0,
        )
    even = LON % lax.axis_size("lon") == 0
    both = (own, other)
    first = jnp.concatenate([v[:, :REACH] for v in both], axis=0)
    if even:
        last = jnp.concatenate([v[:, slots - REACH : slots] for v in both], axis=0)
    else:
        last = jnp.concatenate(
            [lax.dynamic_slice_in_dim(v, held - REACH, REACH, 1) for v in both], axis=0
        )
    left = passed_along(last, "lon", 1)
    right = passed_along(first, "lon", -1)
    if not even:
        rows = jnp.concatenate([v[:, :slots] for v in both], axis=0)
        joined = jnp.concatenate([rows, jnp.zeros_like(right)], axis=1)
        joined = lax.dynamic_update_slice_in_dim(joined, right, held, 1)
        own, other, right = joined[:lat, :slots], joined[lat:, :slots], joined[:, slots:]
    return own, other, jnp.concatenate([left, right], axis=1)


def places(lat, held):
    near = jnp.int32(0)
    if lax.axis_size("mlp") == 2:
        near = jnp.where(lax.axis_index("mlp") == 0, lat + REACH, 0).astype(jnp.int32)
        return jnp.stack([near, held.astype(jnp.int32)])
    return jnp.stack([near, held.astype(jnp.int32), jnp.int32(lat + REACH)])


def conv_tile(lat, slots, rows, flip, where_ref, own, other, sides, taps, wide, lane, sink):
    groups = other.shape[0] // REACH
    wide[REACH : REACH + lat, LEAD : LEAD + slots, :] = own[:, :slots, lane].astype(F32)
    ends = sides[:, :, lane].astype(F32)
    wide[REACH : REACH + lat, LEAD - REACH : LEAD, :] = ends[:lat, :REACH]
    wide[REACH : REACH + lat, LEAD + slots : LEAD + slots + REACH, :] = ends[:lat, REACH:]
    for g in range(groups):
        for k in range(REACH):
            at, src = where_ref[2 * g] + k, g * REACH + k
            wide[at, LEAD : LEAD + slots, :] = other[src, :slots, lane].astype(F32)
            wide[at, LEAD - REACH : LEAD, :] = ends[lat + src, :REACH]
            wide[at, LEAD + slots : LEAD + slots + REACH, :] = ends[lat + src, REACH:]

    def step(jt, carry):
        start = jt * 16
        acc = [[jnp.zeros((8, LANES), F32) for _ in range(lat)] for _ in range(2)]
        for b in range(KS):
            used = [a * KS + b for a in range(KS)]
            if flip:
                used = [KS * KS - 1 - t for t in used]
            taken = [taps[t] for t in used]
            for r in rows:
                for half in range(2):
                    cells = wide[r, pl.ds(start + 8 * half + LEAD - REACH + b, 8), :]
                    for i in range(max(0, r - KS + 1), min(lat, r + 1)):
                        acc[half][i] = acc[half][i] + taken[r - i] * cells
        for half in range(2):
            for i in range(lat):
                sink(i, pl.ds(pl.multiple_of(start + 8 * half, 8), 8), acc[half][i])
        return carry

    lax.fori_loop(0, -(-slots // 16), step, 0)


def conv(lat, slots, flip, where_ref, own, other, sides, weight, taps, wide, finish, sink):
    width = own.shape[-1]

    def over(rows):
        def channels(ct, carry):
            lane = pl.ds(pl.multiple_of(ct * LANES, LANES), LANES)
            for a in range(KS):
                row = weight[a, :, lane].astype(F32)
                for b in range(KS):
                    taps[a * KS + b] = jnp.broadcast_to(row[b : b + 1], (8, LANES))
            conv_tile(
                lat, slots, rows, flip, where_ref, own, other, sides, taps, wide, lane,
                functools.partial(sink, lane),
            )
            finish(lane)
            return carry

        lax.fori_loop(0, width // LANES, channels, 0)

    if other.shape[0] == REACH:
        first = where_ref[0] != 0
        pl.when(first)(lambda: over(range(REACH, lat + 2 * REACH)))
        pl.when(jnp.logical_not(first))(lambda: over(range(lat + REACH)))
    else:
        over(range(lat + 2 * REACH))


def forward_kernel(
    lat, slots, where_ref, own, other, sides, weight, gain, normed, hat, inv, taps, wide, mixed
):
    def sink(lane, i, at, value):
        mixed[i, at, lane] = value

    conv(
        lat, slots, False, where_ref, own, other, sides, weight, taps, wide,
        lambda lane: None, sink,
    )
    tile = 32 if mixed.shape[1] % 32 == 0 else 16
    tiles = mixed.shape[1] // tile

    def norm(step, carry):
        i, start = step // tiles, pl.multiple_of(step % tiles * tile, tile)
        at = pl.ds(start, tile)
        values = mixed[i, at, :]
        centred = values - jnp.mean(values, axis=-1, keepdims=True)
        scale = lax.rsqrt(jnp.mean(centred * centred, axis=-1, keepdims=True) + 1e-06)
        live = start + lax.broadcasted_iota(jnp.int32, (tile, 1), 0) < where_ref[1]
        unit = jnp.where(live, centred * scale, 0.0)
        hat[i, at, :] = unit
        normed[i, at, :] = (unit * gain[...]).astype(BF16)
        inv[i, at, :] = jnp.broadcast_to(jnp.where(live, scale, 0.0), (tile, LANES))
        return carry

    lax.fori_loop(0, lat * tiles, norm, 0)


def backward_kernel(
    lat, slots, where_ref, own, other, sides, weight, cot, out, taps, wide, mixed
):
    def sink(lane, i, at, value):
        mixed[i, at, :] = value

    def finish(lane):
        live = lax.broadcasted_iota(jnp.int32, (slots, 1), 0) < where_ref[1]
        for i in range(lat):
            total = cot[i, :, lane].astype(F32) + mixed[i, :slots, :]
            out[i, :, lane] = jnp.where(live, total, 0.0).astype(BF16)

    conv(lat, slots, True, where_ref, own, other, sides, weight, taps, wide, finish, sink)


def kernel_call(kernel, lat, slots, slots_pad, width, outs, mixed, operands):
    vmem = pl.BlockSpec(memory_space=pltpu.VMEM)
    return pl.pallas_call(
        functools.partial(kernel, lat, slots),
        out_shape=outs,
        in_specs=[pl.BlockSpec(memory_space=pltpu.SMEM)] + [vmem] * (len(operands) - 1),
        out_specs=jax.tree.map(lambda _: vmem, outs),
        scratch_shapes=[
            pltpu.VMEM((KS * KS, 8, LANES), F32),
            pltpu.VMEM((lat + 2 * REACH, slots_pad + 16, LANES), F32),
            pltpu.VMEM(mixed, F32),
        ],
        compiler_params=pltpu.CompilerParams(vmem_limit_bytes=12 * 2**20),
        cost_estimate=pl.CostEstimate(flops=2**20, bytes_accessed=2**20, transcendentals=0),
    )(*operands)


def gate(values):
    cumulative = 0.5 * (1.0 + lax.erf(values * (1.0 / math.sqrt(2.0))))
    density = jnp.exp(-0.5 * values * values) * (1.0 / math.sqrt(2.0 * math.pi))
    return cumulative, density


def upper(bit):
    return (lax.axis_index("lon") & bit) // bit


def swapped(value, bit):
    count = lax.axis_size("lon")
    return lax.ppermute(value, "lon", [(i, i ^ bit) for i in range(count)])


def merged(low_first, own, got):
    place = lax.broadcasted_iota(jnp.int32, (2, 1, 1), 0) == low_first
    return jnp.where(place, own[None], got[None]).reshape(-1, own.shape[1])


def lon_bits():
    bits, bit = [], 1
    while bit < lax.axis_size("lon"):
        bits.append(bit)
        bit *= 2
    return bits


class State:
    def __init__(self):
        self.held = {}

    def sync(self, *more):
        names = list(self.held)
        tied = lax.optimization_barrier(tuple(self.held.values()) + more)
        self.held = dict(zip(names, tied))
        return tied[len(names) :]


class Pair:
    def __init__(self, state, name, parts, ways):
        self.state, self.names, self.sent = state, (name + "0", name + "1"), None
        self.terms, self.rows = [[], []], 0
        self.keep(parts)
        self.stages = []
        for near, far in ways:
            down = [(g, "down") for g in [near[:1], near[1:], far[:-1]]]
            self.stages.append(down + [(far[-1:], "meet"), (far[-2::-1], "up")])
        self.near = [near for near, _ in ways]

    def keep(self, parts):
        for terms in self.terms:
            for key, _ in terms:
                del self.state.held[key]
        self.terms = [[(name + "t0", 0)] for name in self.names]
        self.state.held.update((terms[0][0], p) for terms, p in zip(self.terms, parts))
        self.rows = parts[0].shape[0]

    def parts(self):
        return [self.state.held[terms[0][0]] for terms in self.terms]

    def rows_of(self, terms, start, rows):
        total = 0.0
        for key, offset in terms:
            rows_here = lax.dynamic_slice_in_dim(self.state.held[key], offset + start, rows, 0)
            total = total + rows_here.astype(F32)
        return total.astype(BF16)

    def outgoing(self, bits, kind):
        if kind == "down":
            half = self.rows // 2
            return [
                self.rows_of(terms, (1 - upper(b)) * half, half)
                for terms, b in zip(self.terms, bits)
            ]
        if kind == "meet":
            self.keep([self.rows_of(terms, 0, self.rows) for terms in self.terms])
        return self.parts()

    def launch(self, bits, kind, sent):
        self.sent = (bits, kind, [swapped(v, b) for v, b in zip(sent, bits)])

    def start(self, bits, kind):
        if kind == "down":
            self.launch(bits, kind, self.state.sync(*self.outgoing(bits, kind)))
        else:
            self.outgoing(bits, kind)
            self.state.sync()
            self.launch(bits, kind, self.parts())

    def close(self):
        bits, kind, got = self.sent
        if kind == "up":
            self.keep([merged(upper(b), p, g) for p, g, b in zip(self.parts(), got, bits)])
        elif kind == "meet":
            both = zip(self.parts(), got)
            self.keep([(p.astype(F32) + g.astype(F32)).astype(BF16) for p, g in both])
        else:
            self.rows //= 2
            for k, (g, b) in enumerate(zip(got, bits)):
                key = self.names[k] + "t" + str(len(self.terms[k]))
                moved = [(old, at + upper(b) * self.rows) for old, at in self.terms[k]]
                self.terms[k] = moved + [(key, 0)]
                self.state.held[key] = g

    def cross(self, which, name):
        self.state.sync()
        sent = [self.state.held[tag] for tag in self.tags(name)]
        return [swapped(v, near[which]) for v, near in zip(sent, self.near)]

    def arrive(self, name, values):
        self.state.held.update(zip(self.tags(name), values))

    def tags(self, name):
        return [own + name for own in self.names]

    def place(self, out, values, other0, other1):
        for k, (v, (bit0, bit1)) in enumerate(zip(values, self.near)):
            block = 4 * k + 2 * (upper(bit0) ^ other0) + (upper(bit1) ^ other1)
            out = lax.dynamic_update_slice_in_dim(out, v, block * self.rows, 0)
        return out

    def spread(self):
        own = self.parts()
        out = jnp.zeros((4 * len(own) * self.rows, own[0].shape[1]), BF16)
        return self.place(out, own, 0, 0)

    def get(self, name):
        return [self.state.held[tag] for tag in self.tags(name)]

    def next_stage(self):
        groups = [stages.pop(0) for stages in self.stages]
        return list(zip(*(bits for bits, _ in groups))), groups[0][1]

    def open(self):
        steps, kind = self.next_stage()
        for bits in steps[:-1]:
            self.start(bits, kind)
            self.close()
        self.start(steps[-1], kind)

    def advance(self):
        self.close()
        self.open()

    def prepare(self, shares):
        (bits,), kind = self.next_stage()
        sent, at = self.outgoing(bits, kind), 0
        rows = sent[0].shape[0]
        for k, share in enumerate(shares):
            self.arrive("r" + str(k), [v[at : at + rows // share] for v in sent])
            at += rows // share
        self.piece, self.pieces, self.going = -1, len(shares), (bits, kind)

    def next_piece(self):
        self.piece += 1
        self.state.sync()
        sent = [self.state.held.pop(tag) for tag in self.tags("r" + str(self.piece))]
        self.launch(*self.going, sent)

    def arrived(self):
        self.arrive("g" + str(self.piece), self.sent[2])

    def gather_pieces(self):
        self.arrived()
        got = [
            [self.state.held.pop(tag) for tag in self.tags("g" + str(k))]
            for k in range(self.pieces)
        ]
        self.sent = (*self.going, [jnp.concatenate(parts, axis=0) for parts in zip(*got)])


def both_ways():
    bits = lon_bits()
    fast, slow = bits[:2], bits[2:]
    return (fast, slow), (fast[::-1], slow[::-1])


def all_rows(own):
    if lax.axis_size("mlp") == 2:
        return jnp.concatenate([own, lax.ppermute(own, "mlp", [(0, 1), (1, 0)])], axis=0)
    return lax.all_gather(own, "mlp", axis=0, tiled=True)


def own_rows_sum(partial):
    if lax.axis_size("mlp") == 2:
        rows = partial.shape[0] // 2
        theirs = lax.ppermute(partial[rows:], "mlp", [(0, 1), (1, 0)])
        return partial[:rows].astype(F32) + theirs.astype(F32)
    return lax.psum_scatter(partial, "mlp", scatter_dimension=0, tiled=True).astype(F32)


def across_rows(left, right):
    return lax.dot_general(left, right, (((0,), (0,)), ((), ())), preferred_element_type=F32)


def across_width(left, right):
    return lax.dot_general(left, right, (((1,), (1,)), ((), ())), preferred_element_type=F32)


def body(fields, cotangent, conv_weight, norm_gain, weight_in, weight_out):
    lat, slots, width = fields.shape
    slots_pad = -(-slots // 16) * 16
    held = live_count()
    slot_live = lax.broadcasted_iota(jnp.int32, (1, slots, 1), 1) < held
    spare = ((0, 0), (0, slots_pad - slots), (0, 0))
    where = places(lat, held)
    gain = norm_gain.astype(F32).reshape(1, width)
    cot_all = all_rows(jnp.pad(jnp.where(slot_live, cotangent, 0), spare).reshape(-1, width))

    grid = (lat, slots_pad, width)
    normed, hat, inv = kernel_call(
        forward_kernel, lat, slots, slots_pad, width,
        (
            jax.ShapeDtypeStruct(grid, BF16),
            jax.ShapeDtypeStruct(grid, F32),
            jax.ShapeDtypeStruct((lat, slots_pad, LANES), F32),
        ),
        grid,
        (where,) + halo(fields, slots, held) + (conv_weight, gain),
    )
    normed_all = all_rows(normed.reshape(-1, width))

    cells = lax.axis_size("mlp") * lat * LON
    factor = jnp.float32(1.0 / math.sqrt(cells))
    state = State()
    ways = both_ways()

    def pair(name, grad):
        half = grad.shape[0] // 2
        return Pair(state, name, (grad[:half], grad[half:]), ways)

    hidden = jnp.dot(normed_all, weight_in, preferred_element_type=F32)
    cumulative, density = gate(hidden)
    activated = (hidden * cumulative).astype(BF16)
    state.held["cot"] = cot_all
    a = pair("a", (across_rows(activated, cot_all) * factor).astype(BF16))
    a.open()
    upstream = across_width(state.held.pop("cot"), weight_out)
    grad_hidden = (upstream * (cumulative + hidden * density)).astype(BF16)
    partial = across_width(grad_hidden, weight_in).astype(BF16)
    grad_normed = own_rows_sum(partial)
    state.held["hidden"] = grad_hidden
    state.held["partial"] = partial
    a.advance()
    grad_first = across_rows(normed_all, state.held.pop("hidden")) * factor
    b = pair("b", grad_first.astype(BF16))
    state.held["gain"] = gain
    state.held["back"] = grad_normed
    a.advance()
    b.prepare((2, 2))
    b.next_piece()

    scaled = state.held.pop("back").reshape(grid) * state.held.pop("gain")
    inv = inv[:, :, :1]
    grad_mixed = inv * (
        scaled
        - jnp.mean(scaled, axis=-1, keepdims=True)
        - hat * jnp.mean(scaled * hat, axis=-1, keepdims=True)
    )
    del state.held["partial"]
    b.arrived()
    a.advance()
    b.next_piece()
    state.held["mixed"] = grad_mixed.astype(BF16)
    b.arrived()
    a.advance()
    b.gather_pieces()
    b.advance()
    a.close()
    from_near = a.cross(1, "t0")
    b.advance()
    own, other, sides = halo(state.held.pop("mixed"), slots, held)

    b.advance()
    a.arrive("n", from_near)
    from_far = a.cross(0, "t0")
    a.arrive("f", from_far)
    b.advance()
    from_both = a.cross(0, "n")
    a.arrive("b", from_both)
    b.close()
    from_near = b.cross(1, "t0")
    from_far = b.cross(0, "t0")
    state.held["sides"] = sides
    state.sync()
    state.held["result"] = kernel_call(
        backward_kernel, lat, slots, slots_pad, width,
        jax.ShapeDtypeStruct((lat, slots, width), BF16),
        (lat, slots_pad, LANES),
        (where, own, other, state.held["sides"], conv_weight, cotangent),
    )
    state.held["out"] = b.spread()
    b.arrive("n", from_near)
    b.arrive("f", from_far)
    from_both = b.cross(0, "n")
    out_first = b.place(b.place(state.held["out"], b.get("n"), 0, 1), b.get("f"), 1, 0)
    out_second = a.place(a.place(a.spread(), a.get("n"), 0, 1), a.get("f"), 1, 0)
    out_second = a.place(out_second, a.get("b"), 1, 1)
    return (state.held["result"], b.place(out_first, from_both, 1, 1), out_second)


def solution(mesh):
    in_specs = (
        P("mlp", "lon", None),
        P("mlp", "lon", None),
        P(),
        P(),
        P(None, "mlp"),
        P("mlp", None),
    )
    out_specs = (P("mlp", "lon", None), P(None, "mlp"), P("mlp", None))
    return jax.shard_map(body, mesh=mesh, in_specs=in_specs, out_specs=out_specs, check_vma=False)
```

```python
import functools
import math

import jax
import jax.numpy as jnp
from jax import lax
from jax.experimental import pallas as pl
from jax.experimental.pallas import tpu as pltpu
from jax.sharding import PartitionSpec as P

KS = 7
LON = 1440
REACH = KS // 2
LANES = 128
BF16 = jnp.bfloat16
F32 = jnp.float32
LEAD = 8


def passed_along(value, axis, by):
    count = lax.axis_size(axis)
    return lax.ppermute(value, axis, [(i, (i + by) % count) for i in range(count)])


def live_count():
    members = lax.axis_size("lon")
    position = lax.axis_index("lon")
    return LON // members + (position < LON % members).astype(jnp.int32)


def halo(own, slots, held):
    lat, count = own.shape[0], lax.axis_size("mlp")
    if count == 2:
        mine = jnp.where(lax.axis_index("mlp") == 0, own[lat - REACH :], own[:REACH])
        other = lax.ppermute(mine, "mlp", [(0, 1), (1, 0)])
    else:
        ends = count - 1
        other = jnp.concatenate(
            [
                lax.ppermute(own[lat - REACH :], "mlp", [(i, i + 1) for i in range(ends)]),
                lax.ppermute(own[:REACH], "mlp", [(i + 1, i) for i in range(ends)]),
            ],
            axis=0,
        )
    even = LON % lax.axis_size("lon") == 0
    both = (own, other)
    first = jnp.concatenate([v[:, :REACH] for v in both], axis=0)
    if even:
        last = jnp.concatenate([v[:, slots - REACH : slots] for v in both], axis=0)
    else:
        last = jnp.concatenate(
            [lax.dynamic_slice_in_dim(v, held - REACH, REACH, 1) for v in both], axis=0
        )
    left = passed_along(last, "lon", 1)
    right = passed_along(first, "lon", -1)
    if not even:
        rows = jnp.concatenate([v[:, :slots] for v in both], axis=0)
        joined = jnp.concatenate([rows, jnp.zeros_like(right)], axis=1)
        joined = lax.dynamic_update_slice_in_dim(joined, right, held, 1)
        own, other, right = joined[:lat, :slots], joined[lat:, :slots], joined[:, slots:]
    return own, other, jnp.concatenate([left, right], axis=1)


def places(lat, held):
    near = jnp.int32(0)
    if lax.axis_size("mlp") == 2:
        near = jnp.where(lax.axis_index("mlp") == 0, lat + REACH, 0).astype(jnp.int32)
        return jnp.stack([near, held.astype(jnp.int32)])
    return jnp.stack([near, held.astype(jnp.int32), jnp.int32(lat + REACH)])


def conv_tile(lat, slots, rows, flip, where_ref, own, other, sides, taps, wide, lane, sink):
    groups = other.shape[0] // REACH
    wide[REACH : REACH + lat, LEAD : LEAD + slots, :] = own[:, :slots, lane].astype(F32)
    ends = sides[:, :, lane].astype(F32)
    wide[REACH : REACH + lat, LEAD - REACH : LEAD, :] = ends[:lat, :REACH]
    wide[REACH : REACH + lat, LEAD + slots : LEAD + slots + REACH, :] = ends[:lat, REACH:]
    for g in range(groups):
        for k in range(REACH):
            at, src = where_ref[2 * g] + k, g * REACH + k
            wide[at, LEAD : LEAD + slots, :] = other[src, :slots, lane].astype(F32)
            wide[at, LEAD - REACH : LEAD, :] = ends[lat + src, :REACH]
            wide[at, LEAD + slots : LEAD + slots + REACH, :] = ends[lat + src, REACH:]

    def step(jt, carry):
        start = jt * 16
        acc = [[jnp.zeros((8, LANES), F32) for _ in range(lat)] for _ in range(2)]
        for b in range(KS):
            used = [a * KS + b for a in range(KS)]
            if flip:
                used = [KS * KS - 1 - t for t in used]
            taken = [taps[t] for t in used]
            for r in rows:
                for half in range(2):
                    cells = wide[r, pl.ds(start + 8 * half + LEAD - REACH + b, 8), :]
                    for i in range(max(0, r - KS + 1), min(lat, r + 1)):
                        acc[half][i] = acc[half][i] + taken[r - i] * cells
        for half in range(2):
            for i in range(lat):
                sink(i, pl.ds(pl.multiple_of(start + 8 * half, 8), 8), acc[half][i])
        return carry

    lax.fori_loop(0, -(-slots // 16), step, 0)


def conv(lat, slots, flip, where_ref, own, other, sides, weight, taps, wide, finish, sink):
    width = own.shape[-1]

    def over(rows):
        def channels(ct, carry):
            lane = pl.ds(pl.multiple_of(ct * LANES, LANES), LANES)
            for a in range(KS):
                row = weight[a, :, lane].astype(F32)
                for b in range(KS):
                    taps[a * KS + b] = jnp.broadcast_to(row[b : b + 1], (8, LANES))
            conv_tile(
                lat, slots, rows, flip, where_ref, own, other, sides, taps, wide, lane,
                functools.partial(sink, lane),
            )
            finish(lane)
            return carry

        lax.fori_loop(0, width // LANES, channels, 0)

    if other.shape[0] == REACH:
        first = where_ref[0] != 0
        pl.when(first)(lambda: over(range(REACH, lat + 2 * REACH)))
        pl.when(jnp.logical_not(first))(lambda: over(range(lat + REACH)))
    else:
        over(range(lat + 2 * REACH))


def forward_kernel(
    lat, slots, where_ref, own, other, sides, weight, gain, normed, hat, inv, taps, wide, mixed
):
    def sink(lane, i, at, value):
        mixed[i, at, lane] = value

    conv(
        lat, slots, False, where_ref, own, other, sides, weight, taps, wide,
        lambda lane: None, sink,
    )
    tile = 32 if mixed.shape[1] % 32 == 0 else 16
    tiles = mixed.shape[1] // tile

    def norm(step, carry):
        i, start = step // tiles, pl.multiple_of(step % tiles * tile, tile)
        at = pl.ds(start, tile)
        values = mixed[i, at, :]
        centred = values - jnp.mean(values, axis=-1, keepdims=True)
        scale = lax.rsqrt(jnp.mean(centred * centred, axis=-1, keepdims=True) + 1e-06)
        live = start + lax.broadcasted_iota(jnp.int32, (tile, 1), 0) < where_ref[1]
        unit = jnp.where(live, centred * scale, 0.0)
        hat[i, at, :] = unit
        normed[i, at, :] = (unit * gain[...]).astype(BF16)
        inv[i, at, :] = jnp.broadcast_to(jnp.where(live, scale, 0.0), (tile, LANES))
        return carry

    lax.fori_loop(0, lat * tiles, norm, 0)


def backward_kernel(
    lat, slots, where_ref, own, other, sides, weight, cot, out, taps, wide, mixed
):
    def sink(lane, i, at, value):
        mixed[i, at, :] = value

    def finish(lane):
        live = lax.broadcasted_iota(jnp.int32, (slots, 1), 0) < where_ref[1]
        for i in range(lat):
            total = cot[i, :, lane].astype(F32) + mixed[i, :slots, :]
            out[i, :, lane] = jnp.where(live, total, 0.0).astype(BF16)

    conv(lat, slots, True, where_ref, own, other, sides, weight, taps, wide, finish, sink)


def kernel_call(kernel, lat, slots, slots_pad, width, outs, mixed, operands):
    vmem = pl.BlockSpec(memory_space=pltpu.VMEM)
    return pl.pallas_call(
        functools.partial(kernel, lat, slots),
        out_shape=outs,
        in_specs=[pl.BlockSpec(memory_space=pltpu.SMEM)] + [vmem] * (len(operands) - 1),
        out_specs=jax.tree.map(lambda _: vmem, outs),
        scratch_shapes=[
            pltpu.VMEM((KS * KS, 8, LANES), F32),
            pltpu.VMEM((lat + 2 * REACH, slots_pad + 16, LANES), F32),
            pltpu.VMEM(mixed, F32),
        ],
        compiler_params=pltpu.CompilerParams(vmem_limit_bytes=12 * 2**20),
        cost_estimate=pl.CostEstimate(flops=2**20, bytes_accessed=2**20, transcendentals=0),
    )(*operands)


def gate(values):
    cumulative = 0.5 * (1.0 + lax.erf(values * (1.0 / math.sqrt(2.0))))
    density = jnp.exp(-0.5 * values * values) * (1.0 / math.sqrt(2.0 * math.pi))
    return cumulative, density


def upper(bit):
    return (lax.axis_index("lon") & bit) // bit


def swapped(value, bit):
    count = lax.axis_size("lon")
    return lax.ppermute(value, "lon", [(i, i ^ bit) for i in range(count)])


def merged(low_first, own, got):
    place = lax.broadcasted_iota(jnp.int32, (2, 1, 1), 0) == low_first
    return jnp.where(place, own[None], got[None]).reshape(-1, own.shape[1])


def lon_bits():
    bits, bit = [], 1
    while bit < lax.axis_size("lon"):
        bits.append(bit)
        bit *= 2
    return bits


class State:
    def __init__(self):
        self.held = {}

    def sync(self, *more):
        names = list(self.held)
        tied = lax.optimization_barrier(tuple(self.held.values()) + more)
        self.held = dict(zip(names, tied))
        return tied[len(names) :]


class Pair:
    def __init__(self, state, name, parts, ways):
        self.state, self.names, self.sent = state, (name + "0", name + "1"), None
        self.terms, self.rows = [[], []], 0
        self.keep(parts)
        self.stages = []
        for near, far in ways:
            down = [(g, "down") for g in [near[:1], near[1:], far[:-1]]]
            self.stages.append(down + [(far[-1:], "meet"), (far[-2::-1], "up")])
        self.near = [near for near, _ in ways]

    def keep(self, parts):
        for terms in self.terms:
            for key, _ in terms:
                del self.state.held[key]
        self.terms = [[(name + "t0", 0)] for name in self.names]
        self.state.held.update((terms[0][0], p) for terms, p in zip(self.terms, parts))
        self.rows = parts[0].shape[0]

    def parts(self):
        return [self.state.held[terms[0][0]] for terms in self.terms]

    def rows_of(self, terms, start, rows):
        total = 0.0
        for key, offset in terms:
            rows_here = lax.dynamic_slice_in_dim(self.state.held[key], offset + start, rows, 0)
            total = total + rows_here.astype(F32)
        return total.astype(BF16)

    def outgoing(self, bits, kind):
        if kind == "down":
            half = self.rows // 2
            return [
                self.rows_of(terms, (1 - upper(b)) * half, half)
                for terms, b in zip(self.terms, bits)
            ]
        if kind == "meet":
            self.keep([self.rows_of(terms, 0, self.rows) for terms in self.terms])
        return self.parts()

    def launch(self, bits, kind, sent):
        self.sent = (bits, kind, [swapped(v, b) for v, b in zip(sent, bits)])

    def start(self, bits, kind):
        if kind == "down":
            self.launch(bits, kind, self.state.sync(*self.outgoing(bits, kind)))
        else:
            self.outgoing(bits, kind)
            self.state.sync()
            self.launch(bits, kind, self.parts())

    def close(self):
        bits, kind, got = self.sent
        if kind == "up":
            self.keep([merged(upper(b), p, g) for p, g, b in zip(self.parts(), got, bits)])
        elif kind == "meet":
            both = zip(self.parts(), got)
            self.keep([(p.astype(F32) + g.astype(F32)).astype(BF16) for p, g in both])
        else:
            if kind == "down":
                self.rows //= 2
            for k, (g, b) in enumerate(zip(got, bits)):
                key = self.names[k] + "t" + str(len(self.terms[k]))
                if kind == "down":
                    self.terms[k] = [(old, at + upper(b) * self.rows) for old, at in self.terms[k]]
                self.terms[k] = self.terms[k] + [(key, 0)]
                self.state.held[key] = g

    def cross(self, which, name):
        self.state.sync()
        sent = [self.state.held[tag] for tag in self.tags(name)]
        return [swapped(v, near[which]) for v, near in zip(sent, self.near)]

    def arrive(self, name, values):
        self.state.held.update(zip(self.tags(name), values))

    def tags(self, name):
        return [own + name for own in self.names]

    def place(self, out, values, other0, other1):
        for k, (v, (bit0, bit1)) in enumerate(zip(values, self.near)):
            block = 4 * k + 2 * (upper(bit0) ^ other0) + (upper(bit1) ^ other1)
            out = lax.dynamic_update_slice_in_dim(out, v, block * self.rows, 0)
        return out

    def spread(self):
        own = self.parts()
        out = jnp.zeros((4 * len(own) * self.rows, own[0].shape[1]), BF16)
        return self.place(out, own, 0, 0)

    def get(self, name):
        return [self.state.held[tag] for tag in self.tags(name)]

    def next_stage(self):
        groups = [stages.pop(0) for stages in self.stages]
        return list(zip(*(bits for bits, _ in groups))), groups[0][1]

    def open(self):
        steps, kind = self.next_stage()
        for bits in steps[:-1]:
            self.start(bits, kind)
            self.close()
        self.start(steps[-1], kind)

    def advance(self):
        self.close()
        self.open()

    def quarter(self, k, other0, other1):
        bit0, bit1 = self.near[k]
        block = 2 * (upper(bit0) ^ other0) + (upper(bit1) ^ other1)
        return block * (self.rows // 4)

    def prepare(self):
        self.next_stage()
        self.next_stage()
        whole, size = self.parts(), self.rows // 4
        for piece, other1 in (("r0", 1), ("r1", 0)):
            cuts = [
                lax.dynamic_slice_in_dim(v, self.quarter(k, 1, other1), size, 0)
                for k, v in enumerate(whole)
            ]
            self.arrive(piece, cuts)
        self.piece, self.going = -1, ([near[0] for near in self.near], "down")

    def forward(self):
        self.arrived()
        size, sent = self.rows // 4, []
        for k, (v, g) in enumerate(zip(self.parts(), self.get("g0"))):
            rows = lax.dynamic_slice_in_dim(v, self.quarter(k, 0, 1), size, 0)
            sent.append((rows.astype(F32) + g.astype(F32)).astype(BF16))
        for k, tag in enumerate(self.tags("g1")):
            self.terms[k] = [(self.terms[k][0][0], self.quarter(k, 0, 0)), (tag, 0)]
        for tag in self.tags("g0"):
            del self.state.held[tag]
        self.rows = size
        bits = [near[1] for near in self.near]
        self.launch(bits, "kept", self.state.sync(*sent))

    def next_piece(self):
        self.piece += 1
        self.state.sync()
        sent = [self.state.held.pop(tag) for tag in self.tags("r" + str(self.piece))]
        self.launch(*self.going, sent)

    def arrived(self):
        self.arrive("g" + str(self.piece), self.sent[2])


def both_ways():
    bits = lon_bits()
    fast, slow = bits[:2], bits[2:]
    return (fast, slow), (fast[::-1], slow[::-1])


def all_rows(own):
    if lax.axis_size("mlp") == 2:
        return jnp.concatenate([own, lax.ppermute(own, "mlp", [(0, 1), (1, 0)])], axis=0)
    return lax.all_gather(own, "mlp", axis=0, tiled=True)


def own_rows_sum(partial):
    if lax.axis_size("mlp") == 2:
        rows = partial.shape[0] // 2
        theirs = lax.ppermute(partial[rows:], "mlp", [(0, 1), (1, 0)])
        return partial[:rows].astype(F32) + theirs.astype(F32)
    return lax.psum_scatter(partial, "mlp", scatter_dimension=0, tiled=True).astype(F32)


def across_rows(left, right):
    return lax.dot_general(left, right, (((0,), (0,)), ((), ())), preferred_element_type=F32)


def across_width(left, right):
    return lax.dot_general(left, right, (((1,), (1,)), ((), ())), preferred_element_type=F32)


def body(fields, cotangent, conv_weight, norm_gain, weight_in, weight_out):
    lat, slots, width = fields.shape
    slots_pad = -(-slots // 16) * 16
    held = live_count()
    slot_live = lax.broadcasted_iota(jnp.int32, (1, slots, 1), 1) < held
    spare = ((0, 0), (0, slots_pad - slots), (0, 0))
    where = places(lat, held)
    gain = norm_gain.astype(F32).reshape(1, width)
    cot_all = all_rows(jnp.pad(jnp.where(slot_live, cotangent, 0), spare).reshape(-1, width))

    grid = (lat, slots_pad, width)
    normed, hat, inv = kernel_call(
        forward_kernel, lat, slots, slots_pad, width,
        (
            jax.ShapeDtypeStruct(grid, BF16),
            jax.ShapeDtypeStruct(grid, F32),
            jax.ShapeDtypeStruct((lat, slots_pad, LANES), F32),
        ),
        grid,
        (where,) + halo(fields, slots, held) + (conv_weight, gain),
    )
    normed_all = all_rows(normed.reshape(-1, width))

    cells = lax.axis_size("mlp") * lat * LON
    factor = jnp.float32(1.0 / math.sqrt(cells))
    state = State()
    ways = both_ways()

    def pair(name, grad):
        half = grad.shape[0] // 2
        return Pair(state, name, (grad[:half], grad[half:]), ways)

    hidden = jnp.dot(normed_all, weight_in, preferred_element_type=F32)
    cumulative, density = gate(hidden)
    activated = (hidden * cumulative).astype(BF16)
    state.held["cot"] = cot_all
    a = pair("a", (across_rows(activated, cot_all) * factor).astype(BF16))
    a.open()
    upstream = across_width(state.held.pop("cot"), weight_out)
    grad_hidden = (upstream * (cumulative + hidden * density)).astype(BF16)
    partial = across_width(grad_hidden, weight_in).astype(BF16)
    grad_normed = own_rows_sum(partial)
    state.held["hidden"] = grad_hidden
    state.held["partial"] = partial
    a.advance()
    grad_first = across_rows(normed_all, state.held.pop("hidden")) * factor
    b = pair("b", grad_first.astype(BF16))
    state.held["gain"] = gain
    state.held["inv"] = inv
    state.held["back"] = grad_normed
    a.advance()
    b.prepare()
    b.next_piece()

    scaled = state.held.pop("back").reshape(grid) * state.held.pop("gain")
    inv = state.held.pop("inv")[:, :, :1]
    grad_mixed = inv * (
        scaled
        - jnp.mean(scaled, axis=-1, keepdims=True)
        - hat * jnp.mean(scaled * hat, axis=-1, keepdims=True)
    )
    del state.held["partial"]
    b.arrived()
    a.advance()
    b.next_piece()
    state.held["mixed"] = grad_mixed.astype(BF16)
    b.arrived()
    a.advance()
    b.forward()
    a.close()
    from_near = a.cross(1, "t0")
    b.advance()
    own, other, sides = halo(state.held.pop("mixed"), slots, held)

    b.advance()
    a.arrive("n", from_near)
    from_far = a.cross(0, "t0")
    a.arrive("f", from_far)
    b.advance()
    from_both = a.cross(0, "n")
    a.arrive("b", from_both)
    b.close()
    from_near = b.cross(1, "t0")
    from_far = b.cross(0, "t0")
    state.held["sides"] = sides
    state.sync()
    state.held["result"] = kernel_call(
        backward_kernel, lat, slots, slots_pad, width,
        jax.ShapeDtypeStruct((lat, slots, width), BF16),
        (lat, slots_pad, LANES),
        (where, own, other, state.held["sides"], conv_weight, cotangent),
    )
    state.held["out"] = b.spread()
    b.arrive("n", from_near)
    b.arrive("f", from_far)
    from_both = b.cross(0, "n")
    out_first = b.place(b.place(state.held["out"], b.get("n"), 0, 1), b.get("f"), 1, 0)
    out_second = a.place(a.place(a.spread(), a.get("n"), 0, 1), a.get("f"), 1, 0)
    out_second = a.place(out_second, a.get("b"), 1, 1)
    return (state.held["result"], b.place(out_first, from_both, 1, 1), out_second)


def solution(mesh):
    in_specs = (
        P("mlp", "lon", None),
        P("mlp", "lon", None),
        P(),
        P(),
        P(None, "mlp"),
        P("mlp", None),
    )
    out_specs = (P("mlp", "lon", None), P(None, "mlp"), P("mlp", None))
    return jax.shard_map(body, mesh=mesh, in_specs=in_specs, out_specs=out_specs, check_vma=False)
```

```python
import functools
import math

import jax
import jax.numpy as jnp
from jax import lax
from jax.experimental import pallas as pl
from jax.experimental.pallas import tpu as pltpu
from jax.sharding import PartitionSpec as P

KS = 7
LON = 1440
REACH = KS // 2
LANES = 128
BF16 = jnp.bfloat16
F32 = jnp.float32
LEAD = 8


def passed_along(value, axis, by):
    count = lax.axis_size(axis)
    return lax.ppermute(value, axis, [(i, (i + by) % count) for i in range(count)])


def live_count():
    members = lax.axis_size("lon")
    position = lax.axis_index("lon")
    return LON // members + (position < LON % members).astype(jnp.int32)


def halo(own, slots, held):
    lat, count = own.shape[0], lax.axis_size("mlp")
    if count == 2:
        mine = jnp.where(lax.axis_index("mlp") == 0, own[lat - REACH :], own[:REACH])
        other = lax.ppermute(mine, "mlp", [(0, 1), (1, 0)])
    else:
        ends = count - 1
        other = jnp.concatenate(
            [
                lax.ppermute(own[lat - REACH :], "mlp", [(i, i + 1) for i in range(ends)]),
                lax.ppermute(own[:REACH], "mlp", [(i + 1, i) for i in range(ends)]),
            ],
            axis=0,
        )
    even = LON % lax.axis_size("lon") == 0
    both = (own, other)
    first = jnp.concatenate([v[:, :REACH] for v in both], axis=0)
    if even:
        last = jnp.concatenate([v[:, slots - REACH : slots] for v in both], axis=0)
    else:
        last = jnp.concatenate(
            [lax.dynamic_slice_in_dim(v, held - REACH, REACH, 1) for v in both], axis=0
        )
    left = passed_along(last, "lon", 1)
    right = passed_along(first, "lon", -1)
    if not even:
        rows = jnp.concatenate([v[:, :slots] for v in both], axis=0)
        joined = jnp.concatenate([rows, jnp.zeros_like(right)], axis=1)
        joined = lax.dynamic_update_slice_in_dim(joined, right, held, 1)
        own, other, right = joined[:lat, :slots], joined[lat:, :slots], joined[:, slots:]
    return own, other, jnp.concatenate([left, right], axis=1)


def places(lat, held):
    near = jnp.int32(0)
    if lax.axis_size("mlp") == 2:
        near = jnp.where(lax.axis_index("mlp") == 0, lat + REACH, 0).astype(jnp.int32)
        return jnp.stack([near, held.astype(jnp.int32)])
    return jnp.stack([near, held.astype(jnp.int32), jnp.int32(lat + REACH)])


def conv_tile(lat, slots, rows, flip, where_ref, own, other, sides, taps, wide, lane, sink):
    groups = other.shape[0] // REACH
    wide[REACH : REACH + lat, LEAD : LEAD + slots, :] = own[:, :slots, lane].astype(F32)
    ends = sides[:, :, lane].astype(F32)
    wide[REACH : REACH + lat, LEAD - REACH : LEAD, :] = ends[:lat, :REACH]
    wide[REACH : REACH + lat, LEAD + slots : LEAD + slots + REACH, :] = ends[:lat, REACH:]
    for g in range(groups):
        for k in range(REACH):
            at, src = where_ref[2 * g] + k, g * REACH + k
            wide[at, LEAD : LEAD + slots, :] = other[src, :slots, lane].astype(F32)
            wide[at, LEAD - REACH : LEAD, :] = ends[lat + src, :REACH]
            wide[at, LEAD + slots : LEAD + slots + REACH, :] = ends[lat + src, REACH:]

    def step(jt, carry):
        start = jt * 16
        acc = [[jnp.zeros((8, LANES), F32) for _ in range(lat)] for _ in range(2)]
        for b in range(KS):
            used = [a * KS + b for a in range(KS)]
            if flip:
                used = [KS * KS - 1 - t for t in used]
            taken = [taps[t] for t in used]
            for r in rows:
                for half in range(2):
                    cells = wide[r, pl.ds(start + 8 * half + LEAD - REACH + b, 8), :]
                    for i in range(max(0, r - KS + 1), min(lat, r + 1)):
                        acc[half][i] = acc[half][i] + taken[r - i] * cells
        for half in range(2):
            for i in range(lat):
                sink(i, pl.ds(pl.multiple_of(start + 8 * half, 8), 8), acc[half][i])
        return carry

    lax.fori_loop(0, -(-slots // 16), step, 0)


def conv(lat, slots, flip, where_ref, own, other, sides, weight, taps, wide, finish, sink):
    width = own.shape[-1]

    def over(rows):
        def channels(ct, carry):
            lane = pl.ds(pl.multiple_of(ct * LANES, LANES), LANES)
            for a in range(KS):
                row = weight[a, :, lane].astype(F32)
                for b in range(KS):
                    taps[a * KS + b] = jnp.broadcast_to(row[b : b + 1], (8, LANES))
            conv_tile(
                lat, slots, rows, flip, where_ref, own, other, sides, taps, wide, lane,
                functools.partial(sink, lane),
            )
            finish(lane)
            return carry

        lax.fori_loop(0, width // LANES, channels, 0)

    if other.shape[0] == REACH:
        first = where_ref[0] != 0
        pl.when(first)(lambda: over(range(REACH, lat + 2 * REACH)))
        pl.when(jnp.logical_not(first))(lambda: over(range(lat + REACH)))
    else:
        over(range(lat + 2 * REACH))


def forward_kernel(
    lat, slots, where_ref, own, other, sides, weight, gain, normed, hat, inv, taps, wide, mixed
):
    def sink(lane, i, at, value):
        mixed[i, at, lane] = value

    conv(
        lat, slots, False, where_ref, own, other, sides, weight, taps, wide,
        lambda lane: None, sink,
    )
    tile = 32 if mixed.shape[1] % 32 == 0 else 16
    tiles = mixed.shape[1] // tile

    def norm(step, carry):
        i, start = step // tiles, pl.multiple_of(step % tiles * tile, tile)
        at = pl.ds(start, tile)
        values = mixed[i, at, :]
        centred = values - jnp.mean(values, axis=-1, keepdims=True)
        scale = lax.rsqrt(jnp.mean(centred * centred, axis=-1, keepdims=True) + 1e-06)
        live = start + lax.broadcasted_iota(jnp.int32, (tile, 1), 0) < where_ref[1]
        unit = jnp.where(live, centred * scale, 0.0)
        hat[i, at, :] = unit
        normed[i, at, :] = (unit * gain[...]).astype(BF16)
        inv[i, at, :] = jnp.broadcast_to(jnp.where(live, scale, 0.0), (tile, LANES))
        return carry

    lax.fori_loop(0, lat * tiles, norm, 0)


def backward_kernel(
    lat, slots, where_ref, own, other, sides, weight, cot, out, taps, wide, mixed
):
    def sink(lane, i, at, value):
        mixed[i, at, :] = value

    def finish(lane):
        live = lax.broadcasted_iota(jnp.int32, (slots, 1), 0) < where_ref[1]
        for i in range(lat):
            total = cot[i, :, lane].astype(F32) + mixed[i, :slots, :]
            out[i, :, lane] = jnp.where(live, total, 0.0).astype(BF16)

    conv(lat, slots, True, where_ref, own, other, sides, weight, taps, wide, finish, sink)


def kernel_call(kernel, lat, slots, slots_pad, width, outs, mixed, operands):
    vmem = pl.BlockSpec(memory_space=pltpu.VMEM)
    return pl.pallas_call(
        functools.partial(kernel, lat, slots),
        out_shape=outs,
        in_specs=[pl.BlockSpec(memory_space=pltpu.SMEM)] + [vmem] * (len(operands) - 1),
        out_specs=jax.tree.map(lambda _: vmem, outs),
        scratch_shapes=[
            pltpu.VMEM((KS * KS, 8, LANES), F32),
            pltpu.VMEM((lat + 2 * REACH, slots_pad + 16, LANES), F32),
            pltpu.VMEM(mixed, F32),
        ],
        compiler_params=pltpu.CompilerParams(vmem_limit_bytes=12 * 2**20),
        cost_estimate=pl.CostEstimate(flops=2**20, bytes_accessed=2**20, transcendentals=0),
    )(*operands)


def gate(values):
    cumulative = 0.5 * (1.0 + lax.erf(values * (1.0 / math.sqrt(2.0))))
    density = jnp.exp(-0.5 * values * values) * (1.0 / math.sqrt(2.0 * math.pi))
    return cumulative, density


def upper(bit):
    return (lax.axis_index("lon") & bit) // bit


def swapped(value, bit):
    count = lax.axis_size("lon")
    return lax.ppermute(value, "lon", [(i, i ^ bit) for i in range(count)])


def merged(high, own, got):
    rows = own.shape[0]
    out = jnp.zeros((2 * rows, own.shape[1]), own.dtype)
    out = lax.dynamic_update_slice_in_dim(out, own, high * rows, 0)
    return lax.dynamic_update_slice_in_dim(out, got, (1 - high) * rows, 0)


def lon_bits():
    bits, bit = [], 1
    while bit < lax.axis_size("lon"):
        bits.append(bit)
        bit *= 2
    return bits


class State:
    def __init__(self):
        self.held = {}

    def sync(self, *more):
        names = list(self.held)
        tied = lax.optimization_barrier(tuple(self.held.values()) + more)
        self.held = dict(zip(names, tied))
        return tied[len(names) :]


class Pair:
    def __init__(self, state, name, parts, ways):
        self.state, self.names, self.sent = state, (name + "0", name + "1"), None
        self.terms, self.rows = [[], []], 0
        self.keep(parts)
        self.stages = []
        for near, far in ways:
            down = [(g, "down") for g in [near[:1], near[1:], far[:-1]]]
            self.stages.append(down + [(far[-1:], "meet"), (far[-2::-1], "up")])
        self.near = [near for near, _ in ways]

    def keep(self, parts):
        for terms in self.terms:
            for key, _ in terms:
                del self.state.held[key]
        self.terms = [[(name + "t0", 0)] for name in self.names]
        self.state.held.update((terms[0][0], p) for terms, p in zip(self.terms, parts))
        self.rows = parts[0].shape[0]

    def parts(self):
        return [self.state.held[terms[0][0]] for terms in self.terms]

    def rows_of(self, terms, start, rows):
        total = 0.0
        for key, offset in terms:
            rows_here = lax.dynamic_slice_in_dim(self.state.held[key], offset + start, rows, 0)
            total = total + rows_here.astype(F32)
        return total.astype(BF16)

    def outgoing(self, bits, kind):
        if kind == "down":
            half = self.rows // 2
            return [
                self.rows_of(terms, (1 - upper(b)) * half, half)
                for terms, b in zip(self.terms, bits)
            ]
        if kind == "meet":
            self.keep([self.rows_of(terms, 0, self.rows) for terms in self.terms])
        return self.parts()

    def launch(self, bits, kind, sent):
        self.sent = (bits, kind, [swapped(v, b) for v, b in zip(sent, bits)])

    def start(self, bits, kind):
        if kind == "down":
            self.launch(bits, kind, self.state.sync(*self.outgoing(bits, kind)))
        else:
            self.outgoing(bits, kind)
            self.state.sync()
            self.launch(bits, kind, self.parts())

    def close(self):
        bits, kind, got = self.sent
        if kind == "up":
            self.keep([merged(upper(b), p, g) for p, g, b in zip(self.parts(), got, bits)])
        elif kind == "meet":
            both = zip(self.parts(), got)
            self.keep([(p.astype(F32) + g.astype(F32)).astype(BF16) for p, g in both])
        else:
            if kind == "down":
                self.rows //= 2
            for k, (g, b) in enumerate(zip(got, bits)):
                key = self.names[k] + "t" + str(len(self.terms[k]))
                if kind == "down":
                    self.terms[k] = [(old, at + upper(b) * self.rows) for old, at in self.terms[k]]
                self.terms[k] = self.terms[k] + [(key, 0)]
                self.state.held[key] = g

    def cross(self, which, name):
        self.state.sync()
        sent = [self.state.held[tag] for tag in self.tags(name)]
        return [swapped(v, near[which]) for v, near in zip(sent, self.near)]

    def arrive(self, name, values):
        self.state.held.update(zip(self.tags(name), values))

    def tags(self, name):
        return [own + name for own in self.names]

    def place(self, out, values, other0, other1):
        for k, (v, (bit0, bit1)) in enumerate(zip(values, self.near)):
            block = 4 * k + 2 * (upper(bit0) ^ other0) + (upper(bit1) ^ other1)
            out = lax.dynamic_update_slice_in_dim(out, v, block * self.rows, 0)
        return out

    def spread(self):
        own = self.parts()
        out = jnp.zeros((4 * len(own) * self.rows, own[0].shape[1]), BF16)
        return self.place(out, own, 0, 0)

    def get(self, name):
        return [self.state.held[tag] for tag in self.tags(name)]

    def next_stage(self):
        groups = [stages.pop(0) for stages in self.stages]
        return list(zip(*(bits for bits, _ in groups))), groups[0][1]

    def open(self):
        steps, kind = self.next_stage()
        for bits in steps[:-1]:
            self.start(bits, kind)
            self.close()
        self.start(steps[-1], kind)

    def advance(self):
        self.close()
        self.open()

    def quarter(self, k, other0, other1):
        bit0, bit1 = self.near[k]
        block = 2 * (upper(bit0) ^ other0) + (upper(bit1) ^ other1)
        return block * (self.rows // 4)

    def prepare(self):
        self.next_stage()
        self.next_stage()
        whole, size = self.parts(), self.rows // 4
        for piece, other1 in (("r0", 1), ("r1", 0)):
            cuts = [
                lax.dynamic_slice_in_dim(v, self.quarter(k, 1, other1), size, 0)
                for k, v in enumerate(whole)
            ]
            self.arrive(piece, cuts)
        self.piece, self.going = -1, ([near[0] for near in self.near], "down")

    def sum_first(self):
        size, sent = self.rows // 4, []
        for k, (v, g) in enumerate(zip(self.parts(), self.get("g0"))):
            rows = lax.dynamic_slice_in_dim(v, self.quarter(k, 0, 1), size, 0)
            sent.append((rows.astype(F32) + g.astype(F32)).astype(BF16))
        self.arrive("s", sent)

    def forward(self):
        self.arrived()
        size = self.rows // 4
        for k, tag in enumerate(self.tags("g1")):
            self.terms[k] = [(self.terms[k][0][0], self.quarter(k, 0, 0)), (tag, 0)]
        for tag in self.tags("g0"):
            del self.state.held[tag]
        self.rows = size
        bits = [near[1] for near in self.near]
        sent = [self.state.held.pop(tag) for tag in self.tags("s")]
        self.launch(bits, "kept", self.state.sync(*sent))

    def next_piece(self):
        self.piece += 1
        self.state.sync()
        sent = [self.state.held.pop(tag) for tag in self.tags("r" + str(self.piece))]
        self.launch(*self.going, sent)

    def arrived(self):
        self.arrive("g" + str(self.piece), self.sent[2])


def both_ways():
    bits = lon_bits()
    fast, slow = bits[:2], bits[2:]
    return (fast, slow), (fast[::-1], slow[::-1])


def all_rows(own):
    if lax.axis_size("mlp") == 2:
        return jnp.concatenate([own, lax.ppermute(own, "mlp", [(0, 1), (1, 0)])], axis=0)
    return lax.all_gather(own, "mlp", axis=0, tiled=True)


def own_rows_sum(partial):
    if lax.axis_size("mlp") == 2:
        rows = partial.shape[0] // 2
        theirs = lax.ppermute(partial[rows:], "mlp", [(0, 1), (1, 0)])
        return partial[:rows].astype(F32) + theirs.astype(F32)
    return lax.psum_scatter(partial, "mlp", scatter_dimension=0, tiled=True).astype(F32)


def across_rows(left, right):
    return lax.dot_general(left, right, (((0,), (0,)), ((), ())), preferred_element_type=F32)


def across_width(left, right):
    return lax.dot_general(left, right, (((1,), (1,)), ((), ())), preferred_element_type=F32)


def body(fields, cotangent, conv_weight, norm_gain, weight_in, weight_out):
    lat, slots, width = fields.shape
    slots_pad = -(-slots // 16) * 16
    held = live_count()
    slot_live = lax.broadcasted_iota(jnp.int32, (1, slots, 1), 1) < held
    spare = ((0, 0), (0, slots_pad - slots), (0, 0))
    where = places(lat, held)
    gain = norm_gain.astype(F32).reshape(1, width)
    cot_all = all_rows(jnp.pad(jnp.where(slot_live, cotangent, 0), spare).reshape(-1, width))

    grid = (lat, slots_pad, width)
    normed, hat, inv = kernel_call(
        forward_kernel, lat, slots, slots_pad, width,
        (
            jax.ShapeDtypeStruct(grid, BF16),
            jax.ShapeDtypeStruct(grid, F32),
            jax.ShapeDtypeStruct((lat, slots_pad, LANES), F32),
        ),
        grid,
        (where,) + halo(fields, slots, held) + (conv_weight, gain),
    )
    normed_all = all_rows(normed.reshape(-1, width))

    cells = lax.axis_size("mlp") * lat * LON
    factor = jnp.float32(1.0 / math.sqrt(cells))
    state = State()
    ways = both_ways()

    def pair(name, grad):
        half = grad.shape[0] // 2
        return Pair(state, name, (grad[:half], grad[half:]), ways)

    hidden = jnp.dot(normed_all, weight_in, preferred_element_type=F32)
    cumulative, density = gate(hidden)
    activated = (hidden * cumulative).astype(BF16)
    state.held["cot"] = cot_all
    a = pair("a", (across_rows(activated, cot_all) * factor).astype(BF16))
    a.open()
    upstream = across_width(state.held.pop("cot"), weight_out)
    grad_hidden = (upstream * (cumulative + hidden * density)).astype(BF16)
    partial = across_width(grad_hidden, weight_in).astype(BF16)
    grad_normed = own_rows_sum(partial)
    state.held["hidden"] = grad_hidden
    state.held["partial"] = partial
    a.advance()
    grad_first = across_rows(normed_all, state.held.pop("hidden")) * factor
    b = pair("b", grad_first.astype(BF16))
    state.held["gain"] = gain
    state.held["inv"] = inv
    state.held["back"] = grad_normed
    a.advance()
    b.prepare()
    b.next_piece()

    scaled = state.held.pop("back").reshape(grid) * state.held.pop("gain")
    inv = state.held.pop("inv")[:, :, :1]
    grad_mixed = inv * (
        scaled
        - jnp.mean(scaled, axis=-1, keepdims=True)
        - hat * jnp.mean(scaled * hat, axis=-1, keepdims=True)
    )
    del state.held["partial"]
    b.arrived()
    a.advance()
    b.next_piece()
    state.held["mixed"] = grad_mixed.astype(BF16)
    b.sum_first()
    b.arrived()
    a.advance()
    b.forward()
    a.close()
    from_near = a.cross(1, "t0")
    b.advance()
    own, other, sides = halo(state.held.pop("mixed"), slots, held)

    b.advance()
    a.arrive("n", from_near)
    from_far = a.cross(0, "t0")
    a.arrive("f", from_far)
    b.advance()
    from_both = a.cross(0, "n")
    a.arrive("b", from_both)
    b.close()
    from_near = b.cross(1, "t0")
    from_far = b.cross(0, "t0")
    state.held["sides"] = sides
    state.sync()
    state.held["result"] = kernel_call(
        backward_kernel, lat, slots, slots_pad, width,
        jax.ShapeDtypeStruct((lat, slots, width), BF16),
        (lat, slots_pad, LANES),
        (where, own, other, state.held["sides"], conv_weight, cotangent),
    )
    state.held["out"] = b.spread()
    out_second = a.place(a.place(a.spread(), a.get("n"), 0, 1), a.get("f"), 1, 0)
    state.held["second"] = a.place(out_second, a.get("b"), 1, 1)
    b.arrive("n", from_near)
    b.arrive("f", from_far)
    from_both = b.cross(0, "n")
    out_first = b.place(b.place(state.held["out"], b.get("n"), 0, 1), b.get("f"), 1, 0)
    out_first = b.place(out_first, from_both, 1, 1)
    return (state.held["result"], out_first, state.held["second"])


def solution(mesh):
    in_specs = (
        P("mlp", "lon", None),
        P("mlp", "lon", None),
        P(),
        P(),
        P(None, "mlp"),
        P("mlp", None),
    )
    out_specs = (P("mlp", "lon", None), P(None, "mlp"), P("mlp", None))
    return jax.shard_map(body, mesh=mesh, in_specs=in_specs, out_specs=out_specs, check_vma=False)
```

```python
import functools
import math

import jax
import jax.numpy as jnp
from jax import lax
from jax.experimental import pallas as pl
from jax.experimental.pallas import tpu as pltpu
from jax.sharding import PartitionSpec as P

KS = 7
LON = 1440
REACH = KS // 2
LANES = 128
BF16 = jnp.bfloat16
F32 = jnp.float32
LEAD = 8


def passed_along(value, axis, by):
    count = lax.axis_size(axis)
    return lax.ppermute(value, axis, [(i, (i + by) % count) for i in range(count)])


def live_count():
    members = lax.axis_size("lon")
    position = lax.axis_index("lon")
    return LON // members + (position < LON % members).astype(jnp.int32)


def halo(own, slots, held):
    lat, count = own.shape[0], lax.axis_size("mlp")
    if count == 2:
        mine = jnp.where(lax.axis_index("mlp") == 0, own[lat - REACH :], own[:REACH])
        other = lax.ppermute(mine, "mlp", [(0, 1), (1, 0)])
    else:
        ends = count - 1
        other = jnp.concatenate(
            [
                lax.ppermute(own[lat - REACH :], "mlp", [(i, i + 1) for i in range(ends)]),
                lax.ppermute(own[:REACH], "mlp", [(i + 1, i) for i in range(ends)]),
            ],
            axis=0,
        )
    even = LON % lax.axis_size("lon") == 0
    both = (own, other)
    first = jnp.concatenate([v[:, :REACH] for v in both], axis=0)
    if even:
        last = jnp.concatenate([v[:, slots - REACH : slots] for v in both], axis=0)
    else:
        last = jnp.concatenate(
            [lax.dynamic_slice_in_dim(v, held - REACH, REACH, 1) for v in both], axis=0
        )
    left = passed_along(last, "lon", 1)
    right = passed_along(first, "lon", -1)
    if not even:
        rows = jnp.concatenate([v[:, :slots] for v in both], axis=0)
        joined = jnp.concatenate([rows, jnp.zeros_like(right)], axis=1)
        joined = lax.dynamic_update_slice_in_dim(joined, right, held, 1)
        own, other, right = joined[:lat, :slots], joined[lat:, :slots], joined[:, slots:]
    return own, other, jnp.concatenate([left, right], axis=1)


def places(lat, held):
    near = jnp.int32(0)
    if lax.axis_size("mlp") == 2:
        near = jnp.where(lax.axis_index("mlp") == 0, lat + REACH, 0).astype(jnp.int32)
        return jnp.stack([near, held.astype(jnp.int32)])
    return jnp.stack([near, held.astype(jnp.int32), jnp.int32(lat + REACH)])


def conv_tile(lat, slots, rows, flip, where_ref, own, other, sides, taps, wide, lane, sink):
    groups = other.shape[0] // REACH
    wide[REACH : REACH + lat, LEAD : LEAD + slots, :] = own[:, :slots, lane].astype(F32)
    ends = sides[:, :, lane].astype(F32)
    wide[REACH : REACH + lat, LEAD - REACH : LEAD, :] = ends[:lat, :REACH]
    wide[REACH : REACH + lat, LEAD + slots : LEAD + slots + REACH, :] = ends[:lat, REACH:]
    for g in range(groups):
        for k in range(REACH):
            at, src = where_ref[2 * g] + k, g * REACH + k
            wide[at, LEAD : LEAD + slots, :] = other[src, :slots, lane].astype(F32)
            wide[at, LEAD - REACH : LEAD, :] = ends[lat + src, :REACH]
            wide[at, LEAD + slots : LEAD + slots + REACH, :] = ends[lat + src, REACH:]

    def step(jt, carry):
        start = jt * 16
        acc = [[jnp.zeros((8, LANES), F32) for _ in range(lat)] for _ in range(2)]
        for b in range(KS):
            used = [a * KS + b for a in range(KS)]
            if flip:
                used = [KS * KS - 1 - t for t in used]
            taken = [taps[t] for t in used]
            for r in rows:
                for half in range(2):
                    cells = wide[r, pl.ds(start + 8 * half + LEAD - REACH + b, 8), :]
                    for i in range(max(0, r - KS + 1), min(lat, r + 1)):
                        acc[half][i] = acc[half][i] + taken[r - i] * cells
        for half in range(2):
            for i in range(lat):
                sink(i, pl.ds(pl.multiple_of(start + 8 * half, 8), 8), acc[half][i])
        return carry

    lax.fori_loop(0, -(-slots // 16), step, 0)


def conv(lat, slots, flip, where_ref, own, other, sides, weight, taps, wide, finish, sink):
    width = own.shape[-1]

    def over(rows):
        def channels(ct, carry):
            lane = pl.ds(pl.multiple_of(ct * LANES, LANES), LANES)
            for a in range(KS):
                row = weight[a, :, lane].astype(F32)
                for b in range(KS):
                    taps[a * KS + b] = jnp.broadcast_to(row[b : b + 1], (8, LANES))
            conv_tile(
                lat, slots, rows, flip, where_ref, own, other, sides, taps, wide, lane,
                functools.partial(sink, lane),
            )
            finish(lane)
            return carry

        lax.fori_loop(0, width // LANES, channels, 0)

    if other.shape[0] == REACH:
        first = where_ref[0] != 0
        pl.when(first)(lambda: over(range(REACH, lat + 2 * REACH)))
        pl.when(jnp.logical_not(first))(lambda: over(range(lat + REACH)))
    else:
        over(range(lat + 2 * REACH))


def forward_kernel(
    lat, slots, where_ref, own, other, sides, weight, gain, normed, hat, inv, taps, wide, mixed
):
    def sink(lane, i, at, value):
        mixed[i, at, lane] = value

    conv(
        lat, slots, False, where_ref, own, other, sides, weight, taps, wide,
        lambda lane: None, sink,
    )
    tile = 32 if mixed.shape[1] % 32 == 0 else 16
    tiles = mixed.shape[1] // tile

    def norm(step, carry):
        i, start = step // tiles, pl.multiple_of(step % tiles * tile, tile)
        at = pl.ds(start, tile)
        values = mixed[i, at, :]
        centred = values - jnp.mean(values, axis=-1, keepdims=True)
        scale = lax.rsqrt(jnp.mean(centred * centred, axis=-1, keepdims=True) + 1e-06)
        live = start + lax.broadcasted_iota(jnp.int32, (tile, 1), 0) < where_ref[1]
        unit = jnp.where(live, centred * scale, 0.0)
        hat[i, at, :] = unit
        normed[i, at, :] = (unit * gain[...]).astype(BF16)
        inv[i, at, :] = jnp.broadcast_to(jnp.where(live, scale, 0.0), (tile, LANES))
        return carry

    lax.fori_loop(0, lat * tiles, norm, 0)


def backward_kernel(
    lat, slots, where_ref, own, other, sides, weight, cot, out, taps, wide, mixed
):
    def sink(lane, i, at, value):
        mixed[i, at, :] = value

    def finish(lane):
        live = lax.broadcasted_iota(jnp.int32, (slots, 1), 0) < where_ref[1]
        for i in range(lat):
            total = cot[i, :, lane].astype(F32) + mixed[i, :slots, :]
            out[i, :, lane] = jnp.where(live, total, 0.0).astype(BF16)

    conv(lat, slots, True, where_ref, own, other, sides, weight, taps, wide, finish, sink)


def kernel_call(kernel, lat, slots, slots_pad, width, outs, mixed, operands):
    vmem = pl.BlockSpec(memory_space=pltpu.VMEM)
    return pl.pallas_call(
        functools.partial(kernel, lat, slots),
        out_shape=outs,
        in_specs=[pl.BlockSpec(memory_space=pltpu.SMEM)] + [vmem] * (len(operands) - 1),
        out_specs=jax.tree.map(lambda _: vmem, outs),
        scratch_shapes=[
            pltpu.VMEM((KS * KS, 8, LANES), F32),
            pltpu.VMEM((lat + 2 * REACH, slots_pad + 16, LANES), F32),
            pltpu.VMEM(mixed, F32),
        ],
        compiler_params=pltpu.CompilerParams(vmem_limit_bytes=12 * 2**20),
        cost_estimate=pl.CostEstimate(flops=2**20, bytes_accessed=2**20, transcendentals=0),
    )(*operands)


def expand_kernel(factor, own, other, cot_own, cot_other, weight, hidden, grad):
    rows = own.shape[0]
    total = jnp.zeros(grad.shape, F32)
    for at, cells, cot in ((0, own, cot_own), (rows, other, cot_other)):
        values = jnp.dot(cells[...], weight[...], preferred_element_type=F32)
        hidden[at : at + rows, :] = values
        activated = values * (0.5 * (1.0 + lax.erf(values * (1.0 / math.sqrt(2.0)))))
        total = total + across_rows(activated.astype(BF16), cot[...])
    grad[...] = (total * factor).astype(BF16)


def expand(normed, cot, weight, factor):
    (rows, width), units = normed[0].shape, weight.shape[1]
    block = min(units, 256)
    whole = pl.BlockSpec((rows, width), lambda i: (0, 0))
    return pl.pallas_call(
        functools.partial(expand_kernel, factor),
        grid=(units // block,),
        in_specs=[whole] * 4 + [pl.BlockSpec((width, block), lambda i: (0, i))],
        out_specs=(
            pl.BlockSpec((2 * rows, block), lambda i: (0, i)),
            pl.BlockSpec((block, width), lambda i: (i, 0)),
        ),
        out_shape=(
            jax.ShapeDtypeStruct((2 * rows, units), F32),
            jax.ShapeDtypeStruct((units, width), BF16),
        ),
        compiler_params=pltpu.CompilerParams(vmem_limit_bytes=32 * 2**20),
        cost_estimate=pl.CostEstimate(
            flops=8 * rows * width * units, bytes_accessed=24 * 2**20, transcendentals=0
        ),
    )(*normed, *cot, weight)


def gate(values):
    cumulative = 0.5 * (1.0 + lax.erf(values * (1.0 / math.sqrt(2.0))))
    density = jnp.exp(-0.5 * values * values) * (1.0 / math.sqrt(2.0 * math.pi))
    return cumulative, density


def upper(bit):
    return (lax.axis_index("lon") & bit) // bit


def swapped(value, bit):
    count = lax.axis_size("lon")
    return lax.ppermute(value, "lon", [(i, i ^ bit) for i in range(count)])


def merged(high, own, got):
    rows = own.shape[0]
    out = jnp.zeros((2 * rows, own.shape[1]), own.dtype)
    out = lax.dynamic_update_slice_in_dim(out, own, high * rows, 0)
    return lax.dynamic_update_slice_in_dim(out, got, (1 - high) * rows, 0)


def lon_bits():
    bits, bit = [], 1
    while bit < lax.axis_size("lon"):
        bits.append(bit)
        bit *= 2
    return bits


class State:
    def __init__(self):
        self.held = {}

    def sync(self, *more):
        names = list(self.held)
        tied = lax.optimization_barrier(tuple(self.held.values()) + more)
        self.held = dict(zip(names, tied))
        return tied[len(names) :]


class Pair:
    def __init__(self, state, name, parts, ways):
        self.state, self.names, self.sent = state, (name + "0", name + "1"), None
        self.terms, self.rows = [[], []], 0
        self.keep(parts)
        self.stages = []
        for near, far in ways:
            down = [(g, "down") for g in [near[:1], near[1:], far[:-1]]]
            self.stages.append(down + [(far[-1:], "meet"), (far[-2::-1], "up")])
        self.near = [near for near, _ in ways]

    def keep(self, parts):
        for terms in self.terms:
            for key, _ in terms:
                del self.state.held[key]
        self.terms = [[(name + "t0", 0)] for name in self.names]
        self.state.held.update((terms[0][0], p) for terms, p in zip(self.terms, parts))
        self.rows = parts[0].shape[0]

    def parts(self):
        return [self.state.held[terms[0][0]] for terms in self.terms]

    def rows_of(self, terms, start, rows):
        total = 0.0
        for key, offset in terms:
            rows_here = lax.dynamic_slice_in_dim(self.state.held[key], offset + start, rows, 0)
            total = total + rows_here.astype(F32)
        return total.astype(BF16)

    def outgoing(self, bits, kind):
        if kind == "down":
            half = self.rows // 2
            return [
                self.rows_of(terms, (1 - upper(b)) * half, half)
                for terms, b in zip(self.terms, bits)
            ]
        if kind == "meet":
            self.keep([self.rows_of(terms, 0, self.rows) for terms in self.terms])
        return self.parts()

    def launch(self, bits, kind, sent):
        self.sent = (bits, kind, [swapped(v, b) for v, b in zip(sent, bits)])

    def start(self, bits, kind):
        if kind == "down":
            self.launch(bits, kind, self.state.sync(*self.outgoing(bits, kind)))
        else:
            self.outgoing(bits, kind)
            self.state.sync()
            self.launch(bits, kind, self.parts())

    def close(self):
        bits, kind, got = self.sent
        if kind == "up":
            self.keep([merged(upper(b), p, g) for p, g, b in zip(self.parts(), got, bits)])
        elif kind == "meet":
            both = zip(self.parts(), got)
            self.keep([(p.astype(F32) + g.astype(F32)).astype(BF16) for p, g in both])
        else:
            if kind == "down":
                self.rows //= 2
            for k, (g, b) in enumerate(zip(got, bits)):
                key = self.names[k] + "t" + str(len(self.terms[k]))
                if kind == "down":
                    self.terms[k] = [(old, at + upper(b) * self.rows) for old, at in self.terms[k]]
                self.terms[k] = self.terms[k] + [(key, 0)]
                self.state.held[key] = g

    def cross(self, which, name):
        self.state.sync()
        sent = [self.state.held[tag] for tag in self.tags(name)]
        return [swapped(v, near[which]) for v, near in zip(sent, self.near)]

    def arrive(self, name, values):
        self.state.held.update(zip(self.tags(name), values))

    def tags(self, name):
        return [own + name for own in self.names]

    def place(self, out, values, other0, other1):
        for k, (v, (bit0, bit1)) in enumerate(zip(values, self.near)):
            block = 4 * k + 2 * (upper(bit0) ^ other0) + (upper(bit1) ^ other1)
            out = lax.dynamic_update_slice_in_dim(out, v, block * self.rows, 0)
        return out

    def spread(self):
        own = self.parts()
        out = jnp.zeros((4 * len(own) * self.rows, own[0].shape[1]), BF16)
        return self.place(out, own, 0, 0)

    def get(self, name):
        return [self.state.held[tag] for tag in self.tags(name)]

    def next_stage(self):
        groups = [stages.pop(0) for stages in self.stages]
        return list(zip(*(bits for bits, _ in groups))), groups[0][1]

    def open(self):
        steps, kind = self.next_stage()
        for bits in steps[:-1]:
            self.start(bits, kind)
            self.close()
        self.start(steps[-1], kind)

    def advance(self):
        self.close()
        self.open()

    def quarter(self, k, other0, other1):
        bit0, bit1 = self.near[k]
        block = 2 * (upper(bit0) ^ other0) + (upper(bit1) ^ other1)
        return block * (self.rows // 4)

    def prepare(self):
        self.next_stage()
        self.next_stage()
        whole, size = self.parts(), self.rows // 4
        for piece, other1 in (("r0", 1), ("r1", 0)):
            cuts = [
                lax.dynamic_slice_in_dim(v, self.quarter(k, 1, other1), size, 0)
                for k, v in enumerate(whole)
            ]
            self.arrive(piece, cuts)
        self.piece, self.going = -1, ([near[0] for near in self.near], "down")

    def sum_first(self):
        size, sent = self.rows // 4, []
        for k, (v, g) in enumerate(zip(self.parts(), self.get("g0"))):
            rows = lax.dynamic_slice_in_dim(v, self.quarter(k, 0, 1), size, 0)
            sent.append((rows.astype(F32) + g.astype(F32)).astype(BF16))
        self.arrive("s", sent)

    def forward(self):
        self.arrived()
        size = self.rows // 4
        for k, tag in enumerate(self.tags("g1")):
            self.terms[k] = [(self.terms[k][0][0], self.quarter(k, 0, 0)), (tag, 0)]
        for tag in self.tags("g0"):
            del self.state.held[tag]
        self.rows = size
        bits = [near[1] for near in self.near]
        sent = [self.state.held.pop(tag) for tag in self.tags("s")]
        self.launch(bits, "kept", self.state.sync(*sent))

    def next_piece(self):
        self.piece += 1
        self.state.sync()
        sent = [self.state.held.pop(tag) for tag in self.tags("r" + str(self.piece))]
        self.launch(*self.going, sent)

    def arrived(self):
        self.arrive("g" + str(self.piece), self.sent[2])


def both_ways():
    bits = lon_bits()
    fast, slow = bits[:2], bits[2:]
    return (fast, slow), (fast[::-1], slow[::-1])


def all_rows(own):
    if lax.axis_size("mlp") == 2:
        return jnp.concatenate([own, lax.ppermute(own, "mlp", [(0, 1), (1, 0)])], axis=0)
    return lax.all_gather(own, "mlp", axis=0, tiled=True)


def own_rows_sum(partial):
    if lax.axis_size("mlp") == 2:
        rows = partial.shape[0] // 2
        theirs = lax.ppermute(partial[rows:], "mlp", [(0, 1), (1, 0)])
        return partial[:rows].astype(F32) + theirs.astype(F32)
    return lax.psum_scatter(partial, "mlp", scatter_dimension=0, tiled=True).astype(F32)


def across_rows(left, right):
    return lax.dot_general(left, right, (((0,), (0,)), ((), ())), preferred_element_type=F32)


def across_width(left, right):
    return lax.dot_general(left, right, (((1,), (1,)), ((), ())), preferred_element_type=F32)


def body(fields, cotangent, conv_weight, norm_gain, weight_in, weight_out):
    lat, slots, width = fields.shape
    slots_pad = -(-slots // 16) * 16
    held = live_count()
    slot_live = lax.broadcasted_iota(jnp.int32, (1, slots, 1), 1) < held
    spare = ((0, 0), (0, slots_pad - slots), (0, 0))
    where = places(lat, held)
    gain = norm_gain.astype(F32).reshape(1, width)
    cot_all = all_rows(jnp.pad(jnp.where(slot_live, cotangent, 0), spare).reshape(-1, width))

    grid = (lat, slots_pad, width)
    normed, hat, inv = kernel_call(
        forward_kernel, lat, slots, slots_pad, width,
        (
            jax.ShapeDtypeStruct(grid, BF16),
            jax.ShapeDtypeStruct(grid, F32),
            jax.ShapeDtypeStruct((lat, slots_pad, LANES), F32),
        ),
        grid,
        (where,) + halo(fields, slots, held) + (conv_weight, gain),
    )
    normed_all = all_rows(normed.reshape(-1, width))

    cells = lax.axis_size("mlp") * lat * LON
    factor = jnp.float32(1.0 / math.sqrt(cells))
    state = State()
    ways = both_ways()

    def pair(name, grad):
        half = grad.shape[0] // 2
        return Pair(state, name, (grad[:half], grad[half:]), ways)

    rows = normed_all.shape[0] // 2
    hidden, grad_second = expand(
        (normed_all[:rows], normed_all[rows:]), (cot_all[:rows], cot_all[rows:]), weight_in,
        1.0 / math.sqrt(cells),
    )
    cumulative, density = gate(hidden)
    state.held["cot"] = cot_all
    a = pair("a", grad_second)
    a.open()
    upstream = across_width(state.held.pop("cot"), weight_out)
    grad_hidden = (upstream * (cumulative + hidden * density)).astype(BF16)
    partial = across_width(grad_hidden, weight_in).astype(BF16)
    grad_normed = own_rows_sum(partial)
    state.held["hidden"] = grad_hidden
    state.held["partial"] = partial
    a.advance()
    grad_first = across_rows(normed_all, state.held.pop("hidden")) * factor
    b = pair("b", grad_first.astype(BF16))
    state.held["gain"] = gain
    state.held["inv"] = inv
    state.held["back"] = grad_normed
    a.advance()
    b.prepare()
    b.next_piece()

    scaled = state.held.pop("back").reshape(grid) * state.held.pop("gain")
    inv = state.held.pop("inv")[:, :, :1]
    grad_mixed = inv * (
        scaled
        - jnp.mean(scaled, axis=-1, keepdims=True)
        - hat * jnp.mean(scaled * hat, axis=-1, keepdims=True)
    )
    del state.held["partial"]
    b.arrived()
    a.advance()
    b.next_piece()
    state.held["mixed"] = grad_mixed.astype(BF16)
    b.sum_first()
    b.arrived()
    a.advance()
    b.forward()
    a.close()
    from_near = a.cross(1, "t0")
    b.advance()
    own, other, sides = halo(state.held.pop("mixed"), slots, held)

    b.advance()
    a.arrive("n", from_near)
    from_far = a.cross(0, "t0")
    a.arrive("f", from_far)
    b.advance()
    from_both = a.cross(0, "n")
    a.arrive("b", from_both)
    b.close()
    from_near = b.cross(1, "t0")
    from_far = b.cross(0, "t0")
    state.held["sides"] = sides
    state.sync()
    state.held["result"] = kernel_call(
        backward_kernel, lat, slots, slots_pad, width,
        jax.ShapeDtypeStruct((lat, slots, width), BF16),
        (lat, slots_pad, LANES),
        (where, own, other, state.held["sides"], conv_weight, cotangent),
    )
    state.held["out"] = b.spread()
    out_second = a.place(a.place(a.spread(), a.get("n"), 0, 1), a.get("f"), 1, 0)
    state.held["second"] = a.place(out_second, a.get("b"), 1, 1)
    b.arrive("n", from_near)
    b.arrive("f", from_far)
    from_both = b.cross(0, "n")
    out_first = b.place(b.place(state.held["out"], b.get("n"), 0, 1), b.get("f"), 1, 0)
    out_first = b.place(out_first, from_both, 1, 1)
    return (state.held["result"], out_first, state.held["second"])


def solution(mesh):
    in_specs = (
        P("mlp", "lon", None),
        P("mlp", "lon", None),
        P(),
        P(),
        P(None, "mlp"),
        P("mlp", None),
    )
    out_specs = (P("mlp", "lon", None), P(None, "mlp"), P("mlp", None))
    return jax.shard_map(body, mesh=mesh, in_specs=in_specs, out_specs=out_specs, check_vma=False)
```

```python
import functools
import math

import jax
import jax.numpy as jnp
from jax import lax
from jax.experimental import pallas as pl
from jax.experimental.pallas import tpu as pltpu
from jax.sharding import PartitionSpec as P

KS = 7
LON = 1440
REACH = KS // 2
LANES = 128
BF16 = jnp.bfloat16
F32 = jnp.float32
LEAD = 8


def passed_along(value, axis, by):
    count = lax.axis_size(axis)
    return lax.ppermute(value, axis, [(i, (i + by) % count) for i in range(count)])


def live_count():
    members = lax.axis_size("lon")
    position = lax.axis_index("lon")
    return LON // members + (position < LON % members).astype(jnp.int32)


def halo(own, slots, held):
    lat, count = own.shape[0], lax.axis_size("mlp")
    if count == 2:
        mine = jnp.where(lax.axis_index("mlp") == 0, own[lat - REACH :], own[:REACH])
        other = lax.ppermute(mine, "mlp", [(0, 1), (1, 0)])
    else:
        ends = count - 1
        other = jnp.concatenate(
            [
                lax.ppermute(own[lat - REACH :], "mlp", [(i, i + 1) for i in range(ends)]),
                lax.ppermute(own[:REACH], "mlp", [(i + 1, i) for i in range(ends)]),
            ],
            axis=0,
        )
    even = LON % lax.axis_size("lon") == 0
    both = (own, other)
    first = jnp.concatenate([v[:, :REACH] for v in both], axis=0)
    if even:
        last = jnp.concatenate([v[:, slots - REACH : slots] for v in both], axis=0)
    else:
        last = jnp.concatenate(
            [lax.dynamic_slice_in_dim(v, held - REACH, REACH, 1) for v in both], axis=0
        )
    left = passed_along(last, "lon", 1)
    right = passed_along(first, "lon", -1)
    if not even:
        rows = jnp.concatenate([v[:, :slots] for v in both], axis=0)
        joined = jnp.concatenate([rows, jnp.zeros_like(right)], axis=1)
        joined = lax.dynamic_update_slice_in_dim(joined, right, held, 1)
        own, other, right = joined[:lat, :slots], joined[lat:, :slots], joined[:, slots:]
    return own, other, jnp.concatenate([left, right], axis=1)


def places(lat, held):
    near = jnp.int32(0)
    if lax.axis_size("mlp") == 2:
        near = jnp.where(lax.axis_index("mlp") == 0, lat + REACH, 0).astype(jnp.int32)
        return jnp.stack([near, held.astype(jnp.int32)])
    return jnp.stack([near, held.astype(jnp.int32), jnp.int32(lat + REACH)])


def conv_tile(lat, slots, rows, flip, where_ref, own, other, sides, taps, wide, lane, sink):
    groups = other.shape[0] // REACH
    wide[REACH : REACH + lat, LEAD : LEAD + slots, :] = own[:, :slots, lane].astype(F32)
    ends = sides[:, :, lane].astype(F32)
    wide[REACH : REACH + lat, LEAD - REACH : LEAD, :] = ends[:lat, :REACH]
    wide[REACH : REACH + lat, LEAD + slots : LEAD + slots + REACH, :] = ends[:lat, REACH:]
    for g in range(groups):
        for k in range(REACH):
            at, src = where_ref[2 * g] + k, g * REACH + k
            wide[at, LEAD : LEAD + slots, :] = other[src, :slots, lane].astype(F32)
            wide[at, LEAD - REACH : LEAD, :] = ends[lat + src, :REACH]
            wide[at, LEAD + slots : LEAD + slots + REACH, :] = ends[lat + src, REACH:]

    def step(jt, carry):
        start = jt * 16
        acc = [[jnp.zeros((8, LANES), F32) for _ in range(lat)] for _ in range(2)]
        for b in range(KS):
            used = [a * KS + b for a in range(KS)]
            if flip:
                used = [KS * KS - 1 - t for t in used]
            taken = [taps[t] for t in used]
            for r in rows:
                for half in range(2):
                    cells = wide[r, pl.ds(start + 8 * half + LEAD - REACH + b, 8), :]
                    for i in range(max(0, r - KS + 1), min(lat, r + 1)):
                        acc[half][i] = acc[half][i] + taken[r - i] * cells
        for half in range(2):
            for i in range(lat):
                sink(i, pl.ds(pl.multiple_of(start + 8 * half, 8), 8), acc[half][i])
        return carry

    lax.fori_loop(0, -(-slots // 16), step, 0)


def conv(lat, slots, flip, where_ref, own, other, sides, weight, taps, wide, finish, sink):
    width = own.shape[-1]

    def over(rows):
        def channels(ct, carry):
            lane = pl.ds(pl.multiple_of(ct * LANES, LANES), LANES)
            for a in range(KS):
                row = weight[a, :, lane].astype(F32)
                for b in range(KS):
                    taps[a * KS + b] = jnp.broadcast_to(row[b : b + 1], (8, LANES))
            conv_tile(
                lat, slots, rows, flip, where_ref, own, other, sides, taps, wide, lane,
                functools.partial(sink, lane),
            )
            finish(lane)
            return carry

        lax.fori_loop(0, width // LANES, channels, 0)

    if other.shape[0] == REACH:
        first = where_ref[0] != 0
        pl.when(first)(lambda: over(range(REACH, lat + 2 * REACH)))
        pl.when(jnp.logical_not(first))(lambda: over(range(lat + REACH)))
    else:
        over(range(lat + 2 * REACH))


def forward_kernel(
    lat, slots, where_ref, own, other, sides, weight, gain, normed, hat, inv, taps, wide, mixed
):
    def sink(lane, i, at, value):
        mixed[i, at, lane] = value

    conv(
        lat, slots, False, where_ref, own, other, sides, weight, taps, wide,
        lambda lane: None, sink,
    )
    tile = 32 if mixed.shape[1] % 32 == 0 else 16
    tiles = mixed.shape[1] // tile

    def norm(step, carry):
        i, start = step // tiles, pl.multiple_of(step % tiles * tile, tile)
        at = pl.ds(start, tile)
        values = mixed[i, at, :]
        centred = values - jnp.mean(values, axis=-1, keepdims=True)
        scale = lax.rsqrt(jnp.mean(centred * centred, axis=-1, keepdims=True) + 1e-06)
        live = start + lax.broadcasted_iota(jnp.int32, (tile, 1), 0) < where_ref[1]
        unit = jnp.where(live, centred * scale, 0.0)
        hat[i, at, :] = unit
        normed[i, at, :] = (unit * gain[...]).astype(BF16)
        inv[i, at, :] = jnp.broadcast_to(jnp.where(live, scale, 0.0), (tile, LANES))
        return carry

    lax.fori_loop(0, lat * tiles, norm, 0)


def backward_kernel(
    lat, slots, where_ref, own, other, sides, weight, cot, out, taps, wide, mixed
):
    def sink(lane, i, at, value):
        mixed[i, at, :] = value

    def finish(lane):
        live = lax.broadcasted_iota(jnp.int32, (slots, 1), 0) < where_ref[1]
        for i in range(lat):
            total = cot[i, :, lane].astype(F32) + mixed[i, :slots, :]
            out[i, :, lane] = jnp.where(live, total, 0.0).astype(BF16)

    conv(lat, slots, True, where_ref, own, other, sides, weight, taps, wide, finish, sink)


def kernel_call(kernel, lat, slots, slots_pad, width, outs, mixed, operands):
    vmem = pl.BlockSpec(memory_space=pltpu.VMEM)
    return pl.pallas_call(
        functools.partial(kernel, lat, slots),
        out_shape=outs,
        in_specs=[pl.BlockSpec(memory_space=pltpu.SMEM)] + [vmem] * (len(operands) - 1),
        out_specs=jax.tree.map(lambda _: vmem, outs),
        scratch_shapes=[
            pltpu.VMEM((KS * KS, 8, LANES), F32),
            pltpu.VMEM((lat + 2 * REACH, slots_pad + 16, LANES), F32),
            pltpu.VMEM(mixed, F32),
        ],
        compiler_params=pltpu.CompilerParams(vmem_limit_bytes=12 * 2**20),
        cost_estimate=pl.CostEstimate(flops=2**20, bytes_accessed=2**20, transcendentals=0),
    )(*operands)


def gate(values):
    cumulative = 0.5 * (1.0 + lax.erf(values * (1.0 / math.sqrt(2.0))))
    density = jnp.exp(-0.5 * values * values) * (1.0 / math.sqrt(2.0 * math.pi))
    return cumulative, density


def upper(bit):
    return (lax.axis_index("lon") & bit) // bit


def swapped(value, bit):
    count = lax.axis_size("lon")
    return lax.ppermute(value, "lon", [(i, i ^ bit) for i in range(count)])


def merged(high, own, got):
    rows = own.shape[0]
    out = jnp.zeros((2 * rows, own.shape[1]), own.dtype)
    out = lax.dynamic_update_slice_in_dim(out, own, high * rows, 0)
    return lax.dynamic_update_slice_in_dim(out, got, (1 - high) * rows, 0)


def lon_bits():
    bits, bit = [], 1
    while bit < lax.axis_size("lon"):
        bits.append(bit)
        bit *= 2
    return bits


class State:
    def __init__(self):
        self.held = {}

    def sync(self, *more):
        names = list(self.held)
        tied = lax.optimization_barrier(tuple(self.held.values()) + more)
        self.held = dict(zip(names, tied))
        return tied[len(names) :]


class Pair:
    def __init__(self, state, name, parts, ways):
        self.state, self.names, self.sent = state, (name + "0", name + "1"), None
        self.terms, self.rows = [[], []], 0
        self.keep(parts)
        self.stages = []
        for near, far in ways:
            down = [(g, "down") for g in [near[:1], near[1:], far[:-1]]]
            self.stages.append(down + [(far[-1:], "meet"), (far[-2::-1], "up")])
        self.near = [near for near, _ in ways]

    def keep(self, parts):
        for terms in self.terms:
            for key, _ in terms:
                del self.state.held[key]
        self.terms = [[(name + "t0", 0)] for name in self.names]
        self.state.held.update((terms[0][0], p) for terms, p in zip(self.terms, parts))
        self.rows = parts[0].shape[0]

    def parts(self):
        return [self.state.held[terms[0][0]] for terms in self.terms]

    def rows_of(self, terms, start, rows):
        total = 0.0
        for key, offset in terms:
            rows_here = lax.dynamic_slice_in_dim(self.state.held[key], offset + start, rows, 0)
            total = total + rows_here.astype(F32)
        return total.astype(BF16)

    def outgoing(self, bits, kind):
        if kind == "down":
            half = self.rows // 2
            return [
                self.rows_of(terms, (1 - upper(b)) * half, half)
                for terms, b in zip(self.terms, bits)
            ]
        if kind == "meet":
            self.keep([self.rows_of(terms, 0, self.rows) for terms in self.terms])
        return self.parts()

    def launch(self, bits, kind, sent):
        self.sent = (bits, kind, [swapped(v, b) for v, b in zip(sent, bits)])

    def start(self, bits, kind):
        if kind == "down":
            self.launch(bits, kind, self.state.sync(*self.outgoing(bits, kind)))
        else:
            self.outgoing(bits, kind)
            self.state.sync()
            self.launch(bits, kind, self.parts())

    def close(self):
        bits, kind, got = self.sent
        if kind == "up":
            self.keep([merged(upper(b), p, g) for p, g, b in zip(self.parts(), got, bits)])
        elif kind == "meet":
            both = zip(self.parts(), got)
            self.keep([(p.astype(F32) + g.astype(F32)).astype(BF16) for p, g in both])
        else:
            if kind == "down":
                self.rows //= 2
            for k, (g, b) in enumerate(zip(got, bits)):
                key = self.names[k] + "t" + str(len(self.terms[k]))
                if kind == "down":
                    self.terms[k] = [(old, at + upper(b) * self.rows) for old, at in self.terms[k]]
                self.terms[k] = self.terms[k] + [(key, 0)]
                self.state.held[key] = g

    def cross(self, which, name):
        self.state.sync()
        sent = [self.state.held[tag] for tag in self.tags(name)]
        return [swapped(v, near[which]) for v, near in zip(sent, self.near)]

    def arrive(self, name, values):
        self.state.held.update(zip(self.tags(name), values))

    def tags(self, name):
        return [own + name for own in self.names]

    def place(self, out, values, other0, other1):
        for k, (v, (bit0, bit1)) in enumerate(zip(values, self.near)):
            block = 4 * k + 2 * (upper(bit0) ^ other0) + (upper(bit1) ^ other1)
            out = lax.dynamic_update_slice_in_dim(out, v, block * self.rows, 0)
        return out

    def spread(self):
        own = self.parts()
        out = jnp.zeros((4 * len(own) * self.rows, own[0].shape[1]), BF16)
        return self.place(out, own, 0, 0)

    def get(self, name):
        return [self.state.held[tag] for tag in self.tags(name)]

    def next_stage(self):
        groups = [stages.pop(0) for stages in self.stages]
        return list(zip(*(bits for bits, _ in groups))), groups[0][1]

    def open(self):
        steps, kind = self.next_stage()
        for bits in steps[:-1]:
            self.start(bits, kind)
            self.close()
        self.start(steps[-1], kind)

    def advance(self):
        self.close()
        self.open()

    def quarter(self, k, other0, other1):
        bit0, bit1 = self.near[k]
        block = 2 * (upper(bit0) ^ other0) + (upper(bit1) ^ other1)
        return block * (self.rows // 4)

    def prepare(self):
        self.next_stage()
        self.next_stage()
        whole, size = self.parts(), self.rows // 4
        for piece, other1 in (("r0", 1), ("r1", 0)):
            cuts = [
                lax.dynamic_slice_in_dim(v, self.quarter(k, 1, other1), size, 0)
                for k, v in enumerate(whole)
            ]
            self.arrive(piece, cuts)
        self.piece, self.going = -1, ([near[0] for near in self.near], "down")

    def sum_first(self):
        size, sent = self.rows // 4, []
        for k, (v, g) in enumerate(zip(self.parts(), self.get("g0"))):
            rows = lax.dynamic_slice_in_dim(v, self.quarter(k, 0, 1), size, 0)
            sent.append((rows.astype(F32) + g.astype(F32)).astype(BF16))
        self.arrive("s", sent)

    def forward(self):
        self.arrived()
        size = self.rows // 4
        for k, tag in enumerate(self.tags("g1")):
            self.terms[k] = [(self.terms[k][0][0], self.quarter(k, 0, 0)), (tag, 0)]
        for tag in self.tags("g0"):
            del self.state.held[tag]
        self.rows = size
        bits = [near[1] for near in self.near]
        sent = [self.state.held.pop(tag) for tag in self.tags("s")]
        self.launch(bits, "kept", self.state.sync(*sent))

    def next_piece(self):
        self.piece += 1
        self.state.sync()
        sent = [self.state.held.pop(tag) for tag in self.tags("r" + str(self.piece))]
        self.launch(*self.going, sent)

    def arrived(self):
        self.arrive("g" + str(self.piece), self.sent[2])


def both_ways():
    bits = lon_bits()
    fast, slow = bits[:2], bits[2:]
    return (fast, slow), (fast[::-1], slow[::-1])


def all_rows(own):
    if lax.axis_size("mlp") == 2:
        return jnp.concatenate([own, lax.ppermute(own, "mlp", [(0, 1), (1, 0)])], axis=0)
    return lax.all_gather(own, "mlp", axis=0, tiled=True)


def own_rows_sum(partial):
    if lax.axis_size("mlp") == 2:
        rows = partial.shape[0] // 2
        theirs = lax.ppermute(partial[rows:], "mlp", [(0, 1), (1, 0)])
        return partial[:rows].astype(F32) + theirs.astype(F32)
    return lax.psum_scatter(partial, "mlp", scatter_dimension=0, tiled=True).astype(F32)


def across_rows(left, right):
    return lax.dot_general(left, right, (((0,), (0,)), ((), ())), preferred_element_type=F32)


def across_width(left, right):
    return lax.dot_general(left, right, (((1,), (1,)), ((), ())), preferred_element_type=F32)


def body(fields, cotangent, conv_weight, norm_gain, weight_in, weight_out):
    lat, slots, width = fields.shape
    slots_pad = -(-slots // 16) * 16
    held = live_count()
    slot_live = lax.broadcasted_iota(jnp.int32, (1, slots, 1), 1) < held
    spare = ((0, 0), (0, slots_pad - slots), (0, 0))
    where = places(lat, held)
    gain = norm_gain.astype(F32).reshape(1, width)
    cot_all = all_rows(jnp.pad(jnp.where(slot_live, cotangent, 0), spare).reshape(-1, width))

    grid = (lat, slots_pad, width)
    normed, hat, inv = kernel_call(
        forward_kernel, lat, slots, slots_pad, width,
        (
            jax.ShapeDtypeStruct(grid, BF16),
            jax.ShapeDtypeStruct(grid, F32),
            jax.ShapeDtypeStruct((lat, slots_pad, LANES), F32),
        ),
        grid,
        (where,) + halo(fields, slots, held) + (conv_weight, gain),
    )
    normed_all = all_rows(normed.reshape(-1, width))

    cells = lax.axis_size("mlp") * lat * LON
    factor = jnp.float32(1.0 / math.sqrt(cells))
    state = State()
    ways = both_ways()

    def pair(name, grad):
        half = grad.shape[0] // 2
        return Pair(state, name, (grad[:half], grad[half:]), ways)

    hidden = jnp.dot(normed_all, weight_in, preferred_element_type=F32)
    cumulative, density = gate(hidden)
    activated = (hidden * cumulative).astype(BF16)
    state.held["cot"] = cot_all
    a = pair("a", (across_rows(activated, cot_all) * factor).astype(BF16))
    a.open()
    upstream = across_width(state.held.pop("cot"), weight_out)
    grad_hidden = (upstream * (cumulative + hidden * density)).astype(BF16)
    partial = across_width(grad_hidden, weight_in).astype(BF16)
    grad_normed = own_rows_sum(partial)
    state.held["hidden"] = grad_hidden
    state.held["partial"] = partial
    a.advance()
    grad_first = across_rows(normed_all, state.held.pop("hidden")) * factor
    b = pair("b", grad_first.astype(BF16))
    state.held["gain"] = gain
    state.held["inv"] = inv
    state.held["back"] = grad_normed
    b.prepare()
    a.advance()
    b.next_piece()

    scaled = state.held.pop("back").reshape(grid) * state.held.pop("gain")
    inv = state.held.pop("inv")[:, :, :1]
    grad_mixed = inv * (
        scaled
        - jnp.mean(scaled, axis=-1, keepdims=True)
        - hat * jnp.mean(scaled * hat, axis=-1, keepdims=True)
    )
    del state.held["partial"]
    b.arrived()
    a.advance()
    b.next_piece()
    state.held["mixed"] = grad_mixed.astype(BF16)
    b.sum_first()
    b.arrived()
    a.advance()
    b.forward()
    a.close()
    from_near = a.cross(1, "t0")
    b.advance()
    own, other, sides = halo(state.held.pop("mixed"), slots, held)

    b.advance()
    a.arrive("n", from_near)
    from_far = a.cross(0, "t0")
    a.arrive("f", from_far)
    b.advance()
    from_both = a.cross(0, "n")
    a.arrive("b", from_both)
    b.close()
    from_near = b.cross(1, "t0")
    from_far = b.cross(0, "t0")
    state.held["sides"] = sides
    state.sync()
    state.held["result"] = kernel_call(
        backward_kernel, lat, slots, slots_pad, width,
        jax.ShapeDtypeStruct((lat, slots, width), BF16),
        (lat, slots_pad, LANES),
        (where, own, other, state.held["sides"], conv_weight, cotangent),
    )
    state.held["out"] = b.spread()
    out_second = a.place(a.place(a.spread(), a.get("n"), 0, 1), a.get("f"), 1, 0)
    state.held["second"] = a.place(out_second, a.get("b"), 1, 1)
    b.arrive("n", from_near)
    b.arrive("f", from_far)
    from_both = b.cross(0, "n")
    out_first = b.place(b.place(state.held["out"], b.get("n"), 0, 1), b.get("f"), 1, 0)
    out_first = b.place(out_first, from_both, 1, 1)
    return (state.held["result"], out_first, state.held["second"])


def solution(mesh):
    in_specs = (
        P("mlp", "lon", None),
        P("mlp", "lon", None),
        P(),
        P(),
        P(None, "mlp"),
        P("mlp", None),
    )
    out_specs = (P("mlp", "lon", None), P(None, "mlp"), P("mlp", None))
    return jax.shard_map(body, mesh=mesh, in_specs=in_specs, out_specs=out_specs, check_vma=False)
```

```python
import functools
import math

import jax
import jax.numpy as jnp
from jax import lax
from jax.experimental import pallas as pl
from jax.experimental.pallas import tpu as pltpu
from jax.sharding import PartitionSpec as P

KS = 7
LON = 1440
REACH = KS // 2
LANES = 128
BF16 = jnp.bfloat16
F32 = jnp.float32
LEAD = 8


def passed_along(value, axis, by):
    count = lax.axis_size(axis)
    return lax.ppermute(value, axis, [(i, (i + by) % count) for i in range(count)])


def live_count():
    members = lax.axis_size("lon")
    position = lax.axis_index("lon")
    return LON // members + (position < LON % members).astype(jnp.int32)


def halo(own, slots, held):
    lat, count = own.shape[0], lax.axis_size("mlp")
    if count == 2:
        mine = jnp.where(lax.axis_index("mlp") == 0, own[lat - REACH :], own[:REACH])
        other = lax.ppermute(mine, "mlp", [(0, 1), (1, 0)])
    else:
        ends = count - 1
        other = jnp.concatenate(
            [
                lax.ppermute(own[lat - REACH :], "mlp", [(i, i + 1) for i in range(ends)]),
                lax.ppermute(own[:REACH], "mlp", [(i + 1, i) for i in range(ends)]),
            ],
            axis=0,
        )
    even = LON % lax.axis_size("lon") == 0
    both = (own, other)
    first = jnp.concatenate([v[:, :REACH] for v in both], axis=0)
    if even:
        last = jnp.concatenate([v[:, slots - REACH : slots] for v in both], axis=0)
    else:
        last = jnp.concatenate(
            [lax.dynamic_slice_in_dim(v, held - REACH, REACH, 1) for v in both], axis=0
        )
    left = passed_along(last, "lon", 1)
    right = passed_along(first, "lon", -1)
    if not even:
        rows = jnp.concatenate([v[:, :slots] for v in both], axis=0)
        joined = jnp.concatenate([rows, jnp.zeros_like(right)], axis=1)
        joined = lax.dynamic_update_slice_in_dim(joined, right, held, 1)
        own, other, right = joined[:lat, :slots], joined[lat:, :slots], joined[:, slots:]
    return own, other, jnp.concatenate([left, right], axis=1)


def places(lat, held):
    near = jnp.int32(0)
    if lax.axis_size("mlp") == 2:
        near = jnp.where(lax.axis_index("mlp") == 0, lat + REACH, 0).astype(jnp.int32)
        return jnp.stack([near, held.astype(jnp.int32)])
    return jnp.stack([near, held.astype(jnp.int32), jnp.int32(lat + REACH)])


def conv_tile(lat, slots, rows, flip, where_ref, own, other, sides, taps, wide, lane, sink):
    groups = other.shape[0] // REACH
    wide[REACH : REACH + lat, LEAD : LEAD + slots, :] = own[:, :slots, lane].astype(F32)
    ends = sides[:, :, lane].astype(F32)
    wide[REACH : REACH + lat, LEAD - REACH : LEAD, :] = ends[:lat, :REACH]
    wide[REACH : REACH + lat, LEAD + slots : LEAD + slots + REACH, :] = ends[:lat, REACH:]
    for g in range(groups):
        for k in range(REACH):
            at, src = where_ref[2 * g] + k, g * REACH + k
            wide[at, LEAD : LEAD + slots, :] = other[src, :slots, lane].astype(F32)
            wide[at, LEAD - REACH : LEAD, :] = ends[lat + src, :REACH]
            wide[at, LEAD + slots : LEAD + slots + REACH, :] = ends[lat + src, REACH:]

    def step(jt, carry):
        start = jt * 16
        acc = [[jnp.zeros((8, LANES), F32) for _ in range(lat)] for _ in range(2)]
        for b in range(KS):
            used = [a * KS + b for a in range(KS)]
            if flip:
                used = [KS * KS - 1 - t for t in used]
            taken = [taps[t] for t in used]
            for r in rows:
                for half in range(2):
                    cells = wide[r, pl.ds(start + 8 * half + LEAD - REACH + b, 8), :]
                    for i in range(max(0, r - KS + 1), min(lat, r + 1)):
                        acc[half][i] = acc[half][i] + taken[r - i] * cells
        for half in range(2):
            for i in range(lat):
                sink(i, pl.ds(pl.multiple_of(start + 8 * half, 8), 8), acc[half][i])
        return carry

    lax.fori_loop(0, -(-slots // 16), step, 0)


def conv(lat, slots, flip, where_ref, own, other, sides, weight, taps, wide, finish, sink):
    width = own.shape[-1]

    def over(rows):
        def channels(ct, carry):
            lane = pl.ds(pl.multiple_of(ct * LANES, LANES), LANES)
            for a in range(KS):
                row = weight[a, :, lane].astype(F32)
                for b in range(KS):
                    taps[a * KS + b] = jnp.broadcast_to(row[b : b + 1], (8, LANES))
            conv_tile(
                lat, slots, rows, flip, where_ref, own, other, sides, taps, wide, lane,
                functools.partial(sink, lane),
            )
            finish(lane)
            return carry

        lax.fori_loop(0, width // LANES, channels, 0)

    if other.shape[0] == REACH:
        first = where_ref[0] != 0
        pl.when(first)(lambda: over(range(REACH, lat + 2 * REACH)))
        pl.when(jnp.logical_not(first))(lambda: over(range(lat + REACH)))
    else:
        over(range(lat + 2 * REACH))


def forward_kernel(
    lat, slots, where_ref, own, other, sides, weight, gain, normed, hat, inv, taps, wide, mixed
):
    def sink(lane, i, at, value):
        mixed[i, at, lane] = value

    conv(
        lat, slots, False, where_ref, own, other, sides, weight, taps, wide,
        lambda lane: None, sink,
    )
    tile = 32 if mixed.shape[1] % 32 == 0 else 16
    tiles = mixed.shape[1] // tile

    def norm(step, carry):
        i, start = step // tiles, pl.multiple_of(step % tiles * tile, tile)
        at = pl.ds(start, tile)
        values = mixed[i, at, :]
        centred = values - jnp.mean(values, axis=-1, keepdims=True)
        scale = lax.rsqrt(jnp.mean(centred * centred, axis=-1, keepdims=True) + 1e-06)
        live = start + lax.broadcasted_iota(jnp.int32, (tile, 1), 0) < where_ref[1]
        unit = jnp.where(live, centred * scale, 0.0)
        hat[i, at, :] = unit
        normed[i, at, :] = (unit * gain[...]).astype(BF16)
        inv[i, at, :] = jnp.broadcast_to(jnp.where(live, scale, 0.0), (tile, LANES))
        return carry

    lax.fori_loop(0, lat * tiles, norm, 0, unroll=3)


def backward_kernel(
    lat, slots, where_ref, own, other, sides, weight, cot, out, taps, wide, mixed
):
    def sink(lane, i, at, value):
        mixed[i, at, :] = value

    def finish(lane):
        live = lax.broadcasted_iota(jnp.int32, (slots, 1), 0) < where_ref[1]
        for i in range(lat):
            total = cot[i, :, lane].astype(F32) + mixed[i, :slots, :]
            out[i, :, lane] = jnp.where(live, total, 0.0).astype(BF16)

    conv(lat, slots, True, where_ref, own, other, sides, weight, taps, wide, finish, sink)


def kernel_call(kernel, lat, slots, slots_pad, width, outs, mixed, operands):
    vmem = pl.BlockSpec(memory_space=pltpu.VMEM)
    return pl.pallas_call(
        functools.partial(kernel, lat, slots),
        out_shape=outs,
        in_specs=[pl.BlockSpec(memory_space=pltpu.SMEM)] + [vmem] * (len(operands) - 1),
        out_specs=jax.tree.map(lambda _: vmem, outs),
        scratch_shapes=[
            pltpu.VMEM((KS * KS, 8, LANES), F32),
            pltpu.VMEM((lat + 2 * REACH, slots_pad + 16, LANES), F32),
            pltpu.VMEM(mixed, F32),
        ],
        compiler_params=pltpu.CompilerParams(vmem_limit_bytes=12 * 2**20),
        cost_estimate=pl.CostEstimate(flops=2**20, bytes_accessed=2**20, transcendentals=0),
    )(*operands)


def gate(values):
    cumulative = 0.5 * (1.0 + lax.erf(values * (1.0 / math.sqrt(2.0))))
    density = jnp.exp(-0.5 * values * values) * (1.0 / math.sqrt(2.0 * math.pi))
    return cumulative, density


def upper(bit):
    return (lax.axis_index("lon") & bit) // bit


def swapped(value, bit):
    count = lax.axis_size("lon")
    return lax.ppermute(value, "lon", [(i, i ^ bit) for i in range(count)])


def merged(high, own, got):
    rows = own.shape[0]
    out = jnp.zeros((2 * rows, own.shape[1]), own.dtype)
    out = lax.dynamic_update_slice_in_dim(out, own, high * rows, 0)
    return lax.dynamic_update_slice_in_dim(out, got, (1 - high) * rows, 0)


def lon_bits():
    bits, bit = [], 1
    while bit < lax.axis_size("lon"):
        bits.append(bit)
        bit *= 2
    return bits


class State:
    def __init__(self):
        self.held = {}

    def sync(self, *more):
        names = list(self.held)
        tied = lax.optimization_barrier(tuple(self.held.values()) + more)
        self.held = dict(zip(names, tied))
        return tied[len(names) :]


class Pair:
    def __init__(self, state, name, parts, ways):
        self.state, self.names, self.sent = state, (name + "0", name + "1"), None
        self.terms, self.rows = [[], []], 0
        self.keep(parts)
        self.stages = []
        for near, far in ways:
            down = [(g, "down") for g in [near[:1], near[1:], far[:-1]]]
            self.stages.append(down + [(far[-1:], "meet"), (far[-2::-1], "up")])
        self.near = [near for near, _ in ways]

    def keep(self, parts):
        for terms in self.terms:
            for key, _ in terms:
                del self.state.held[key]
        self.terms = [[(name + "t0", 0)] for name in self.names]
        self.state.held.update((terms[0][0], p) for terms, p in zip(self.terms, parts))
        self.rows = parts[0].shape[0]

    def parts(self):
        return [self.state.held[terms[0][0]] for terms in self.terms]

    def rows_of(self, terms, start, rows):
        total = 0.0
        for key, offset in terms:
            rows_here = lax.dynamic_slice_in_dim(self.state.held[key], offset + start, rows, 0)
            total = total + rows_here.astype(F32)
        return total.astype(BF16)

    def outgoing(self, bits, kind):
        if kind == "down":
            half = self.rows // 2
            return [
                self.rows_of(terms, (1 - upper(b)) * half, half)
                for terms, b in zip(self.terms, bits)
            ]
        if kind == "meet":
            self.keep([self.rows_of(terms, 0, self.rows) for terms in self.terms])
        return self.parts()

    def launch(self, bits, kind, sent):
        self.sent = (bits, kind, [swapped(v, b) for v, b in zip(sent, bits)])

    def start(self, bits, kind):
        if kind == "down":
            self.launch(bits, kind, self.state.sync(*self.outgoing(bits, kind)))
        else:
            self.outgoing(bits, kind)
            self.state.sync()
            self.launch(bits, kind, self.parts())

    def close(self):
        bits, kind, got = self.sent
        if kind == "up":
            self.keep([merged(upper(b), p, g) for p, g, b in zip(self.parts(), got, bits)])
        elif kind == "meet":
            both = zip(self.parts(), got)
            self.keep([(p.astype(F32) + g.astype(F32)).astype(BF16) for p, g in both])
        else:
            if kind == "down":
                self.rows //= 2
            for k, (g, b) in enumerate(zip(got, bits)):
                key = self.names[k] + "t" + str(len(self.terms[k]))
                if kind == "down":
                    self.terms[k] = [(old, at + upper(b) * self.rows) for old, at in self.terms[k]]
                self.terms[k] = self.terms[k] + [(key, 0)]
                self.state.held[key] = g

    def cross(self, which, name):
        self.state.sync()
        sent = [self.state.held[tag] for tag in self.tags(name)]
        return [swapped(v, near[which]) for v, near in zip(sent, self.near)]

    def arrive(self, name, values):
        self.state.held.update(zip(self.tags(name), values))

    def tags(self, name):
        return [own + name for own in self.names]

    def place(self, out, values, other0, other1):
        for k, (v, (bit0, bit1)) in enumerate(zip(values, self.near)):
            block = 4 * k + 2 * (upper(bit0) ^ other0) + (upper(bit1) ^ other1)
            out = lax.dynamic_update_slice_in_dim(out, v, block * self.rows, 0)
        return out

    def spread(self):
        own = self.parts()
        out = jnp.zeros((4 * len(own) * self.rows, own[0].shape[1]), BF16)
        return self.place(out, own, 0, 0)

    def get(self, name):
        return [self.state.held[tag] for tag in self.tags(name)]

    def next_stage(self):
        groups = [stages.pop(0) for stages in self.stages]
        return list(zip(*(bits for bits, _ in groups))), groups[0][1]

    def open(self):
        steps, kind = self.next_stage()
        for bits in steps[:-1]:
            self.start(bits, kind)
            self.close()
        self.start(steps[-1], kind)

    def advance(self):
        self.close()
        self.open()

    def quarter(self, k, other0, other1):
        bit0, bit1 = self.near[k]
        block = 2 * (upper(bit0) ^ other0) + (upper(bit1) ^ other1)
        return block * (self.rows // 4)

    def prepare(self):
        self.next_stage()
        self.next_stage()
        whole, size = self.parts(), self.rows // 4
        for piece, other1 in (("r0", 1), ("r1", 0)):
            cuts = [
                lax.dynamic_slice_in_dim(v, self.quarter(k, 1, other1), size, 0)
                for k, v in enumerate(whole)
            ]
            self.arrive(piece, cuts)
        self.piece, self.going = -1, ([near[0] for near in self.near], "down")

    def sum_first(self):
        size, sent = self.rows // 4, []
        for k, (v, g) in enumerate(zip(self.parts(), self.get("g0"))):
            rows = lax.dynamic_slice_in_dim(v, self.quarter(k, 0, 1), size, 0)
            sent.append((rows.astype(F32) + g.astype(F32)).astype(BF16))
        self.arrive("s", sent)

    def forward(self):
        self.arrived()
        size = self.rows // 4
        for k, tag in enumerate(self.tags("g1")):
            self.terms[k] = [(self.terms[k][0][0], self.quarter(k, 0, 0)), (tag, 0)]
        for tag in self.tags("g0"):
            del self.state.held[tag]
        self.rows = size
        bits = [near[1] for near in self.near]
        sent = [self.state.held.pop(tag) for tag in self.tags("s")]
        self.launch(bits, "kept", self.state.sync(*sent))

    def next_piece(self):
        self.piece += 1
        self.state.sync()
        sent = [self.state.held.pop(tag) for tag in self.tags("r" + str(self.piece))]
        self.launch(*self.going, sent)

    def arrived(self):
        self.arrive("g" + str(self.piece), self.sent[2])


def both_ways():
    bits = lon_bits()
    fast, slow = bits[:2], bits[2:]
    return (fast, slow), (fast[::-1], slow[::-1])


def all_rows(own):
    if lax.axis_size("mlp") == 2:
        return jnp.concatenate([own, lax.ppermute(own, "mlp", [(0, 1), (1, 0)])], axis=0)
    return lax.all_gather(own, "mlp", axis=0, tiled=True)


def own_rows_sum(partial):
    if lax.axis_size("mlp") == 2:
        rows = partial.shape[0] // 2
        theirs = lax.ppermute(partial[rows:], "mlp", [(0, 1), (1, 0)])
        return partial[:rows].astype(F32) + theirs.astype(F32)
    return lax.psum_scatter(partial, "mlp", scatter_dimension=0, tiled=True).astype(F32)


def across_rows(left, right):
    return lax.dot_general(left, right, (((0,), (0,)), ((), ())), preferred_element_type=F32)


def across_width(left, right):
    return lax.dot_general(left, right, (((1,), (1,)), ((), ())), preferred_element_type=F32)


def body(fields, cotangent, conv_weight, norm_gain, weight_in, weight_out):
    lat, slots, width = fields.shape
    slots_pad = -(-slots // 16) * 16
    held = live_count()
    slot_live = lax.broadcasted_iota(jnp.int32, (1, slots, 1), 1) < held
    spare = ((0, 0), (0, slots_pad - slots), (0, 0))
    where = places(lat, held)
    gain = norm_gain.astype(F32).reshape(1, width)
    cot_all = all_rows(jnp.pad(jnp.where(slot_live, cotangent, 0), spare).reshape(-1, width))

    grid = (lat, slots_pad, width)
    normed, hat, inv = kernel_call(
        forward_kernel, lat, slots, slots_pad, width,
        (
            jax.ShapeDtypeStruct(grid, BF16),
            jax.ShapeDtypeStruct(grid, F32),
            jax.ShapeDtypeStruct((lat, slots_pad, LANES), F32),
        ),
        grid,
        (where,) + halo(fields, slots, held) + (conv_weight, gain),
    )
    normed_all = all_rows(normed.reshape(-1, width))

    cells = lax.axis_size("mlp") * lat * LON
    factor = jnp.float32(1.0 / math.sqrt(cells))
    state = State()
    ways = both_ways()

    def pair(name, grad):
        half = grad.shape[0] // 2
        return Pair(state, name, (grad[:half], grad[half:]), ways)

    hidden = jnp.dot(normed_all, weight_in, preferred_element_type=F32)
    cumulative, density = gate(hidden)
    activated = (hidden * cumulative).astype(BF16)
    state.held["cot"] = cot_all
    a = pair("a", (across_rows(activated, cot_all) * factor).astype(BF16))
    a.open()
    upstream = across_width(state.held.pop("cot"), weight_out)
    grad_hidden = (upstream * (cumulative + hidden * density)).astype(BF16)
    partial = across_width(grad_hidden, weight_in).astype(BF16)
    grad_normed = own_rows_sum(partial)
    state.held["hidden"] = grad_hidden
    state.held["partial"] = partial
    a.advance()
    grad_first = across_rows(normed_all, state.held.pop("hidden")) * factor
    b = pair("b", grad_first.astype(BF16))
    state.held["gain"] = gain
    state.held["inv"] = inv
    state.held["back"] = grad_normed
    b.prepare()
    a.advance()
    b.next_piece()

    scaled = state.held.pop("back").reshape(grid) * state.held.pop("gain")
    inv = state.held.pop("inv")[:, :, :1]
    grad_mixed = inv * (
        scaled
        - jnp.mean(scaled, axis=-1, keepdims=True)
        - hat * jnp.mean(scaled * hat, axis=-1, keepdims=True)
    )
    del state.held["partial"]
    b.arrived()
    a.advance()
    b.next_piece()
    state.held["mixed"] = grad_mixed.astype(BF16)
    b.sum_first()
    b.arrived()
    a.advance()
    b.forward()
    a.close()
    from_near = a.cross(1, "t0")
    b.advance()
    own, other, sides = halo(state.held.pop("mixed"), slots, held)

    b.advance()
    a.arrive("n", from_near)
    from_far = a.cross(0, "t0")
    a.arrive("f", from_far)
    b.advance()
    from_both = a.cross(0, "n")
    a.arrive("b", from_both)
    b.close()
    from_near = b.cross(1, "t0")
    from_far = b.cross(0, "t0")
    state.held["sides"] = sides
    state.sync()
    state.held["result"] = kernel_call(
        backward_kernel, lat, slots, slots_pad, width,
        jax.ShapeDtypeStruct((lat, slots, width), BF16),
        (lat, slots_pad, LANES),
        (where, own, other, state.held["sides"], conv_weight, cotangent),
    )
    state.held["out"] = b.spread()
    out_second = a.place(a.place(a.spread(), a.get("n"), 0, 1), a.get("f"), 1, 0)
    state.held["second"] = a.place(out_second, a.get("b"), 1, 1)
    b.arrive("n", from_near)
    b.arrive("f", from_far)
    from_both = b.cross(0, "n")
    out_first = b.place(b.place(state.held["out"], b.get("n"), 0, 1), b.get("f"), 1, 0)
    out_first = b.place(out_first, from_both, 1, 1)
    return (state.held["result"], out_first, state.held["second"])


def solution(mesh):
    in_specs = (
        P("mlp", "lon", None),
        P("mlp", "lon", None),
        P(),
        P(),
        P(None, "mlp"),
        P("mlp", None),
    )
    out_specs = (P("mlp", "lon", None), P(None, "mlp"), P("mlp", None))
    return jax.shard_map(body, mesh=mesh, in_specs=in_specs, out_specs=out_specs, check_vma=False)
```
